32 devices in a mesh: layer: 4 (over x, core), feat: 8 (over z, y).
Axes of the slice: x: 2, y: 2, z: 4, core: 2. Of those that a mesh axis runs over, the one named last changes fastest.
Arguments:
- layer_inputs: bfloat16 [4, 512, 2048], P('layer', 'feat'), may hold values from -6 to 6
- targets: float32 [4, 512, 2048], P('layer', None, 'feat'), may hold values from -5 to 5
- encoder: bfloat16 [4, 2048, 32768], P('layer', None, 'feat'), may hold values from -0.125 to 0.125
- encoder_bias: float32 [4, 32768], P('layer', 'feat'), may hold values from -3 to 3
- decoder: bfloat16 [4, 4, 32768, 2048], P('layer', None, 'feat'), may hold values from -0.03125 to 0.03125
Outputs:
- residual: float32 [4, 512, 2048], P('layer', None, 'feat')
The draws below stay inside these ranges and needn't reach their ends.
All inputs are finite; a program needn't handle non-finite values.
Results may differ from the reference program's by a relative error of at most 0.0025.
Values may be sent and summed in bfloat16 or wider, within the bound.
No kernel may reach another device: no remote copies, remote signals or barrier semaphores. Data moves between devices by JAX's collectives and lax.ppermute only.
A program may use at most 192 MiB of HBM per device.

```python
import jax
import jax.numpy as jnp

D = 2048
F = 32768
L_WIN = 4
TOK = 512
GROUPS = 1
N_LAYER = 4


def levels(key, dims, shards, smallest, high):
    def one(axis_at, blocks):
        heights = jax.random.uniform(jax.random.fold_in(jax.random.fold_in(key, 6), axis_at), (blocks,), jnp.float32, smallest / len(shards), high / len(shards))
        return jnp.repeat(jnp.exp(heights), dims[axis_at] // blocks).reshape((-1,) + (1,) * (len(dims) - axis_at - 1))

    factor_of = one(*shards[0])
    for cut in shards[1:]:
        factor_of = factor_of * one(*cut)
    return factor_of


def gaussian(rng, shape, deviation, limit, cuts=(), dtype=jnp.bfloat16):
    values = jax.random.normal(rng, shape, jnp.float32) * deviation
    if len(cuts) > 0:
        values = levels(rng, shape, cuts, -0.22, 0.18) * values
    return jnp.clip(values, min=-limit, max=limit).astype(dtype)


def setup_inputs(seed: int = 0) -> dict:
    arg_keys = jax.random.split(jax.random.key(seed), 6)
    return {
        "layer_inputs": gaussian(arg_keys[0], (N_LAYER, TOK // GROUPS, D), 1.0, 6.0, ((0, 4), (1, 8))),
        "targets": gaussian(arg_keys[1], (N_LAYER, TOK // GROUPS, D), 0.7, 5.0, ((0, 4), (2, 8)), jnp.float32),
        "encoder": gaussian(arg_keys[2], (N_LAYER, D, F // GROUPS), D ** -0.5, 0.125, ((0, 4), (2, 8))),
        "encoder_bias": gaussian(arg_keys[3], (N_LAYER, F // GROUPS), 0.5, 3.0, ((0, 4), (1, 8)), jnp.float32),
        "decoder": gaussian(arg_keys[4], (N_LAYER, L_WIN, F // GROUPS, D), F ** -0.5, 0.03125, ((0, 4), (2, 8))),
    }


def reference(layer_inputs, targets, encoder, encoder_bias, decoder):
    groups = N_LAYER // L_WIN
    activations = []
    for layer_index in range(L_WIN):
        lower = layer_index * groups
        tokens = layer_inputs[lower:lower + groups].reshape(TOK, D)
        weight = jnp.transpose(encoder[lower:lower + groups], (1, 0, 2)).reshape(D, F)
        offset = encoder_bias[lower:lower + groups].reshape(F)
        preact = jnp.dot(tokens, weight, preferred_element_type=jnp.float32) + offset
        activations.append(jax.nn.relu(preact).astype(jnp.bfloat16))
    results = []
    for target in range(L_WIN):
        lower = target * groups
        rebuilt = jnp.zeros((TOK, D), jnp.float32)
        for source in range(target + 1):
            weight = decoder[lower:lower + groups, target - source].reshape(F, D)
            rebuilt = rebuilt + jnp.dot(activations[source], weight, preferred_element_type=jnp.float32)
        wanted = targets[lower:lower + groups].reshape(TOK, D)
        results.append((rebuilt - wanted).reshape(groups, TOK // groups, D))
    return jnp.concatenate(results, axis=0)
```

```python
import functools

import jax
import jax.numpy as jnp
from jax import lax
from jax.experimental import pallas as pl
from jax.experimental.pallas import tpu as pltpu
from jax.sharding import PartitionSpec as P

L_WIN = 4
VMEM_BYTES = 56 * 1024 * 1024


def exchange(array, axis, flip):
    size = lax.axis_size(axis)
    return lax.ppermute(array, axis, [(i, i ^ flip) for i in range(size)])


def load_rows(parts, dest, sems):
    copies = []
    row = 0
    for i, part in enumerate(parts):
        rows = part.shape[0]
        copies.append(pltpu.make_async_copy(part, dest.at[pl.ds(row, rows)], sems.at[i]))
        row += rows
    for copy in copies:
        copy.start()
    for copy in copies:
        copy.wait()


def encode_kernel(n_in, n_out, *refs):
    parts, refs = refs[:n_in], refs[n_in:]
    weight, bias, refs = refs[0], refs[1], refs[3:]
    outs, (tokens, sems) = refs[:n_out], refs[n_out:]

    @pl.when(pl.program_id(0) == 0)
    def _():
        load_rows(parts, tokens, sems)

    preact = jnp.dot(tokens[...], weight[0], preferred_element_type=jnp.float32) + bias[...]
    acts = jnp.maximum(preact, 0.0).astype(jnp.bfloat16)
    row = 0
    for out in outs:
        out[...] = acts[row : row + out.shape[0]]
        row += out.shape[0]


def encode(parts, out_rows, weight, bias, after):
    rows = sum(part.shape[0] for part in parts)
    _, width, features = weight.shape
    block = min(512, features)
    anywhere = pl.BlockSpec(memory_space=pl.ANY)
    return pl.pallas_call(
        functools.partial(encode_kernel, len(parts), len(out_rows)),
        grid=(features // block,),
        in_specs=[anywhere] * len(parts)
        + [
            pl.BlockSpec((1, width, block), lambda j: (0, 0, j)),
            pl.BlockSpec((1, block), lambda j: (0, j)),
            anywhere,
        ],
        out_specs=[pl.BlockSpec((n, block), lambda j: (0, j)) for n in out_rows],
        out_shape=[jax.ShapeDtypeStruct((n, features), jnp.bfloat16) for n in out_rows],
        scratch_shapes=[
            pltpu.VMEM((rows, width), jnp.bfloat16),
            pltpu.SemaphoreType.DMA((len(parts),)),
        ],
        compiler_params=pltpu.CompilerParams(vmem_limit_bytes=VMEM_BYTES),
        name="encode",
    )(*parts, weight, bias, after)


def own_kernel(n_parts, info, *refs):
    mine, theirs, refs = refs[:n_parts], refs[n_parts : 2 * n_parts], refs[2 * n_parts :]
    w_mine, w_theirs, out, a_mine, a_theirs, sems = refs
    first = pl.program_id(0) == 0
    has_neighbour = info[1] == 1

    @pl.when(first)
    def _():
        load_rows(mine, a_mine, sems)

    @pl.when(first & has_neighbour)
    def _():
        load_rows(theirs, a_theirs, sems)

    out[...] = jnp.dot(a_mine[...], w_mine[0, 0], preferred_element_type=jnp.float32)

    @pl.when(has_neighbour)
    def _():
        out[...] += jnp.dot(a_theirs[...], w_theirs[0, 0], preferred_element_type=jnp.float32)


def decode_own(info, mine, theirs, decoder, shards):
    rows = sum(part.shape[0] for part in mine)
    _, _, features, width = decoder.shape
    cols = width // shards
    anywhere = pl.BlockSpec(memory_space=pl.ANY)
    return pl.pallas_call(
        functools.partial(own_kernel, len(mine)),
        grid_spec=pltpu.PrefetchScalarGridSpec(
            num_scalar_prefetch=1,
            grid=(shards,),
            in_specs=[anywhere] * (2 * len(mine))
            + [
                pl.BlockSpec((1, 1, features, cols), lambda j, info: (0, 0, 0, info[0] ^ j)),
                pl.BlockSpec(
                    (1, 1, features, cols), lambda j, info: (0, info[1], 0, info[0] ^ (j * info[1]))
                ),
            ],
            out_specs=pl.BlockSpec((rows, cols), lambda j, info: (0, j)),
            scratch_shapes=[
                pltpu.VMEM((rows, features), jnp.bfloat16),
                pltpu.VMEM((rows, features), jnp.bfloat16),
                pltpu.SemaphoreType.DMA((len(mine),)),
            ],
        ),
        out_shape=jax.ShapeDtypeStruct((rows, width), jnp.float32),
        compiler_params=pltpu.CompilerParams(vmem_limit_bytes=VMEM_BYTES),
        name="decode_own",
    )(info, *mine, *theirs, decoder, decoder)


def crossed_kernel(n_parts, shards, info, *refs):
    direct, swapped, refs = refs[:n_parts], refs[n_parts : 2 * n_parts], refs[2 * n_parts :]
    w_direct, w_swapped, base, refs = refs[0], refs[1], refs[2], refs[4:]
    outs, (a_direct, a_swapped, sems) = refs[:shards], refs[shards:]
    step = pl.program_id(0)
    has_crossed = info[2] == 1

    @pl.when((step == 0) & has_crossed)
    def _():
        load_rows(direct, a_direct, sems)
        load_rows(swapped, a_swapped, sems)

    def store(value):
        for r, out in enumerate(outs):

            @pl.when(step == r)
            def _():
                out[...] = value.astype(out.dtype)

    @pl.when(has_crossed)
    def _():
        store(
            base[...]
            + jnp.dot(a_direct[...], w_direct[0, 0], preferred_element_type=jnp.float32)
            + jnp.dot(a_swapped[...], w_swapped[0, 0], preferred_element_type=jnp.float32)
        )

    @pl.when(jnp.logical_not(has_crossed))
    def _():
        store(base[...])


def decode_crossed(info, direct, swapped, decoder, base, row, shards, after):
    rows = sum(part.shape[0] for part in direct)
    _, _, features, width = decoder.shape
    cols = width // shards
    at = row // rows
    anywhere = pl.BlockSpec(memory_space=pl.ANY)
    return pl.pallas_call(
        functools.partial(crossed_kernel, len(direct), shards),
        grid_spec=pltpu.PrefetchScalarGridSpec(
            num_scalar_prefetch=1,
            grid=(shards,),
            in_specs=[anywhere] * (2 * len(direct))
            + [
                pl.BlockSpec(
                    (1, 1, features, cols), lambda j, info: (0, info[3], 0, info[0] ^ (j * info[2]))
                ),
                pl.BlockSpec(
                    (1, 1, features, cols), lambda j, info: (0, info[4], 0, info[0] ^ (j * info[2]))
                ),
                pl.BlockSpec((rows, cols), lambda j, info: (at, j)),
                anywhere,
            ],
            out_specs=[pl.BlockSpec((rows, cols), lambda j, info: (0, 0))] * shards,
            scratch_shapes=[
                pltpu.VMEM((rows, features), jnp.bfloat16),
                pltpu.VMEM((rows, features), jnp.bfloat16),
                pltpu.SemaphoreType.DMA((len(direct),)),
            ],
        ),
        out_shape=[
            jax.ShapeDtypeStruct((rows, cols), jnp.float32 if r == 0 else jnp.bfloat16)
            for r in range(shards)
        ],
        compiler_params=pltpu.CompilerParams(vmem_limit_bytes=VMEM_BYTES),
        name="decode_crossed",
    )(info, *direct, *swapped, decoder, decoder, base, after)


def sum_kernel(blocks, sign, info, base, *refs):
    received, out = refs[:-1], refs[-1]
    me = info[0]
    out[...] = sign * base[...]
    for (source, slot), ref in zip(blocks, received):
        size = ref.shape[0] // len(slot)
        for k, s in enumerate(slot):
            at = pl.ds(pl.multiple_of((me ^ (source ^ s)) * size, size), size)
            out[at, :] += ref[pl.ds(k * size, size), :].astype(jnp.float32)


def add_up(info, base, sign, blocks, received):
    whole = lambda array: pl.BlockSpec(array.shape, lambda i, info: (0, 0))
    return pl.pallas_call(
        functools.partial(sum_kernel, blocks, sign),
        grid_spec=pltpu.PrefetchScalarGridSpec(
            num_scalar_prefetch=1,
            grid=(1,),
            in_specs=[whole(base)] + [whole(array) for array in received],
            out_specs=whole(base),
        ),
        out_shape=jax.ShapeDtypeStruct(base.shape, base.dtype),
        compiler_params=pltpu.CompilerParams(vmem_limit_bytes=VMEM_BYTES),
        name="add_up",
    )(info, base, *received)


def pipelined(layer_inputs, targets, encoder, encoder_bias, decoder):
    shards = lax.axis_size("feat")
    layers = lax.axis_size("layer")
    half = layers // 2
    layer = lax.axis_index("layer")
    feat = lax.axis_index("feat")
    upper = layer >= half
    source = jnp.where(upper, layer - half, 0)
    other = jnp.where(upper, (layer ^ 1) - half, 0)
    info = jnp.stack(
        [
            feat,
            layer & 1,
            upper.astype(jnp.int32),
            jnp.where(upper, layer - source, 0),
            jnp.where(upper, layer - other, 0),
        ]
    ).astype(jnp.int32)

    tokens = layer_inputs[0]
    size = tokens.shape[0]
    mid = shards // 2
    groups = [[0], [1], list(range(2, mid)), list(range(mid, shards - 2)), [shards - 2], [shards - 1]]
    calls = [[0], [1], [2], [3, 4, 5]]
    waves = [[0, 1, 2], [3], [4], [5]]

    inputs = [tokens] + [exchange(tokens, "feat", s) for s in range(1, shards)]
    acts = []
    after = tokens
    for call in calls:
        parts = [inputs[s] for g in call for s in groups[g]]
        rows = [len(groups[g]) * size for g in call]
        acts += encode(parts, rows, encoder, encoder_bias, after)
        after = acts[-1]

    up = [(i, i + half) for i in range(half)]
    across = [(i, i ^ 1) for i in range(half, layers)]
    beside = [(i, i + 1) for i in range(0, layers, 2)]
    direct = [lax.ppermute(a, "layer", up) for a in acts]
    neighbour = [lax.ppermute(a, "layer", beside) for a in acts]
    swapped = [lax.ppermute(a, "layer", across) for a in direct]

    base = decode_own(info, acts, neighbour, decoder, shards)
    total = targets[0]
    sign = -1.0
    row = 0
    after = base
    blocks, received = [], []
    for number, wave in enumerate(waves):
        slots = [s for g in wave for s in groups[g]]
        partial = decode_crossed(
            info,
            [direct[g] for g in wave],
            [swapped[g] for g in wave],
            decoder,
            base,
            row,
            shards,
            after,
        )
        after = partial[0]
        row += len(slots) * size
        if number == len(waves) - 1:
            total = add_up(info, total, sign, blocks, received)
            sign, blocks, received = 1.0, [], []
        for r, part in enumerate(partial):
            blocks.append((r, slots))
            received.append(part if r == 0 else exchange(part, "feat", r))
    return add_up(info, total, sign, blocks, received)[None]


def grouped(layer_inputs, targets, encoder, encoder_bias, decoder):
    groups = lax.axis_size("layer") // L_WIN
    depth_bits = groups.bit_length() - 1
    position = lax.axis_index("layer")
    target_layer = position // groups
    group_index = position % groups
    gathered = lax.all_gather(layer_inputs[0], "feat", axis=0, tiled=True)
    for bit_index in range(depth_bits):
        partner = exchange(gathered, "layer", 1 << bit_index)
        upper_bit = position >> bit_index & 1
        gathered = jnp.where(
            upper_bit == 1,
            jnp.concatenate([partner, gathered], 0),
            jnp.concatenate([gathered, partner], 0),
        )
    preact = (
        jnp.dot(gathered, encoder[0], preferred_element_type=jnp.float32) + encoder_bias[0][None, :]
    )
    features = jax.nn.relu(preact).astype(jnp.bfloat16)
    tok_count = features.shape[0]
    every_layer = lax.all_gather(features[None], "layer", axis=0, tiled=True)
    by_layer = every_layer.reshape(L_WIN, groups, tok_count, features.shape[1])
    mine_only = lax.dynamic_index_in_dim(by_layer, group_index, 1, keepdims=False)
    flipped = mine_only[::-1]
    padded = jnp.concatenate([flipped, jnp.zeros_like(flipped)], 0)
    stacked = lax.dynamic_slice_in_dim(padded, L_WIN - 1 - target_layer, L_WIN, 0)
    rebuilt = jnp.einsum("ktf,kfd->td", stacked, decoder[0], preferred_element_type=jnp.float32)
    for bit_index in reversed(range(depth_bits)):
        half_rows = rebuilt.shape[0] // 2
        upper_bit = position >> bit_index & 1
        kept_half = jnp.where(upper_bit == 1, rebuilt[half_rows:], rebuilt[:half_rows])
        sent_half = jnp.where(upper_bit == 1, rebuilt[:half_rows], rebuilt[half_rows:])
        rebuilt = kept_half + exchange(sent_half, "layer", 1 << bit_index)
    summed = lax.psum_scatter(rebuilt, "feat", scatter_dimension=1, tiled=True)
    residual = summed - targets[0]
    return residual[None]


def solution(mesh):
    placed = (
        P("layer", "feat", None),
        P("layer", None, "feat"),
        P("layer", None, "feat"),
        P("layer", "feat"),
        P("layer", None, "feat", None),
    )
    shards = mesh.shape["feat"]
    simple = mesh.shape["layer"] == L_WIN and shards >= 8 and shards & (shards - 1) == 0
    return jax.shard_map(
        pipelined if simple else grouped,
        mesh=mesh,
        in_specs=placed,
        out_specs=P("layer", None, "feat"),
        check_vma=False,
    )
```

```python
import functools

import jax
import jax.numpy as jnp
from jax import lax
from jax.experimental import pallas as pl
from jax.experimental.pallas import tpu as pltpu
from jax.sharding import PartitionSpec as P

L_WIN = 4
MIB = 1024 * 1024


def exchange(array, axis, flip):
    size = lax.axis_size(axis)
    return lax.ppermute(array, axis, [(i, i ^ flip) for i in range(size)])


ENCODE_MIB = 28
DECODE_MIB = 40
SLOTS = 4
ANYWHERE = pl.BlockSpec(memory_space=pl.ANY)


def streamed(source, buffer, sems):
    slots, block = buffer.shape[0], buffer.shape[1]
    step, steps = pl.program_id(0), pl.num_programs(0)

    def copy(k):
        slot = lax.rem(k, slots)
        rows = pl.ds(pl.multiple_of(k * block, block), block)
        return pltpu.make_async_copy(source.at[rows], buffer.at[slot], sems.at[slot])

    @pl.when(step == 0)
    def _():
        for k in range(slots - 1):
            copy(jnp.int32(k)).start()

    @pl.when(step + slots - 1 < steps)
    def _():
        copy(step + slots - 1).start()

    copy(step).wait()
    return buffer[lax.rem(step, slots)]


def stacked(parts):
    values = [part[...] for part in parts]
    return values[0] if len(values) == 1 else jnp.concatenate(values, axis=0)


def encode_kernel(n_in, n_out, *refs):
    parts, (weight, bias), refs = refs[:n_in], refs[n_in : n_in + 2], refs[n_in + 2 :]
    outs, (total, buffer, sems) = refs[-3 - n_out : -3], refs[-3:]
    step = pl.program_id(0)

    @pl.when(step == 0)
    def _():
        total[...] = jnp.broadcast_to(bias[...], total.shape)

    block = streamed(weight.at[0], buffer, sems)
    total[...] += jnp.dot(stacked(parts), block, preferred_element_type=jnp.float32)

    @pl.when(step == pl.num_programs(0) - 1)
    def _():
        row = 0
        for out in outs:
            size = out.shape[0]
            out[...] = jnp.maximum(total[pl.ds(row, size), :], 0.0).astype(out.dtype)
            row += size


def encode(parts, out_rows, weight, bias, after):
    rows = sum(part.shape[0] for part in parts)
    _, width, features = weight.shape
    block = min(256, width)
    return pl.pallas_call(
        functools.partial(encode_kernel, len(parts), len(out_rows)),
        grid=(width // block,),
        in_specs=[pl.BlockSpec((part.shape[0], block), lambda k: (0, k)) for part in parts]
        + [
            ANYWHERE,
            pl.BlockSpec((1, features), lambda k: (0, 0)),
        ]
        + [ANYWHERE] * len(after),
        out_specs=[pl.BlockSpec((n, features), lambda k: (0, 0)) for n in out_rows],
        out_shape=[jax.ShapeDtypeStruct((n, features), jnp.bfloat16) for n in out_rows],
        scratch_shapes=[
            pltpu.VMEM((rows, features), jnp.float32),
            pltpu.VMEM((SLOTS, block, features), weight.dtype),
            pltpu.SemaphoreType.DMA((SLOTS,)),
        ],
        compiler_params=pltpu.CompilerParams(vmem_limit_bytes=ENCODE_MIB * MIB),
        name="encode",
    )(*parts, weight, bias, *after)


def decode_kernel(n, lags, flags, n_base, n_out, info, *refs):
    first, second, refs = refs[:n], refs[n : 2 * n], refs[2 * n :]
    weights, base, refs = refs[0], refs[1 : 1 + n_base], refs[1 + n_base :]
    buffers, sems, refs = refs[-4:-2], refs[-2:], refs[:-4]
    if n_out:
        out, total = refs[-2:]
    else:
        out = total = refs[-1]
    step = pl.program_id(0)

    @pl.when(step == 0)
    def _():
        total[...] = base[0][...] if n_base else jnp.zeros_like(total)

    def add(parts, lag, buffer, sem):
        block = streamed(weights.at[0, 0 if lag is None else info[lag]], buffer, sem)
        total[...] += jnp.dot(stacked(parts), block, preferred_element_type=jnp.float32)

    for flag, *source in zip(flags, (first, second), lags, buffers, sems):
        if flag is None:
            add(*source)
        else:
            pl.when(info[flag] == 1)(functools.partial(add, *source))

    if n_out:

        @pl.when(step == pl.num_programs(0) - 1)
        def _():
            for j in range(n_out):
                cols = out.shape[2]
                out[j] = total[:, j * cols : (j + 1) * cols].astype(out.dtype)


def decode(info, first, second, decoder, lags, flags, base, row, shards, after):
    n = len(first)
    rows = sum(part.shape[0] for part in first)
    _, _, features, width = decoder.shape
    block = min(512, features)

    def masked(k, info, flag):
        return k if flag is None else k * info[flag]

    def acts(part, flag):
        return pl.BlockSpec((part.shape[0], block), lambda k, info: (0, masked(k, info, flag)))

    in_specs = [acts(part, flags[0]) for part in first] + [acts(part, flags[1]) for part in second]
    in_specs.append(ANYWHERE)
    operands = [*first, *second, decoder]
    if base is not None:
        at = row // rows
        in_specs.append(
            pl.BlockSpec((rows, width), lambda k, info: (at, 0), pipeline_mode=pl.Buffered(1))
        )
        operands.append(base)
        shape, dtype = (shards, rows, width // shards), jnp.bfloat16
    else:
        shape, dtype = (rows, width), jnp.float32
    return pl.pallas_call(
        functools.partial(
            decode_kernel, n, lags, flags, int(base is not None), 0 if base is None else shards
        ),
        grid_spec=pltpu.PrefetchScalarGridSpec(
            num_scalar_prefetch=1,
            grid=(features // block,),
            in_specs=in_specs + [ANYWHERE] * len(after),
            out_specs=pl.BlockSpec(shape, lambda k, info: (0,) * len(shape)),
            scratch_shapes=([] if base is None else [pltpu.VMEM((rows, width), jnp.float32)])
            + [pltpu.VMEM((SLOTS, block, width), decoder.dtype)] * 2
            + [pltpu.SemaphoreType.DMA((SLOTS,))] * 2,
        ),
        out_shape=jax.ShapeDtypeStruct(shape, dtype),
        compiler_params=pltpu.CompilerParams(vmem_limit_bytes=DECODE_MIB * MIB),
        name="decode_own" if base is None else "decode_crossed",
    )(info, *operands, *after)


def sum_kernel(sign, slots, base, *refs):
    received, out = refs[: len(slots)], refs[-1]
    out[...] = sign * base[...]
    for ref, blocks in zip(received, slots):
        size = ref.shape[1] // len(blocks)
        for source in range(ref.shape[0]):
            for k, s in enumerate(blocks):
                at = pl.ds((source ^ s) * size, size)
                out[at, :] += ref[source, pl.ds(k * size, size), :].astype(jnp.float32)


def add_up(base, sign, slots, received, after):
    return pl.pallas_call(
        functools.partial(sum_kernel, sign, slots),
        in_specs=[pl.BlockSpec(memory_space=pltpu.VMEM)] * (1 + len(received))
        + [ANYWHERE] * len(after),
        out_specs=pl.BlockSpec(memory_space=pltpu.VMEM),
        out_shape=jax.ShapeDtypeStruct(base.shape, base.dtype),
        compiler_params=pltpu.CompilerParams(vmem_limit_bytes=ENCODE_MIB * MIB),
        name="add_up",
    )(base, *received, *after)


def pipelined(layer_inputs, targets, encoder, encoder_bias, decoder):
    shards = lax.axis_size("feat")
    layers = lax.axis_size("layer")
    half = layers // 2
    layer = lax.axis_index("layer")
    upper = layer >= half
    info = jnp.stack(
        [
            layer & 1,
            upper.astype(jnp.int32),
            jnp.full_like(layer, half),
            jnp.where(upper, layer - ((layer ^ 1) - half), 0),
        ]
    ).astype(jnp.int32)
    odd_, upper_, lag_direct, lag_swapped = range(4)

    def up(a):
        return lax.ppermute(a, "layer", [(i, i + half) for i in range(half)])

    def across(a):
        return lax.ppermute(a, "layer", [(i, i ^ 1) for i in range(half, layers)])

    def beside(a):
        return lax.ppermute(a, "layer", [(i, i + 1) for i in range(0, layers, 2)])

    def scatter(partial):
        return lax.all_to_all(partial, "feat", 0, 0)

    def run_encode(slots, after):
        parts = [x[s] for s in slots]
        return encode(parts, [len(slots) * size], encoder, encoder_bias, after)[0]

    x = {0: layer_inputs[0]}
    size = x[0].shape[0]
    for s in range(1, shards):
        if s == 1 or s % 2 == 0:
            x[s] = exchange(x[0], "feat", s)
    for s in range(3, shards, 2):
        x[s] = exchange(x[s - 1], "feat", 1)
    slots = [[0], [1, 2], [3] + list(range(4, shards, 2)), list(range(5, shards, 2))]

    a0 = run_encode(slots[0], [])
    d0, n0 = up(a0), beside(a0)
    a1 = run_encode(slots[1], [a0])
    d1, n1 = up(a1), beside(a1)
    a2 = run_encode(slots[2], [a1, d0])
    d2, n2 = up(a2), beside(a2)
    a3 = run_encode(slots[3], [a2, d1])
    d3, n3 = up(a3), beside(a3)
    acts = [a0, a1, a2, a3]
    d0, d1, _ = lax.optimization_barrier((d0, d1, a3))
    c0, c1 = across(d0), across(d1)
    base = decode(
        info, acts, [n0, n1, n2, n3], decoder, (None, odd_), (None, odd_), None, 0, shards, []
    )
    lags, flags = (lag_direct, lag_swapped), (upper_, upper_)
    waves = [slots[0] + slots[1], slots[2], slots[3]]
    p0 = decode(info, [d0, d1], [c0, c1], decoder, lags, flags, base, 0, shards, [])
    r0 = scatter(p0)
    d2, _ = lax.optimization_barrier((d2, p0))
    c2 = across(d2)
    row = size * len(waves[0])
    p1 = decode(info, [d2], [c2], decoder, lags, flags, base, row, shards, [p0])
    r1 = scatter(p1)
    d3, _ = lax.optimization_barrier((d3, p1))
    c3 = across(d3)
    row += size * len(waves[1])
    p2 = decode(info, [d3], [c3], decoder, lags, flags, base, row, shards, [p1])
    r2 = scatter(p2)
    total = add_up(targets[0], -1.0, waves[:2], [r0, r1], [p2])
    return add_up(total, 1.0, waves[2:], [r2], [])[None]


def grouped(layer_inputs, targets, encoder, encoder_bias, decoder):
    groups = lax.axis_size("layer") // L_WIN
    depth_bits = groups.bit_length() - 1
    position = lax.axis_index("layer")
    target_layer = position // groups
    group_index = position % groups
    gathered = lax.all_gather(layer_inputs[0], "feat", axis=0, tiled=True)
    for bit_index in range(depth_bits):
        partner = exchange(gathered, "layer", 1 << bit_index)
        upper_bit = position >> bit_index & 1
        gathered = jnp.where(
            upper_bit == 1,
            jnp.concatenate([partner, gathered], 0),
            jnp.concatenate([gathered, partner], 0),
        )
    preact = (
        jnp.dot(gathered, encoder[0], preferred_element_type=jnp.float32) + encoder_bias[0][None, :]
    )
    features = jax.nn.relu(preact).astype(jnp.bfloat16)
    tok_count = features.shape[0]
    every_layer = lax.all_gather(features[None], "layer", axis=0, tiled=True)
    by_layer = every_layer.reshape(L_WIN, groups, tok_count, features.shape[1])
    mine_only = lax.dynamic_index_in_dim(by_layer, group_index, 1, keepdims=False)
    flipped = mine_only[::-1]
    padded = jnp.concatenate([flipped, jnp.zeros_like(flipped)], 0)
    stacked = lax.dynamic_slice_in_dim(padded, L_WIN - 1 - target_layer, L_WIN, 0)
    rebuilt = jnp.einsum("ktf,kfd->td", stacked, decoder[0], preferred_element_type=jnp.float32)
    for bit_index in reversed(range(depth_bits)):
        half_rows = rebuilt.shape[0] // 2
        upper_bit = position >> bit_index & 1
        kept_half = jnp.where(upper_bit == 1, rebuilt[half_rows:], rebuilt[:half_rows])
        sent_half = jnp.where(upper_bit == 1, rebuilt[:half_rows], rebuilt[half_rows:])
        rebuilt = kept_half + exchange(sent_half, "layer", 1 << bit_index)
    summed = lax.psum_scatter(rebuilt, "feat", scatter_dimension=1, tiled=True)
    residual = summed - targets[0]
    return residual[None]


def solution(mesh):
    placed = (
        P("layer", "feat", None),
        P("layer", None, "feat"),
        P("layer", None, "feat"),
        P("layer", "feat"),
        P("layer", None, "feat", None),
    )
    shards = mesh.shape["feat"]
    simple = mesh.shape["layer"] == L_WIN and shards >= 8 and shards & (shards - 1) == 0
    return jax.shard_map(
        pipelined if simple else grouped,
        mesh=mesh,
        in_specs=placed,
        out_specs=P("layer", None, "feat"),
        check_vma=False,
    )
```

```python
import functools

import jax
import jax.numpy as jnp
from jax import lax
from jax.experimental import pallas as pl
from jax.experimental.pallas import tpu as pltpu
from jax.sharding import PartitionSpec as P

L_WIN = 4
MIB = 1024 * 1024


def exchange(array, axis, flip):
    size = lax.axis_size(axis)
    return lax.ppermute(array, axis, [(i, i ^ flip) for i in range(size)])


ANYWHERE = pl.BlockSpec(memory_space=pl.ANY)
WHOLE = pl.BlockSpec(memory_space=pltpu.VMEM)
SLOTS = 3
ENCODE_MIB = 12
FIRST_MIB = 46
LATER_MIB = 26


def encode_kernel(n_in, n_out, *refs):
    parts, (weight, bias), refs = refs[:n_in], refs[n_in : n_in + 2], refs[n_in + 2 :]
    outs, tokens = refs[-1 - n_out : -1], refs[-1]
    row = 0
    for part in parts:
        size = part.shape[0]
        tokens[pl.ds(row, size), :] = part[...]
        row += size
    features = weight.shape[2]
    block = min(512, features)

    @pl.loop(0, features // block)
    def _(j):
        cols = pl.ds(pl.multiple_of(j * block, block), block)
        preact = jnp.dot(tokens[...], weight[0, :, cols], preferred_element_type=jnp.float32)
        acts = jnp.maximum(preact + bias[:, cols], 0.0).astype(jnp.bfloat16)
        row = 0
        for out in outs:
            size = out.shape[0]
            out[:, cols] = acts[row : row + size]
            row += size


def first_kernel(*refs):
    *parts, weight, bias, out, keep, tokens, sems = refs
    row = 0
    features = weight.shape[2]
    block = features // sems.shape[0]

    def fetch(j):
        cols = pl.ds(pl.multiple_of(j * block, block), block)
        return pltpu.make_async_copy(weight.at[0, :, cols], keep.at[0, :, cols], sems.at[j])

    for j in range(sems.shape[0]):
        fetch(jnp.int32(j)).start()
    for part in parts:
        size = part.shape[0]
        tokens[pl.ds(row, size), :] = part[...]
        row += size

    @pl.loop(0, sems.shape[0])
    def _(j):
        fetch(j).wait()
        cols = pl.ds(pl.multiple_of(j * block, block), block)
        preact = jnp.dot(tokens[...], keep[0, :, cols], preferred_element_type=jnp.float32)
        out[:, cols] = jnp.maximum(preact + bias[:, cols], 0.0).astype(out.dtype)


def encode_first(parts, weight, bias):
    rows = sum(part.shape[0] for part in parts)
    _, width, features = weight.shape
    steps = max(1, features // 512)
    return pl.pallas_call(
        first_kernel,
        in_specs=[WHOLE] * len(parts) + [ANYWHERE, WHOLE],
        out_specs=[WHOLE, WHOLE],
        out_shape=[
            jax.ShapeDtypeStruct((rows, features), jnp.bfloat16),
            pltpu.VMEM(weight.shape, weight.dtype),
        ],
        scratch_shapes=[pltpu.VMEM((rows, width), jnp.bfloat16), pltpu.SemaphoreType.DMA((steps,))],
        compiler_params=pltpu.CompilerParams(vmem_limit_bytes=ENCODE_MIB * MIB),
        name="encode_first",
    )(*parts, weight, bias)


def encode(parts, out_rows, weight, bias, after):
    rows = sum(part.shape[0] for part in parts)
    _, width, features = weight.shape
    return pl.pallas_call(
        functools.partial(encode_kernel, len(parts), len(out_rows)),
        in_specs=[WHOLE] * (len(parts) + 2) + [ANYWHERE] * len(after),
        out_specs=[WHOLE] * len(out_rows),
        out_shape=[jax.ShapeDtypeStruct((n, features), jnp.bfloat16) for n in out_rows],
        scratch_shapes=[pltpu.VMEM((rows, width), jnp.bfloat16)],
        compiler_params=pltpu.CompilerParams(vmem_limit_bytes=ENCODE_MIB * MIB),
        name="encode",
    )(*parts, weight, bias, *after)


def wave_kernel(pairs, base_row, n_base, keep_total, n_parts, info, *refs):
    parts, refs = refs[:n_parts], refs[n_parts:]
    weights, base, refs = refs[0], refs[1 : 1 + n_base], refs[1 + n_base :]
    n_rings = 2 * len(pairs)
    rings, sems, refs = refs[-2 * n_rings : -n_rings], refs[-n_rings:], refs[: -2 * n_rings]
    out, total = refs[-2:]
    step, steps = pl.program_id(0), pl.num_programs(0)
    slots, block = rings[0].shape[0], rings[0].shape[1]

    def on(flag, action):
        if flag is None:
            action()
        else:
            pl.when(info[flag] == 1)(action)

    def fetch(i, lag, k):
        slot = lax.rem(k, slots)
        rows = pl.ds(pl.multiple_of(k * block, block), block)
        source = weights.at[0, 0 if lag is None else info[lag], rows]
        return pltpu.make_async_copy(source, rings[i].at[slot], sems[i].at[slot])

    def fetch_all(k):
        for i, (_, lag, flag) in enumerate(s for _, _, *pair in pairs for s in pair):
            on(flag, lambda: fetch(i, lag, k).start())

    @pl.when(step == 0)
    def _():
        for k in range(slots - 1):
            fetch_all(jnp.int32(k))

    pl.when(step + slots - 1 < steps)(lambda: fetch_all(step + slots - 1))

    @pl.when(step == 0)
    def _():
        total[...] = base[0][pl.ds(base_row, total.shape[0]), :] if n_base else jnp.zeros_like(total)

    def product(i, source):
        places, lag, _ = source
        fetch(i, lag, step).wait()
        values = [parts[p][...] for p in places]
        acts = values[0] if len(values) == 1 else jnp.concatenate(values, axis=0)
        return jnp.dot(acts, rings[i][lax.rem(step, slots)], preferred_element_type=jnp.float32)

    for number, (row, size, first, second) in enumerate(pairs):
        at = pl.ds(row, size)
        i = 2 * number

        def both():
            total[at, :] += product(i, first) + product(i + 1, second)

        def one():
            total[at, :] += product(i, first)

        if first[2] is None:
            pl.when(info[second[2]] == 0)(one)
        pl.when(info[second[2]] == 1)(both)

    @pl.when(step == steps - 1)
    def _():
        cols = out.shape[2]
        for j in range(out.shape[0]):
            out[j] = total[: out.shape[1], j * cols : (j + 1) * cols].astype(out.dtype)


def decode_wave(info, pairs, decoder, base, base_row, done_rows, keep_total, shards, after, limit):
    _, _, features, width = decoder.shape
    block = min(512, features)
    rows = max(row + size for row, size, _, _ in pairs)
    operands, in_specs, numbered = [], [], []
    for row, size, *pair in pairs:
        placed = []
        for parts, lag, flag in pair:
            places = []
            for part in parts:
                places.append(len(operands))
                operands.append(part)
                in_specs.append(
                    pl.BlockSpec(
                        (part.shape[0], block),
                        lambda k, info, flag=flag: (0, k if flag is None else k * info[flag]),
                    )
                )
            placed.append((tuple(places), lag, flag))
        numbered.append((row, size, *placed))
    n_parts = len(operands)
    operands.append(decoder)
    in_specs.append(ANYWHERE)
    if base is not None:
        operands.append(base)
        in_specs.append(
            pl.BlockSpec(base.shape, lambda k, info: (0, 0), pipeline_mode=pl.Buffered(1))
        )
    total_shape = jax.ShapeDtypeStruct((rows, width), jnp.float32)
    out_shape = jax.ShapeDtypeStruct((shards, done_rows, width // shards), jnp.bfloat16)
    out_spec = pl.BlockSpec(out_shape.shape, lambda k, info: (0, 0, 0))
    total_spec = pl.BlockSpec(total_shape.shape, lambda k, info: (0, 0))
    return pl.pallas_call(
        functools.partial(
            wave_kernel, numbered, base_row, int(base is not None), keep_total, n_parts
        ),
        grid_spec=pltpu.PrefetchScalarGridSpec(
            num_scalar_prefetch=1,
            grid=(features // block,),
            in_specs=in_specs + [ANYWHERE] * len(after),
            out_specs=[out_spec, total_spec] if keep_total else [out_spec],
            scratch_shapes=([] if keep_total else [pltpu.VMEM(total_shape.shape, jnp.float32)])
            + [pltpu.VMEM((SLOTS, block, width), decoder.dtype)] * (2 * len(pairs))
            + [pltpu.SemaphoreType.DMA((SLOTS,))] * (2 * len(pairs)),
        ),
        out_shape=[out_shape, total_shape] if keep_total else [out_shape],
        compiler_params=pltpu.CompilerParams(vmem_limit_bytes=limit * MIB),
        name="decode_wave",
    )(info, *operands, *after)


def sum_kernel(sign, slots, base, *refs):
    received, out = refs[: len(slots)], refs[-1]
    out[...] = sign * base[...]
    for ref, blocks in zip(received, slots):
        size = ref.shape[1] // len(blocks)
        for source in range(ref.shape[0]):
            for k, s in enumerate(blocks):
                at = pl.ds((source ^ s) * size, size)
                out[at, :] += ref[source, pl.ds(k * size, size), :].astype(jnp.float32)


def add_up(base, sign, slots, received, after):
    return pl.pallas_call(
        functools.partial(sum_kernel, sign, slots),
        in_specs=[WHOLE] * (1 + len(received)) + [ANYWHERE] * len(after),
        out_specs=WHOLE,
        out_shape=jax.ShapeDtypeStruct(base.shape, base.dtype),
        compiler_params=pltpu.CompilerParams(vmem_limit_bytes=ENCODE_MIB * MIB),
        name="add_up",
    )(base, *received, *after)


def pipelined(layer_inputs, targets, encoder, encoder_bias, decoder):
    shards = lax.axis_size("feat")
    layers = lax.axis_size("layer")
    half = layers // 2
    layer = lax.axis_index("layer")
    upper = layer >= half
    info = jnp.stack(
        [
            layer & 1,
            upper.astype(jnp.int32),
            jnp.full_like(layer, half),
            jnp.where(upper, layer - ((layer ^ 1) - half), 0),
        ]
    ).astype(jnp.int32)

    def up(a):
        return lax.ppermute(a, "layer", [(i, i + half) for i in range(half)])

    def across(a):
        return lax.ppermute(a, "layer", [(i, i ^ 1) for i in range(half, layers)])

    def beside(a):
        return lax.ppermute(a, "layer", [(i, i + 1) for i in range(0, layers, 2)])

    def scatter(partial):
        return lax.all_to_all(partial, "feat", 0, 0)

    def after(value, *earlier):
        return lax.optimization_barrier((value, *earlier))[0]

    tokens = layer_inputs[0]
    size = tokens.shape[0]
    near = exchange(tokens, "feat", 1)
    far = [exchange(tokens, "feat", s) for s in range(2, shards, 2)]
    a0, kept = encode_first([tokens, near], pltpu.with_memory_space_constraint(encoder, pltpu.HBM), encoder_bias)
    weight = pltpu.with_memory_space_constraint(kept, pltpu.VMEM)
    def run_encode(parts, earlier):
        return encode(parts, [sum(p.shape[0] for p in parts)], weight, encoder_bias, earlier)[0]

    d0, n0 = up(a0), beside(a0)
    rest = exchange(jnp.concatenate(far, axis=0), "feat", 1)
    a1 = run_encode(far, [a0])
    d1, n1 = up(a1), beside(a1)
    a2 = run_encode([rest], [a1, d0])
    d2, n2 = up(a2), beside(a2)
    slots = [[0, 1], list(range(2, shards, 2)), list(range(3, shards, 2))]

    odd_, upper_, lag_direct, lag_swapped = range(4)
    c0 = across(after(d0, a2))
    held = 2 * size
    wave, base = decode_wave(
        info,
        [
            (0, shards * size, ([a0, a1, a2], None, None), ([n0, n1, n2], odd_, odd_)),
            (0, held, ([d0], lag_direct, upper_), ([c0], lag_swapped, upper_)),
        ],
        decoder,
        None,
        0,
        held,
        True,
        shards,
        [],
        FIRST_MIB,
    )
    received = [scatter(wave)]
    row = held
    for blocks, d in zip(slots[1:], (d1, d2)):
        d = after(d, wave)
        rows = size * len(blocks)
        c = across(d)
        (wave,) = decode_wave(
            info,
            [(0, rows, ([d], lag_direct, upper_), ([c], lag_swapped, upper_))],
            decoder,
            base,
            row,
            rows,
            False,
            shards,
            [wave],
            LATER_MIB,
        )
        received.append(scatter(wave))
        row += rows
    total = add_up(targets[0], -1.0, slots[:2], received[:2], [wave])
    return add_up(total, 1.0, slots[2:], received[2:], [])[None]


def grouped(layer_inputs, targets, encoder, encoder_bias, decoder):
    groups = lax.axis_size("layer") // L_WIN
    depth_bits = groups.bit_length() - 1
    position = lax.axis_index("layer")
    target_layer = position // groups
    group_index = position % groups
    gathered = lax.all_gather(layer_inputs[0], "feat", axis=0, tiled=True)
    for bit_index in range(depth_bits):
        partner = exchange(gathered, "layer", 1 << bit_index)
        upper_bit = position >> bit_index & 1
        gathered = jnp.where(
            upper_bit == 1,
            jnp.concatenate([partner, gathered], 0),
            jnp.concatenate([gathered, partner], 0),
        )
    preact = (
        jnp.dot(gathered, encoder[0], preferred_element_type=jnp.float32) + encoder_bias[0][None, :]
    )
    features = jax.nn.relu(preact).astype(jnp.bfloat16)
    tok_count = features.shape[0]
    every_layer = lax.all_gather(features[None], "layer", axis=0, tiled=True)
    by_layer = every_layer.reshape(L_WIN, groups, tok_count, features.shape[1])
    mine_only = lax.dynamic_index_in_dim(by_layer, group_index, 1, keepdims=False)
    flipped = mine_only[::-1]
    padded = jnp.concatenate([flipped, jnp.zeros_like(flipped)], 0)
    stacked = lax.dynamic_slice_in_dim(padded, L_WIN - 1 - target_layer, L_WIN, 0)
    rebuilt = jnp.einsum("ktf,kfd->td", stacked, decoder[0], preferred_element_type=jnp.float32)
    for bit_index in reversed(range(depth_bits)):
        half_rows = rebuilt.shape[0] // 2
        upper_bit = position >> bit_index & 1
        kept_half = jnp.where(upper_bit == 1, rebuilt[half_rows:], rebuilt[:half_rows])
        sent_half = jnp.where(upper_bit == 1, rebuilt[:half_rows], rebuilt[half_rows:])
        rebuilt = kept_half + exchange(sent_half, "layer", 1 << bit_index)
    summed = lax.psum_scatter(rebuilt, "feat", scatter_dimension=1, tiled=True)
    residual = summed - targets[0]
    return residual[None]


def solution(mesh):
    placed = (
        P("layer", "feat", None),
        P("layer", None, "feat"),
        P("layer", None, "feat"),
        P("layer", "feat"),
        P("layer", None, "feat", None),
    )
    shards = mesh.shape["feat"]
    simple = mesh.shape["layer"] == L_WIN and shards >= 8 and shards & (shards - 1) == 0
    return jax.shard_map(
        pipelined if simple else grouped,
        mesh=mesh,
        in_specs=placed,
        out_specs=P("layer", None, "feat"),
        check_vma=False,
    )
```

```python
import functools

import jax
import jax.numpy as jnp
from jax import lax
from jax.experimental import pallas as pl
from jax.experimental.pallas import tpu as pltpu
from jax.sharding import PartitionSpec as P

L_WIN = 4
MIB = 1024 * 1024


def exchange(array, axis, flip):
    size = lax.axis_size(axis)
    return lax.ppermute(array, axis, [(i, i ^ flip) for i in range(size)])


ANYWHERE = pl.BlockSpec(memory_space=pl.ANY)
WHOLE = pl.BlockSpec(memory_space=pltpu.VMEM)
SLOTS = 3
ENCODE_MIB = 12
DECODE_MIB = 26


def fill(order, parts, rows_of):
    at = 0
    for part, row, size in order:
        rows_of[pl.ds(at, size), :] = parts[part][pl.ds(row, size), :]
        at += size


def encode_kernel(order, pieces, n_in, n_after, stream, *refs):
    parts, weight, bias, refs = refs[:n_in], refs[n_in], refs[n_in + 1], refs[n_in + 2 + n_after :]
    outs, refs = refs[: len(pieces)], refs[len(pieces) :]
    features = weight.shape[2]
    if stream:
        kept, tokens, sems = refs
        block = features // sems.shape[0]
    else:
        kept, (tokens,) = weight, refs
        block = min(512, features)

    def fetch(j):
        cols = pl.ds(pl.multiple_of(j * block, block), block)
        return pltpu.make_async_copy(weight.at[0, :, cols], kept.at[0, :, cols], sems.at[j])

    if stream:
        for j in range(features // block):
            fetch(jnp.int32(j)).start()
    fill(order, parts, tokens)

    @pl.loop(0, features // block)
    def _(j):
        if stream:
            fetch(j).wait()
        cols = pl.ds(pl.multiple_of(j * block, block), block)
        preact = jnp.dot(tokens[...], kept[0, :, cols], preferred_element_type=jnp.float32)
        acts = jnp.maximum(preact + bias[:, cols], 0.0).astype(jnp.bfloat16)
        for out, (row, size) in zip(outs, pieces):
            out[:, cols] = acts[row : row + size]


def encode(parts, order, pieces, weight, bias, after, stream=False):
    rows = sum(size for _, _, size in order)
    _, width, features = weight.shape
    out_shape = [jax.ShapeDtypeStruct((size, features), jnp.bfloat16) for _, size in pieces]
    scratch = [pltpu.VMEM((rows, width), jnp.bfloat16)]
    if stream:
        out_shape.append(pltpu.VMEM(weight.shape, weight.dtype))
        scratch.append(pltpu.SemaphoreType.DMA((max(1, features // 512),)))
        weight = pltpu.with_memory_space_constraint(weight, pltpu.HBM)
    else:
        weight = pltpu.with_memory_space_constraint(weight, pltpu.VMEM)
    return pl.pallas_call(
        functools.partial(encode_kernel, order, pieces, len(parts), len(after), stream),
        in_specs=[WHOLE] * len(parts) + [ANYWHERE if stream else WHOLE, WHOLE] + [ANYWHERE] * len(after),
        out_specs=[WHOLE] * len(out_shape),
        out_shape=out_shape,
        scratch_shapes=scratch,
        compiler_params=pltpu.CompilerParams(vmem_limit_bytes=ENCODE_MIB * MIB),
        name="encode",
    )(*parts, weight, bias, *after)


def first_wave_kernel(counts, info, *refs):
    groups = []
    for count in counts:
        groups.append(refs[:count])
        refs = refs[count:]
    mine, theirs, direct, swapped = groups
    weights, out, total, *kept = refs[:5]
    rings, ring_sems, kept_sems = refs[-3:]
    step, steps = pl.program_id(0), pl.num_programs(0)
    slots, block = rings.shape[1], rings.shape[2]
    odd, upper = info[0] == 1, info[1] == 1

    def rows(k):
        return pl.ds(pl.multiple_of(k * block, block), block)

    def fetch(source, k):
        slot = lax.rem(k, slots)
        return pltpu.make_async_copy(
            weights.at[0, source, rows(k)], rings.at[source, slot], ring_sems.at[source, slot]
        )

    def keep(source, k):
        return pltpu.make_async_copy(
            weights.at[0, info[2 + source], rows(k)],
            kept[source].at[rows(k)],
            kept_sems.at[source, k],
        )

    def fetch_all(k):
        fetch(0, k).start()
        pl.when(odd)(lambda: fetch(1, k).start())

        @pl.when(upper)
        def _():
            keep(0, k).start()
            keep(1, k).start()

    @pl.when(step == 0)
    def _():
        for k in range(slots - 1):
            fetch_all(jnp.int32(k))
        total[...] = jnp.zeros_like(total)

    pl.when(step + slots - 1 < steps)(lambda: fetch_all(step + slots - 1))

    def product(parts, weight):
        values = [part[...] for part in parts]
        acts = values[0] if len(values) == 1 else jnp.concatenate(values, axis=0)
        return jnp.dot(acts, weight, preferred_element_type=jnp.float32)

    slot = lax.rem(step, slots)
    fetch(0, step).wait()

    @pl.when(jnp.logical_not(odd))
    def _():
        total[...] += product(mine, rings[0, slot])

    @pl.when(odd)
    def _():
        fetch(1, step).wait()
        total[...] += product(mine, rings[0, slot]) + product(theirs, rings[1, slot])

    done = out.shape[1]

    @pl.when(upper)
    def _():
        keep(0, step).wait()
        keep(1, step).wait()
        total[:done, :] += product(direct, kept[0][rows(step), :]) + product(
            swapped, kept[1][rows(step), :]
        )

    @pl.when(step == steps - 1)
    def _():
        cols = out.shape[2]
        for j in range(out.shape[0]):
            out[j] = total[:done, j * cols : (j + 1) * cols].astype(out.dtype)


def decode_first(info, mine, theirs, direct, swapped, decoder, shards, after):
    _, _, features, width = decoder.shape
    block = min(512, features)
    steps = features // block
    rows = sum(part.shape[0] for part in mine)
    done = sum(part.shape[0] for part in direct)

    def acts(part, flag):
        return pl.BlockSpec(
            (part.shape[0], block), lambda k, info: (0, k if flag is None else k * info[flag])
        )

    groups = (mine, theirs, direct, swapped)
    in_specs = [acts(p, flag) for parts, flag in zip(groups, (None, 0, 1, 1)) for p in parts]
    return pl.pallas_call(
        functools.partial(first_wave_kernel, [len(parts) for parts in groups]),
        grid_spec=pltpu.PrefetchScalarGridSpec(
            num_scalar_prefetch=1,
            grid=(steps,),
            in_specs=in_specs + [ANYWHERE] * (1 + len(after)),
            out_specs=[
                pl.BlockSpec((shards, done, width // shards), lambda k, info: (0, 0, 0)),
                pl.BlockSpec((rows, width), lambda k, info: (0, 0)),
                WHOLE,
                WHOLE,
            ],
            scratch_shapes=[
                pltpu.VMEM((2, SLOTS, block, width), decoder.dtype),
                pltpu.SemaphoreType.DMA((2, SLOTS)),
                pltpu.SemaphoreType.DMA((2, steps)),
            ],
        ),
        out_shape=[
            jax.ShapeDtypeStruct((shards, done, width // shards), jnp.bfloat16),
            pltpu.HBM((rows, width), jnp.float32),
            pltpu.VMEM((features, width), decoder.dtype),
            pltpu.VMEM((features, width), decoder.dtype),
        ],
        compiler_params=pltpu.CompilerParams(vmem_limit_bytes=DECODE_MIB * MIB),
        name="decode_first",
    )(info, *sum(groups, []), decoder, *after)


def later_wave_kernel(order, row, n, info, *refs):
    direct, swapped, (base, *kept) = refs[:n], refs[n : 2 * n], refs[2 * n : 2 * n + 3]
    out, first, second, start, sem = refs[-5:]
    rows = out.shape[1]
    shards, cols = out.shape[0], out.shape[2]
    span = 2 if shards % 2 == 0 else 1
    copy = pltpu.make_async_copy(base.at[pl.ds(row, rows)], start, sem)
    copy.start()
    fill(order, direct, first)
    fill(order, swapped, second)
    copy.wait()

    @pl.loop(0, shards // span)
    def _(j):
        at = pl.ds(pl.multiple_of(j * span * cols, span * cols), span * cols)

        def store(value):
            for i in range(span):
                out[j * span + i] = value[:, i * cols : (i + 1) * cols].astype(out.dtype)

        @pl.when(info[1] == 1)
        def _():
            store(
                start[:, at]
                + jnp.dot(first[...], kept[0][:, at], preferred_element_type=jnp.float32)
                + jnp.dot(second[...], kept[1][:, at], preferred_element_type=jnp.float32)
            )

        @pl.when(info[1] == 0)
        def _():
            store(start[:, at])


def decode_later(info, direct, swapped, order, base, kept, row, shards, after):
    rows = sum(size for _, _, size in order)
    features, width = kept[0].shape
    kept = [pltpu.with_memory_space_constraint(weight, pltpu.VMEM) for weight in kept]
    return pl.pallas_call(
        functools.partial(later_wave_kernel, order, row, len(direct)),
        in_specs=[pl.BlockSpec(memory_space=pltpu.SMEM)]
        + [WHOLE] * (2 * len(direct))
        + [ANYWHERE, WHOLE, WHOLE]
        + [ANYWHERE] * len(after),
        out_specs=WHOLE,
        out_shape=jax.ShapeDtypeStruct((shards, rows, width // shards), jnp.bfloat16),
        scratch_shapes=[
            pltpu.VMEM((rows, features), jnp.bfloat16),
            pltpu.VMEM((rows, features), jnp.bfloat16),
            pltpu.VMEM((rows, width), jnp.float32),
            pltpu.SemaphoreType.DMA,
        ],
        compiler_params=pltpu.CompilerParams(vmem_limit_bytes=DECODE_MIB * MIB),
        name="decode_later",
    )(info, *direct, *swapped, base, *kept, *after)


def sum_kernel(sign, slots, base, *refs):
    received, out = refs[: len(slots)], refs[-1]
    out[...] = sign * base[...]
    for ref, blocks in zip(received, slots):
        size = ref.shape[1] // len(blocks)
        for source in range(ref.shape[0]):
            for k, s in enumerate(blocks):
                at = pl.ds((source ^ s) * size, size)
                out[at, :] += ref[source, pl.ds(k * size, size), :].astype(jnp.float32)


def add_up(base, sign, slots, received, after):
    return pl.pallas_call(
        functools.partial(sum_kernel, sign, slots),
        in_specs=[WHOLE] * (1 + len(received)) + [ANYWHERE] * len(after),
        out_specs=WHOLE,
        out_shape=jax.ShapeDtypeStruct(base.shape, base.dtype),
        compiler_params=pltpu.CompilerParams(vmem_limit_bytes=ENCODE_MIB * MIB),
        name="add_up",
    )(base, *received, *after)


def pipelined(layer_inputs, targets, encoder, encoder_bias, decoder):
    shards = lax.axis_size("feat")
    layers = lax.axis_size("layer")
    half = layers // 2
    layer = lax.axis_index("layer")
    upper = layer >= half
    info = jnp.stack(
        [
            layer & 1,
            upper.astype(jnp.int32),
            jnp.full_like(layer, half),
            jnp.where(upper, layer - ((layer ^ 1) - half), 0),
        ]
    ).astype(jnp.int32)

    def up(a):
        return lax.ppermute(a, "layer", [(i, i + half) for i in range(half)])

    def across(a):
        return lax.ppermute(a, "layer", [(i, i ^ 1) for i in range(half, layers)])

    def beside(a):
        return lax.ppermute(a, "layer", [(i, i + 1) for i in range(0, layers, 2)])

    def scatter(partial):
        return lax.all_to_all(partial, "feat", 0, 0)

    def after(value, *earlier):
        return lax.optimization_barrier((value, *earlier))[0]

    tokens = layer_inputs[0]
    size = tokens.shape[0]
    near = exchange(tokens, "feat", 1)
    far = [exchange(tokens, "feat", s) for s in range(2, shards, 2)]
    three = exchange(near, "feat", 2)

    a0, a0a, a0b, encoder_kept = encode(
        [tokens, near],
        [(0, 0, size), (1, 0, size)],
        [(0, 2 * size), (0, size), (size, size)],
        encoder,
        encoder_bias,
        [],
        stream=True,
    )
    d0a, d0b, n0 = up(a0a), up(a0b), beside(a0)
    rest = exchange(after(jnp.concatenate(far[1:], axis=0), far[0], three), "feat", 1)
    (a1,) = encode(
        [far[0], three],
        [(0, 0, size), (1, 0, size)],
        [(0, 2 * size)],
        encoder_kept,
        encoder_bias,
        [a0],
    )
    d1, n1 = up(a1), beside(a1)
    others = shards - 4
    order = []
    for k in range(others // 2):
        order += [(k, 0, size), (others // 2, k * size, size)]
    a2, a2a, a2b = encode(
        far[1:] + [rest],
        order,
        [(0, others * size), (0, (others - 1) * size), ((others - 1) * size, size)],
        encoder_kept,
        encoder_bias,
        [a1, d0a],
    )
    d2, d3, n2 = up(a2a), up(a2b), beside(after(a2, d0b))

    c0a, c0b = across(after(d0a, a2)), across(d0b)
    wave, base, *kept = decode_first(
        info, [a0, a1, a2], [n0, n1, n2], [d0a, d0b], [c0a, c0b], decoder, shards, []
    )
    received = [scatter(wave)]
    c1 = across(after(d1, wave))
    wave = decode_later(
        info, [d1], [c1], [(0, 0, 2 * size)], base, kept, 2 * size, shards, [wave]
    )
    received.append(scatter(wave))
    c2 = across(after(d2, wave))
    early = (others - 2) * size
    wave = decode_later(
        info, [d2], [c2], [(0, 0, early)], base, kept, 4 * size, shards, [wave]
    )
    received.append(scatter(wave))
    c3 = across(after(d3, wave))
    wave = decode_later(
        info,
        [d2, d3],
        [c2, c3],
        [(0, early, size), (1, 0, size)],
        base,
        kept,
        4 * size + early,
        shards,
        [wave],
    )
    received.append(scatter(wave))
    slots = [[0, 1], [2, 3], list(range(4, shards - 2)), [shards - 2, shards - 1]]
    total = add_up(targets[0], -1.0, slots[:3], received[:3], [wave])
    return add_up(total, 1.0, slots[3:], received[3:], [])[None]


def grouped(layer_inputs, targets, encoder, encoder_bias, decoder):
    groups = lax.axis_size("layer") // L_WIN
    depth_bits = groups.bit_length() - 1
    position = lax.axis_index("layer")
    target_layer = position // groups
    group_index = position % groups
    gathered = lax.all_gather(layer_inputs[0], "feat", axis=0, tiled=True)
    for bit_index in range(depth_bits):
        partner = exchange(gathered, "layer", 1 << bit_index)
        upper_bit = position >> bit_index & 1
        gathered = jnp.where(
            upper_bit == 1,
            jnp.concatenate([partner, gathered], 0),
            jnp.concatenate([gathered, partner], 0),
        )
    preact = (
        jnp.dot(gathered, encoder[0], preferred_element_type=jnp.float32) + encoder_bias[0][None, :]
    )
    features = jax.nn.relu(preact).astype(jnp.bfloat16)
    tok_count = features.shape[0]
    every_layer = lax.all_gather(features[None], "layer", axis=0, tiled=True)
    by_layer = every_layer.reshape(L_WIN, groups, tok_count, features.shape[1])
    mine_only = lax.dynamic_index_in_dim(by_layer, group_index, 1, keepdims=False)
    flipped = mine_only[::-1]
    padded = jnp.concatenate([flipped, jnp.zeros_like(flipped)], 0)
    stacked = lax.dynamic_slice_in_dim(padded, L_WIN - 1 - target_layer, L_WIN, 0)
    rebuilt = jnp.einsum("ktf,kfd->td", stacked, decoder[0], preferred_element_type=jnp.float32)
    for bit_index in reversed(range(depth_bits)):
        half_rows = rebuilt.shape[0] // 2
        upper_bit = position >> bit_index & 1
        kept_half = jnp.where(upper_bit == 1, rebuilt[half_rows:], rebuilt[:half_rows])
        sent_half = jnp.where(upper_bit == 1, rebuilt[:half_rows], rebuilt[half_rows:])
        rebuilt = kept_half + exchange(sent_half, "layer", 1 << bit_index)
    summed = lax.psum_scatter(rebuilt, "feat", scatter_dimension=1, tiled=True)
    residual = summed - targets[0]
    return residual[None]


def solution(mesh):
    placed = (
        P("layer", "feat", None),
        P("layer", None, "feat"),
        P("layer", None, "feat"),
        P("layer", "feat"),
        P("layer", None, "feat", None),
    )
    shards = mesh.shape["feat"]
    simple = mesh.shape["layer"] == L_WIN and shards >= 8 and shards & (shards - 1) == 0
    return jax.shard_map(
        pipelined if simple else grouped,
        mesh=mesh,
        in_specs=placed,
        out_specs=P("layer", None, "feat"),
        check_vma=False,
    )
```

```python
import functools

import jax
import jax.numpy as jnp
from jax import lax
from jax.experimental import pallas as pl
from jax.experimental.pallas import tpu as pltpu
from jax.sharding import PartitionSpec as P

L_WIN = 4
MIB = 1024 * 1024


def exchange(array, axis, flip):
    size = lax.axis_size(axis)
    return lax.ppermute(array, axis, [(i, i ^ flip) for i in range(size)])


ANYWHERE = pl.BlockSpec(memory_space=pl.ANY)
WHOLE = pl.BlockSpec(memory_space=pltpu.VMEM)
SLOTS = 3
ENCODE_MIB = 16
DECODE_MIB = 27
SUM_MIB = 12


def fill(order, parts, rows_of):
    at = 0
    for part, row, size in order:
        rows_of[pl.ds(at, size), :] = parts[part][pl.ds(row, size), :]
        at += size


def encode_kernel(order, pieces, n_in, n_after, stream, *refs):
    parts, weight, bias, refs = refs[:n_in], refs[n_in], refs[n_in + 1], refs[n_in + 2 + n_after :]
    outs, refs = refs[: len(pieces)], refs[len(pieces) :]
    features = weight.shape[2]
    if stream:
        kept, tokens, sems = refs
        block = features // sems.shape[0]
    else:
        kept, (tokens,) = weight, refs
        block = min(512, features)

    def fetch(j):
        cols = pl.ds(pl.multiple_of(j * block, block), block)
        return pltpu.make_async_copy(weight.at[0, :, cols], kept.at[0, :, cols], sems.at[j])

    if stream:
        for j in range(features // block):
            fetch(jnp.int32(j)).start()
    fill(order, parts, tokens)

    @pl.loop(0, features // block)
    def _(j):
        if stream:
            fetch(j).wait()
        cols = pl.ds(pl.multiple_of(j * block, block), block)
        preact = jnp.dot(tokens[...], kept[0, :, cols], preferred_element_type=jnp.float32)
        acts = jnp.maximum(preact + bias[:, cols], 0.0).astype(jnp.bfloat16)
        for out, (row, size) in zip(outs, pieces):
            out[:, cols] = acts[row : row + size]


def encode(parts, order, pieces, weight, bias, after, stream=False):
    rows = sum(size for _, _, size in order)
    _, width, features = weight.shape
    out_shape = [jax.ShapeDtypeStruct((size, features), jnp.bfloat16) for _, size in pieces]
    scratch = [pltpu.VMEM((rows, width), jnp.bfloat16)]
    if stream:
        out_shape.append(pltpu.VMEM(weight.shape, weight.dtype))
        scratch.append(pltpu.SemaphoreType.DMA((max(1, features // 512),)))
        weight = pltpu.with_memory_space_constraint(weight, pltpu.HBM)
    else:
        weight = pltpu.with_memory_space_constraint(weight, pltpu.VMEM)
    return pl.pallas_call(
        functools.partial(encode_kernel, order, pieces, len(parts), len(after), stream),
        in_specs=[WHOLE] * len(parts) + [ANYWHERE if stream else WHOLE, WHOLE] + [ANYWHERE] * len(after),
        out_specs=[WHOLE] * len(out_shape),
        out_shape=out_shape,
        scratch_shapes=scratch,
        compiler_params=pltpu.CompilerParams(vmem_limit_bytes=ENCODE_MIB * MIB),
        name="encode",
    )(*parts, weight, bias, *after)


def split(info, value, out, sent, j):
    cols = out.shape[2]
    low, high = value[:, :cols], value[:, cols:]

    @pl.when(info[4] == 0)
    def _():
        out[j] = low
        sent[j] = high.astype(sent.dtype)

    @pl.when(info[4] == 1)
    def _():
        out[j] = high
        sent[j] = low.astype(sent.dtype)


def halves(shards, rows, width):
    shape = (shards // 2, rows, width // shards)
    return [jax.ShapeDtypeStruct(shape, jnp.float32), jax.ShapeDtypeStruct(shape, jnp.bfloat16)]


def first_wave_kernel(counts, info, *refs):
    groups = []
    for count in counts:
        groups.append(refs[:count])
        refs = refs[count:]
    mine, theirs, direct, swapped = groups
    weights, out, sent, total, *kept = refs[:6]
    rings, ring_sems, kept_sems = refs[-3:]
    step, steps = pl.program_id(0), pl.num_programs(0)
    slots, block = rings.shape[1], rings.shape[2]
    odd, upper = info[0] == 1, info[1] == 1

    def rows(k):
        return pl.ds(pl.multiple_of(k * block, block), block)

    def fetch(source, k):
        slot = lax.rem(k, slots)
        return pltpu.make_async_copy(
            weights.at[0, source, rows(k)], rings.at[source, slot], ring_sems.at[source, slot]
        )

    def keep(source, k):
        return pltpu.make_async_copy(
            weights.at[0, info[2 + source], rows(k)],
            kept[source].at[rows(k)],
            kept_sems.at[source, k],
        )

    def fetch_all(k):
        fetch(0, k).start()
        pl.when(odd)(lambda: fetch(1, k).start())

        @pl.when(upper)
        def _():
            keep(0, k).start()
            keep(1, k).start()

    @pl.when(step == 0)
    def _():
        for k in range(slots - 1):
            fetch_all(jnp.int32(k))
        total[...] = jnp.zeros_like(total)

    pl.when(step + slots - 1 < steps)(lambda: fetch_all(step + slots - 1))

    def product(parts, weight):
        values = [part[...] for part in parts]
        acts = values[0] if len(values) == 1 else jnp.concatenate(values, axis=0)
        return jnp.dot(acts, weight, preferred_element_type=jnp.float32)

    slot = lax.rem(step, slots)
    fetch(0, step).wait()

    @pl.when(jnp.logical_not(odd))
    def _():
        total[...] += product(mine, rings[0, slot])

    @pl.when(odd)
    def _():
        fetch(1, step).wait()
        total[...] += product(mine, rings[0, slot]) + product(theirs, rings[1, slot])

    done = out.shape[1]

    @pl.when(upper)
    def _():
        keep(0, step).wait()
        keep(1, step).wait()
        total[:done, :] += product(direct, kept[0][rows(step), :]) + product(
            swapped, kept[1][rows(step), :]
        )

    @pl.when(step == steps - 1)
    def _():
        cols = out.shape[2]
        for j in range(out.shape[0]):
            split(info, total[:done, 2 * j * cols : 2 * (j + 1) * cols], out, sent, j)


def decode_first(info, mine, theirs, direct, swapped, decoder, shards, after):
    _, _, features, width = decoder.shape
    block = min(512, features)
    steps = features // block
    rows = sum(part.shape[0] for part in mine)
    done = sum(part.shape[0] for part in direct)

    def acts(part, flag):
        return pl.BlockSpec(
            (part.shape[0], block), lambda k, info: (0, k if flag is None else k * info[flag])
        )

    groups = (mine, theirs, direct, swapped)
    in_specs = [acts(p, flag) for parts, flag in zip(groups, (None, 0, 1, 1)) for p in parts]
    return pl.pallas_call(
        functools.partial(first_wave_kernel, [len(parts) for parts in groups]),
        grid_spec=pltpu.PrefetchScalarGridSpec(
            num_scalar_prefetch=1,
            grid=(steps,),
            in_specs=in_specs + [ANYWHERE] * (1 + len(after)),
            out_specs=[
                *[pl.BlockSpec(h.shape, lambda k, info: (0, 0, 0)) for h in halves(shards, done, width)],
                pl.BlockSpec((rows, width), lambda k, info: (0, 0)),
                WHOLE,
                WHOLE,
            ],
            scratch_shapes=[
                pltpu.VMEM((2, SLOTS, block, width), decoder.dtype),
                pltpu.SemaphoreType.DMA((2, SLOTS)),
                pltpu.SemaphoreType.DMA((2, steps)),
            ],
        ),
        out_shape=[
            *halves(shards, done, width),
            pltpu.HBM((rows, width), jnp.float32),
            pltpu.VMEM((features, width), decoder.dtype),
            pltpu.VMEM((features, width), decoder.dtype),
        ],
        compiler_params=pltpu.CompilerParams(vmem_limit_bytes=DECODE_MIB * MIB),
        name="decode_first",
    )(info, *sum(groups, []), decoder, *after)


def later_wave_kernel(order, row, n, info, *refs):
    direct, swapped, (base, *kept) = refs[:n], refs[n : 2 * n], refs[2 * n : 2 * n + 3]
    out, sent, first, second, start, sem = refs[-6:]
    rows = out.shape[1]
    pairs, cols = out.shape[0], out.shape[2]
    copy = pltpu.make_async_copy(base.at[pl.ds(row, rows)], start, sem)
    copy.start()
    fill(order, direct, first)
    fill(order, swapped, second)
    copy.wait()

    @pl.loop(0, pairs)
    def _(j):
        at = pl.ds(pl.multiple_of(j * 2 * cols, 2 * cols), 2 * cols)

        @pl.when(info[1] == 1)
        def _():
            start[:, at] += jnp.dot(
                first[...], kept[0][:, at], preferred_element_type=jnp.float32
            ) + jnp.dot(second[...], kept[1][:, at], preferred_element_type=jnp.float32)

        split(info, start[:, at], out, sent, j)


def decode_later(info, direct, swapped, order, base, kept, row, shards, after):
    rows = sum(size for _, _, size in order)
    features, width = kept[0].shape
    kept = [pltpu.with_memory_space_constraint(weight, pltpu.VMEM) for weight in kept]
    return pl.pallas_call(
        functools.partial(later_wave_kernel, order, row, len(direct)),
        in_specs=[pl.BlockSpec(memory_space=pltpu.SMEM)]
        + [WHOLE] * (2 * len(direct))
        + [ANYWHERE, WHOLE, WHOLE]
        + [ANYWHERE] * len(after),
        out_specs=[WHOLE, WHOLE],
        out_shape=halves(shards, rows, width),
        scratch_shapes=[
            pltpu.VMEM((rows, features), jnp.bfloat16),
            pltpu.VMEM((rows, features), jnp.bfloat16),
            pltpu.VMEM((rows, width), jnp.float32),
            pltpu.SemaphoreType.DMA,
        ],
        compiler_params=pltpu.CompilerParams(vmem_limit_bytes=DECODE_MIB * MIB),
        name="decode_later",
    )(info, *direct, *swapped, base, *kept, *after)


def pair_kernel(size, n_after, info, mine, theirs, *refs):
    outs = refs[n_after:]
    z = info[5]
    rows = mine.shape[1]
    for q, out in enumerate(outs):
        for at in range(0, rows, size):
            partner = at // size ^ 1
            total = mine[z ^ q, pl.ds(at, size), :] + theirs[
                z ^ q, pl.ds(partner * size, size), :
            ].astype(jnp.float32)
            out[pl.ds(at, size), :] = total.astype(out.dtype)


def add_pair(info, mine, theirs, size, after):
    count, rows, cols = mine.shape
    return pl.pallas_call(
        functools.partial(pair_kernel, size, len(after)),
        in_specs=[pl.BlockSpec(memory_space=pltpu.SMEM), WHOLE, WHOLE] + [ANYWHERE] * len(after),
        out_specs=[WHOLE] * count,
        out_shape=[
            jax.ShapeDtypeStruct((rows, cols), jnp.float32 if q == 0 else jnp.bfloat16)
            for q in range(count)
        ],
        compiler_params=pltpu.CompilerParams(vmem_limit_bytes=SUM_MIB * MIB),
        name="add_pair",
    )(info, mine, theirs, *after)


def sum_kernel(sign, pieces, info, base, *refs):
    received, out = refs[: len(pieces)], refs[-1]
    me = info[6]
    out[...] = sign * base[...]
    for ref, (source, blocks) in zip(received, pieces):
        size = ref.shape[0] // len(blocks)
        for k, s in enumerate(blocks):
            at = pl.ds(pl.multiple_of((me ^ (source ^ s)) * size, size), size)
            out[at, :] += ref[pl.ds(k * size, size), :].astype(jnp.float32)


def add_up(info, base, sign, pieces, received, after):
    return pl.pallas_call(
        functools.partial(sum_kernel, sign, pieces),
        in_specs=[pl.BlockSpec(memory_space=pltpu.SMEM)]
        + [WHOLE] * (1 + len(received))
        + [ANYWHERE] * len(after),
        out_specs=WHOLE,
        out_shape=jax.ShapeDtypeStruct(base.shape, base.dtype),
        compiler_params=pltpu.CompilerParams(vmem_limit_bytes=SUM_MIB * MIB),
        name="add_up",
    )(info, base, *received, *after)


def pipelined(layer_inputs, targets, encoder, encoder_bias, decoder):
    shards = lax.axis_size("feat")
    layers = lax.axis_size("layer")
    half = layers // 2
    layer = lax.axis_index("layer")
    feat = lax.axis_index("feat")
    upper = layer >= half
    info = jnp.stack(
        [
            layer & 1,
            upper.astype(jnp.int32),
            jnp.full_like(layer, half),
            jnp.where(upper, layer - ((layer ^ 1) - half), 0),
            feat & 1,
            feat >> 1,
            feat,
        ]
    ).astype(jnp.int32)

    def up(a):
        return lax.ppermute(a, "layer", [(i, i + half) for i in range(half)])

    def across(a):
        return lax.ppermute(a, "layer", [(i, i ^ 1) for i in range(half, layers)])

    def beside(a):
        return lax.ppermute(a, "layer", [(i, i + 1) for i in range(0, layers, 2)])

    def after(value, *earlier):
        return lax.optimization_barrier((value, *earlier))[0]

    tokens = layer_inputs[0]
    size = tokens.shape[0]
    near = exchange(tokens, "feat", 1)
    far = [exchange(tokens, "feat", s) for s in range(2, shards, 2)]
    three = exchange(near, "feat", 2)

    a0, a0a, a0b, encoder_kept = encode(
        [tokens, near],
        [(0, 0, size), (1, 0, size)],
        [(0, 2 * size), (0, size), (size, size)],
        encoder,
        encoder_bias,
        [],
        stream=True,
    )
    d0a, d0b, n0 = up(a0a), up(a0b), beside(a0)
    rest = exchange(after(jnp.concatenate(far[1:], axis=0), far[0], three), "feat", 1)
    (a1,) = encode(
        [far[0], three],
        [(0, 0, size), (1, 0, size)],
        [(0, 2 * size)],
        encoder_kept,
        encoder_bias,
        [a0],
    )
    d1, n1 = up(a1), beside(a1)
    others = shards - 4
    order = []
    for k in range(others // 2):
        order += [(k, 0, size), (others // 2, k * size, size)]
    a2, a2a, a2b = encode(
        far[1:] + [rest],
        order,
        [(0, others * size), (0, (others - 1) * size), ((others - 1) * size, size)],
        encoder_kept,
        encoder_bias,
        [a1, d0a],
    )
    d2, d3, n2 = up(a2a), up(a2b), beside(after(a2, d0b))

    c0a, c0b = across(after(d0a, n2)), across(after(d0b, n2))
    mine, sent, base, *kept = decode_first(
        info, [a0, a1, a2], [n0, n1, n2], [d0a, d0b], [c0a, c0b], decoder, shards, []
    )
    slots = [[0, 1], [2, 3], list(range(4, shards - 2)), [shards - 2, shards - 1]]

    def meet(mine, sent, *earlier):
        return add_pair(info, mine, exchange(sent, "feat", 1), size, list(earlier))

    def spread(number, sums):
        parts = [part if q == 0 else exchange(part, "feat", 2 * q) for q, part in enumerate(sums)]
        return [(2 * q, slots[number]) for q in range(len(parts))], parts

    def later(number, direct, swapped, order, *earlier):
        row = slots[number][0] * size
        return decode_later(info, direct, swapped, order, base, kept, row, shards, list(earlier))

    c1 = across(after(d1, sent))
    mine1, sent1 = later(1, [d1], [c1], [(0, 0, 2 * size)], sent)
    met0 = meet(mine, sent, sent1)
    where0, parts0 = spread(0, met0)
    met1 = meet(mine1, sent1, met0[0])
    where1, parts1 = spread(1, met1)
    c2 = across(after(d2, met1[0]))
    early = (others - 2) * size
    mine2, sent2 = later(2, [d2], [c2], [(0, 0, early)], met1[0], *parts0)
    c3 = across(after(d3, sent2))
    order = [(0, early, size), (1, 0, size)]
    mine3, sent3 = later(3, [d2, d3], [c2, c3], order, sent2, *parts1)
    met2 = meet(mine2, sent2, sent3)
    where2, parts2 = spread(2, met2)
    total = add_up(info, targets[0], -1.0, where0 + where1, parts0 + parts1, [met2[0]])
    met3 = meet(mine3, sent3, total)
    where3, parts3 = spread(3, met3)
    return add_up(info, total, 1.0, where2 + where3, parts2 + parts3, [])[None]


def grouped(layer_inputs, targets, encoder, encoder_bias, decoder):
    groups = lax.axis_size("layer") // L_WIN
    depth_bits = groups.bit_length() - 1
    position = lax.axis_index("layer")
    target_layer = position // groups
    group_index = position % groups
    gathered = lax.all_gather(layer_inputs[0], "feat", axis=0, tiled=True)
    for bit_index in range(depth_bits):
        partner = exchange(gathered, "layer", 1 << bit_index)
        upper_bit = position >> bit_index & 1
        gathered = jnp.where(
            upper_bit == 1,
            jnp.concatenate([partner, gathered], 0),
            jnp.concatenate([gathered, partner], 0),
        )
    preact = (
        jnp.dot(gathered, encoder[0], preferred_element_type=jnp.float32) + encoder_bias[0][None, :]
    )
    features = jax.nn.relu(preact).astype(jnp.bfloat16)
    tok_count = features.shape[0]
    every_layer = lax.all_gather(features[None], "layer", axis=0, tiled=True)
    by_layer = every_layer.reshape(L_WIN, groups, tok_count, features.shape[1])
    mine_only = lax.dynamic_index_in_dim(by_layer, group_index, 1, keepdims=False)
    flipped = mine_only[::-1]
    padded = jnp.concatenate([flipped, jnp.zeros_like(flipped)], 0)
    stacked = lax.dynamic_slice_in_dim(padded, L_WIN - 1 - target_layer, L_WIN, 0)
    rebuilt = jnp.einsum("ktf,kfd->td", stacked, decoder[0], preferred_element_type=jnp.float32)
    for bit_index in reversed(range(depth_bits)):
        half_rows = rebuilt.shape[0] // 2
        upper_bit = position >> bit_index & 1
        kept_half = jnp.where(upper_bit == 1, rebuilt[half_rows:], rebuilt[:half_rows])
        sent_half = jnp.where(upper_bit == 1, rebuilt[:half_rows], rebuilt[half_rows:])
        rebuilt = kept_half + exchange(sent_half, "layer", 1 << bit_index)
    summed = lax.psum_scatter(rebuilt, "feat", scatter_dimension=1, tiled=True)
    residual = summed - targets[0]
    return residual[None]


def solution(mesh):
    placed = (
        P("layer", "feat", None),
        P("layer", None, "feat"),
        P("layer", None, "feat"),
        P("layer", "feat"),
        P("layer", None, "feat", None),
    )
    shards = mesh.shape["feat"]
    simple = mesh.shape["layer"] == L_WIN and shards >= 8 and shards & (shards - 1) == 0
    return jax.shard_map(
        pipelined if simple else grouped,
        mesh=mesh,
        in_specs=placed,
        out_specs=P("layer", None, "feat"),
        check_vma=False,
    )
```

```python
import functools

import jax
import jax.numpy as jnp
from jax import lax
from jax.experimental import pallas as pl
from jax.experimental.pallas import tpu as pltpu
from jax.sharding import PartitionSpec as P

L_WIN = 4
MIB = 1024 * 1024


def exchange(array, axis, flip):
    size = lax.axis_size(axis)
    return lax.ppermute(array, axis, [(i, i ^ flip) for i in range(size)])


ANYWHERE = pl.BlockSpec(memory_space=pl.ANY)
WHOLE = pl.BlockSpec(memory_space=pltpu.VMEM)
SLOTS = 3
ENCODE_MIB = 16
DECODE_MIB = 27
SUM_MIB = 12


def fill(order, parts, rows_of):
    at = 0
    for part, row, size in order:
        rows_of[pl.ds(at, size), :] = parts[part][pl.ds(row, size), :]
        at += size


def encode_kernel(order, pieces, n_in, n_after, stream, *refs):
    parts, weight, bias, refs = refs[:n_in], refs[n_in], refs[n_in + 1], refs[n_in + 2 + n_after :]
    outs, refs = refs[: len(pieces)], refs[len(pieces) :]
    features = weight.shape[2]
    if stream:
        kept, tokens, sems = refs
        block = features // sems.shape[0]
    else:
        kept, (tokens,) = weight, refs
        block = min(512, features)

    def fetch(j):
        cols = pl.ds(pl.multiple_of(j * block, block), block)
        return pltpu.make_async_copy(weight.at[0, :, cols], kept.at[0, :, cols], sems.at[j])

    if stream:
        for j in range(features // block):
            fetch(jnp.int32(j)).start()
    fill(order, parts, tokens)

    @pl.loop(0, features // block)
    def _(j):
        if stream:
            fetch(j).wait()
        cols = pl.ds(pl.multiple_of(j * block, block), block)
        preact = jnp.dot(tokens[...], kept[0, :, cols], preferred_element_type=jnp.float32)
        acts = jnp.maximum(preact + bias[:, cols], 0.0).astype(jnp.bfloat16)
        for out, (row, size) in zip(outs, pieces):
            out[:, cols] = acts[row : row + size]


def encode(parts, order, pieces, weight, bias, after, stream=False):
    rows = sum(size for _, _, size in order)
    _, width, features = weight.shape
    out_shape = [jax.ShapeDtypeStruct((size, features), jnp.bfloat16) for _, size in pieces]
    scratch = [pltpu.VMEM((rows, width), jnp.bfloat16)]
    if stream:
        out_shape.append(pltpu.VMEM(weight.shape, weight.dtype))
        scratch.append(pltpu.SemaphoreType.DMA((max(1, features // 512),)))
        weight = pltpu.with_memory_space_constraint(weight, pltpu.HBM)
    else:
        weight = pltpu.with_memory_space_constraint(weight, pltpu.VMEM)
    return pl.pallas_call(
        functools.partial(encode_kernel, order, pieces, len(parts), len(after), stream),
        in_specs=[WHOLE] * len(parts) + [ANYWHERE if stream else WHOLE, WHOLE] + [ANYWHERE] * len(after),
        out_specs=[WHOLE] * len(out_shape),
        out_shape=out_shape,
        scratch_shapes=scratch,
        compiler_params=pltpu.CompilerParams(vmem_limit_bytes=ENCODE_MIB * MIB),
        name="encode",
    )(*parts, weight, bias, *after)


def split(info, value, out, sent, j):
    cols = out.shape[2]
    low, high = value[:, :cols], value[:, cols:]

    @pl.when(info[4] == 0)
    def _():
        out[j] = low
        sent[j] = high.astype(sent.dtype)

    @pl.when(info[4] == 1)
    def _():
        out[j] = high
        sent[j] = low.astype(sent.dtype)


def halves(shards, rows, width):
    shape = (shards // 2, rows, width // shards)
    return [jax.ShapeDtypeStruct(shape, jnp.float32), jax.ShapeDtypeStruct(shape, jnp.bfloat16)]


def first_wave_kernel(counts, info, *refs):
    groups = []
    for count in counts:
        groups.append(refs[:count])
        refs = refs[count:]
    mine, theirs = groups
    weights, total, *kept = refs[:4]
    rings, ring_sems, kept_sems = refs[-3:]
    step, steps = pl.program_id(0), pl.num_programs(0)
    slots, block = rings.shape[1], rings.shape[2]
    odd, upper = info[0] == 1, info[1] == 1

    def rows(k):
        return pl.ds(pl.multiple_of(k * block, block), block)

    def fetch(source, k):
        slot = lax.rem(k, slots)
        return pltpu.make_async_copy(
            weights.at[0, source, rows(k)], rings.at[source, slot], ring_sems.at[source, slot]
        )

    def keep(source, k):
        return pltpu.make_async_copy(
            weights.at[0, info[2 + source], rows(k)],
            kept[source].at[rows(k)],
            kept_sems.at[source, k],
        )

    def fetch_all(k):
        fetch(0, k).start()
        pl.when(odd)(lambda: fetch(1, k).start())

        @pl.when(upper)
        def _():
            keep(0, k).start()
            keep(1, k).start()

    @pl.when(step == 0)
    def _():
        for k in range(slots - 1):
            fetch_all(jnp.int32(k))
        total[...] = jnp.zeros_like(total)

    pl.when(step + slots - 1 < steps)(lambda: fetch_all(step + slots - 1))

    def product(parts, weight):
        values = [part[...] for part in parts]
        acts = values[0] if len(values) == 1 else jnp.concatenate(values, axis=0)
        return jnp.dot(acts, weight, preferred_element_type=jnp.float32)

    slot = lax.rem(step, slots)
    fetch(0, step).wait()

    @pl.when(jnp.logical_not(odd))
    def _():
        total[...] += product(mine, rings[0, slot])

    @pl.when(odd)
    def _():
        fetch(1, step).wait()
        total[...] += product(mine, rings[0, slot]) + product(theirs, rings[1, slot])

    @pl.when((step == steps - 1) & upper)
    def _():
        for k in range(kept_sems.shape[1]):
            keep(0, jnp.int32(k)).wait()
            keep(1, jnp.int32(k)).wait()


def decode_first(info, mine, theirs, decoder, after):
    _, _, features, width = decoder.shape
    block = min(512, features)
    steps = features // block
    rows = sum(part.shape[0] for part in mine)

    def acts(part, flag):
        return pl.BlockSpec(
            (part.shape[0], block), lambda k, info: (0, k if flag is None else k * info[flag])
        )

    groups = (mine, theirs)
    in_specs = [acts(p, flag) for parts, flag in zip(groups, (None, 0)) for p in parts]
    return pl.pallas_call(
        functools.partial(first_wave_kernel, [len(parts) for parts in groups]),
        grid_spec=pltpu.PrefetchScalarGridSpec(
            num_scalar_prefetch=1,
            grid=(steps,),
            in_specs=in_specs + [ANYWHERE] * (1 + len(after)),
            out_specs=[
                pl.BlockSpec((rows, width), lambda k, info: (0, 0)),
                WHOLE,
                WHOLE,
            ],
            scratch_shapes=[
                pltpu.VMEM((2, SLOTS, block, width), decoder.dtype),
                pltpu.SemaphoreType.DMA((2, SLOTS)),
                pltpu.SemaphoreType.DMA((2, steps)),
            ],
        ),
        out_shape=[
            pltpu.HBM((rows, width), jnp.float32),
            pltpu.VMEM((features, width), decoder.dtype),
            pltpu.VMEM((features, width), decoder.dtype),
        ],
        compiler_params=pltpu.CompilerParams(vmem_limit_bytes=DECODE_MIB * MIB),
        name="decode_first",
    )(info, *sum(groups, []), decoder, *after)


def later_wave_kernel(order, row, n, info, *refs):
    direct, swapped, (base, *kept) = refs[:n], refs[n : 2 * n], refs[2 * n : 2 * n + 3]
    out, sent, first, second, start, sem = refs[-6:]
    rows = out.shape[1]
    pairs, cols = out.shape[0], out.shape[2]
    copy = pltpu.make_async_copy(base.at[pl.ds(row, rows)], start, sem)
    copy.start()
    fill(order, direct, first)
    fill(order, swapped, second)
    copy.wait()

    @pl.loop(0, pairs)
    def _(j):
        at = pl.ds(pl.multiple_of(j * 2 * cols, 2 * cols), 2 * cols)

        @pl.when(info[1] == 1)
        def _():
            start[:, at] += jnp.dot(
                first[...], kept[0][:, at], preferred_element_type=jnp.float32
            ) + jnp.dot(second[...], kept[1][:, at], preferred_element_type=jnp.float32)

        split(info, start[:, at], out, sent, j)


def decode_later(info, direct, swapped, order, base, kept, row, shards, after):
    rows = sum(size for _, _, size in order)
    features, width = kept[0].shape
    kept = [pltpu.with_memory_space_constraint(weight, pltpu.VMEM) for weight in kept]
    return pl.pallas_call(
        functools.partial(later_wave_kernel, order, row, len(direct)),
        in_specs=[pl.BlockSpec(memory_space=pltpu.SMEM)]
        + [WHOLE] * (2 * len(direct))
        + [ANYWHERE, WHOLE, WHOLE]
        + [ANYWHERE] * len(after),
        out_specs=[WHOLE, WHOLE],
        out_shape=halves(shards, rows, width),
        scratch_shapes=[
            pltpu.VMEM((rows, features), jnp.bfloat16),
            pltpu.VMEM((rows, features), jnp.bfloat16),
            pltpu.VMEM((rows, width), jnp.float32),
            pltpu.SemaphoreType.DMA,
        ],
        compiler_params=pltpu.CompilerParams(vmem_limit_bytes=DECODE_MIB * MIB),
        name="decode_later",
    )(info, *direct, *swapped, base, *kept, *after)


def pair_kernel(size, n_after, info, mine, theirs, *refs):
    outs = refs[n_after:]
    z = info[5]
    rows = mine.shape[1]
    for q, out in enumerate(outs):
        for at in range(0, rows, size):
            partner = at // size ^ 1
            total = mine[z ^ q, pl.ds(at, size), :] + theirs[
                z ^ q, pl.ds(partner * size, size), :
            ].astype(jnp.float32)
            out[pl.ds(at, size), :] = total.astype(out.dtype)


def add_pair(info, mine, theirs, size, after):
    count, rows, cols = mine.shape
    return pl.pallas_call(
        functools.partial(pair_kernel, size, len(after)),
        in_specs=[pl.BlockSpec(memory_space=pltpu.SMEM), WHOLE, WHOLE] + [ANYWHERE] * len(after),
        out_specs=[WHOLE] * count,
        out_shape=[
            jax.ShapeDtypeStruct((rows, cols), jnp.float32 if q == 0 else jnp.bfloat16)
            for q in range(count)
        ],
        compiler_params=pltpu.CompilerParams(vmem_limit_bytes=SUM_MIB * MIB),
        name="add_pair",
    )(info, mine, theirs, *after)


def sum_kernel(sign, pieces, info, base, *refs):
    received, out = refs[: len(pieces)], refs[-1]
    me = info[6]
    out[...] = sign * base[...]
    for ref, (source, blocks) in zip(received, pieces):
        size = ref.shape[0] // len(blocks)
        for k, s in enumerate(blocks):
            at = pl.ds(pl.multiple_of((me ^ (source ^ s)) * size, size), size)
            out[at, :] += ref[pl.ds(k * size, size), :].astype(jnp.float32)


def add_up(info, base, sign, pieces, received, after):
    return pl.pallas_call(
        functools.partial(sum_kernel, sign, pieces),
        in_specs=[pl.BlockSpec(memory_space=pltpu.SMEM)]
        + [WHOLE] * (1 + len(received))
        + [ANYWHERE] * len(after),
        out_specs=WHOLE,
        out_shape=jax.ShapeDtypeStruct(base.shape, base.dtype),
        compiler_params=pltpu.CompilerParams(vmem_limit_bytes=SUM_MIB * MIB),
        name="add_up",
    )(info, base, *received, *after)


def pipelined(layer_inputs, targets, encoder, encoder_bias, decoder):
    shards = lax.axis_size("feat")
    layers = lax.axis_size("layer")
    half = layers // 2
    layer = lax.axis_index("layer")
    feat = lax.axis_index("feat")
    upper = layer >= half
    info = jnp.stack(
        [
            layer & 1,
            upper.astype(jnp.int32),
            jnp.full_like(layer, half),
            jnp.where(upper, layer - ((layer ^ 1) - half), 0),
            feat & 1,
            feat >> 1,
            feat,
        ]
    ).astype(jnp.int32)

    def up(a):
        return lax.ppermute(a, "layer", [(i, i + half) for i in range(half)])

    def across(a):
        return lax.ppermute(a, "layer", [(i, i ^ 1) for i in range(half, layers)])

    def beside(a):
        return lax.ppermute(a, "layer", [(i, i + 1) for i in range(0, layers, 2)])

    def after(value, *earlier):
        return lax.optimization_barrier((value, *earlier))[0]

    tokens = layer_inputs[0]
    size = tokens.shape[0]
    near = exchange(tokens, "feat", 1)
    far = [exchange(tokens, "feat", s) for s in range(2, shards, 2)]
    three = exchange(near, "feat", 2)

    a0, a0a, a0b, encoder_kept = encode(
        [tokens, near],
        [(0, 0, size), (1, 0, size)],
        [(0, 2 * size), (0, size), (size, size)],
        encoder,
        encoder_bias,
        [],
        stream=True,
    )
    d0a, d0b, n0 = up(a0a), up(a0b), beside(a0)
    rest = exchange(after(jnp.concatenate(far[1:], axis=0), far[0], a0a), "feat", 1)
    (a1,) = encode(
        [far[0], three],
        [(0, 0, size), (1, 0, size)],
        [(0, 2 * size)],
        encoder_kept,
        encoder_bias,
        [a0],
    )
    d1, n1 = up(a1), beside(a1)
    others = shards - 4
    order = []
    for k in range(others // 2):
        order += [(k, 0, size), (others // 2, k * size, size)]
    a2, a2a, a2b = encode(
        far[1:] + [rest],
        order,
        [(0, others * size), (0, (others - 1) * size), ((others - 1) * size, size)],
        encoder_kept,
        encoder_bias,
        [a1, d0a],
    )
    d2, d3, n2 = up(a2a), up(a2b), beside(after(a2, d0b))

    base, *kept = decode_first(info, [a0, a1, a2], [n0, n1, n2], decoder, [])
    slots = [list(range(4)), list(range(4, shards - 2)), [shards - 2, shards - 1]]

    def meet(mine, sent, *earlier):
        return add_pair(info, mine, exchange(sent, "feat", 1), size, list(earlier))

    def spread(number, sums):
        parts = [part if q == 0 else exchange(part, "feat", 2 * q) for q, part in enumerate(sums)]
        return [(2 * q, slots[number]) for q in range(len(parts))], parts

    def later(number, direct, swapped, order, *earlier):
        row = slots[number][0] * size
        return decode_later(info, direct, swapped, order, base, kept, row, shards, list(earlier))

    c0a, c0b, c1 = across(d0a), across(d0b), across(after(d1, base))
    order = [(0, 0, size), (1, 0, size), (2, 0, 2 * size)]
    mine0, sent0 = later(0, [d0a, d0b, d1], [c0a, c0b, c1], order)
    met0 = meet(mine0, sent0)
    where0, parts0 = spread(0, met0)
    c2 = across(after(d2, met0[0]))
    c3 = across(after(d3, met0[0]))
    early = (others - 2) * size
    mine1, sent1 = later(1, [d2], [c2], [(0, 0, early)], met0[0])
    order = [(0, early, size), (1, 0, size)]
    mine2, sent2 = later(2, [d2, d3], [c2, c3], order, sent1, *parts0)
    met1 = meet(mine1, sent1, sent2)
    where1, parts1 = spread(1, met1)
    met2 = meet(mine2, sent2, *parts1)
    where2, parts2 = spread(2, met2)
    return add_up(info, targets[0], -1.0, where0 + where1 + where2, parts0 + parts1 + parts2, [])[None]


def grouped(layer_inputs, targets, encoder, encoder_bias, decoder):
    groups = lax.axis_size("layer") // L_WIN
    depth_bits = groups.bit_length() - 1
    position = lax.axis_index("layer")
    target_layer = position // groups
    group_index = position % groups
    gathered = lax.all_gather(layer_inputs[0], "feat", axis=0, tiled=True)
    for bit_index in range(depth_bits):
        partner = exchange(gathered, "layer", 1 << bit_index)
        upper_bit = position >> bit_index & 1
        gathered = jnp.where(
            upper_bit == 1,
            jnp.concatenate([partner, gathered], 0),
            jnp.concatenate([gathered, partner], 0),
        )
    preact = (
        jnp.dot(gathered, encoder[0], preferred_element_type=jnp.float32) + encoder_bias[0][None, :]
    )
    features = jax.nn.relu(preact).astype(jnp.bfloat16)
    tok_count = features.shape[0]
    every_layer = lax.all_gather(features[None], "layer", axis=0, tiled=True)
    by_layer = every_layer.reshape(L_WIN, groups, tok_count, features.shape[1])
    mine_only = lax.dynamic_index_in_dim(by_layer, group_index, 1, keepdims=False)
    flipped = mine_only[::-1]
    padded = jnp.concatenate([flipped, jnp.zeros_like(flipped)], 0)
    stacked = lax.dynamic_slice_in_dim(padded, L_WIN - 1 - target_layer, L_WIN, 0)
    rebuilt = jnp.einsum("ktf,kfd->td", stacked, decoder[0], preferred_element_type=jnp.float32)
    for bit_index in reversed(range(depth_bits)):
        half_rows = rebuilt.shape[0] // 2
        upper_bit = position >> bit_index & 1
        kept_half = jnp.where(upper_bit == 1, rebuilt[half_rows:], rebuilt[:half_rows])
        sent_half = jnp.where(upper_bit == 1, rebuilt[:half_rows], rebuilt[half_rows:])
        rebuilt = kept_half + exchange(sent_half, "layer", 1 << bit_index)
    summed = lax.psum_scatter(rebuilt, "feat", scatter_dimension=1, tiled=True)
    residual = summed - targets[0]
    return residual[None]


def solution(mesh):
    placed = (
        P("layer", "feat", None),
        P("layer", None, "feat"),
        P("layer", None, "feat"),
        P("layer", "feat"),
        P("layer", None, "feat", None),
    )
    shards = mesh.shape["feat"]
    simple = mesh.shape["layer"] == L_WIN and shards >= 8 and shards & (shards - 1) == 0
    return jax.shard_map(
        pipelined if simple else grouped,
        mesh=mesh,
        in_specs=placed,
        out_specs=P("layer", None, "feat"),
        check_vma=False,
    )
```

```python
import functools

import jax
import jax.numpy as jnp
from jax import lax
from jax.experimental import pallas as pl
from jax.experimental.pallas import tpu as pltpu
from jax.sharding import PartitionSpec as P

L_WIN = 4
MIB = 1024 * 1024


def exchange(array, axis, flip):
    size = lax.axis_size(axis)
    return lax.ppermute(array, axis, [(i, i ^ flip) for i in range(size)])


ANYWHERE = pl.BlockSpec(memory_space=pl.ANY)
WHOLE = pl.BlockSpec(memory_space=pltpu.VMEM)
SLOTS = 3
ENCODE_MIB = 16
DECODE_MIB = 27
SUM_MIB = 12


def fill(order, parts, rows_of):
    at = 0
    for part, row, size in order:
        rows_of[pl.ds(at, size), :] = parts[part][pl.ds(row, size), :]
        at += size


def encode_kernel(order, pieces, n_in, n_after, stream, *refs):
    parts, weight, bias, refs = refs[:n_in], refs[n_in], refs[n_in + 1], refs[n_in + 2 + n_after :]
    outs, refs = refs[: len(pieces)], refs[len(pieces) :]
    features = weight.shape[2]
    if stream:
        kept, tokens, sems = refs
        block = features // sems.shape[0]
    else:
        kept, (tokens,) = weight, refs
        block = min(512, features)

    def fetch(j):
        cols = pl.ds(pl.multiple_of(j * block, block), block)
        return pltpu.make_async_copy(weight.at[0, :, cols], kept.at[0, :, cols], sems.at[j])

    if stream:
        for j in range(features // block):
            fetch(jnp.int32(j)).start()
    fill(order, parts, tokens)

    @pl.loop(0, features // block)
    def _(j):
        if stream:
            fetch(j).wait()
        cols = pl.ds(pl.multiple_of(j * block, block), block)
        preact = jnp.dot(tokens[...], kept[0, :, cols], preferred_element_type=jnp.float32)
        acts = jnp.maximum(preact + bias[:, cols], 0.0).astype(jnp.bfloat16)
        for out, (row, size) in zip(outs, pieces):
            out[:, cols] = acts[row : row + size]


def encode(parts, order, pieces, weight, bias, after, stream=False):
    rows = sum(size for _, _, size in order)
    _, width, features = weight.shape
    out_shape = [jax.ShapeDtypeStruct((size, features), jnp.bfloat16) for _, size in pieces]
    scratch = [pltpu.VMEM((rows, width), jnp.bfloat16)]
    if stream:
        out_shape.append(pltpu.VMEM(weight.shape, weight.dtype))
        scratch.append(pltpu.SemaphoreType.DMA((max(1, features // 512),)))
        weight = pltpu.with_memory_space_constraint(weight, pltpu.HBM)
    else:
        weight = pltpu.with_memory_space_constraint(weight, pltpu.VMEM)
    return pl.pallas_call(
        functools.partial(encode_kernel, order, pieces, len(parts), len(after), stream),
        in_specs=[WHOLE] * len(parts) + [ANYWHERE if stream else WHOLE, WHOLE] + [ANYWHERE] * len(after),
        out_specs=[WHOLE] * len(out_shape),
        out_shape=out_shape,
        scratch_shapes=scratch,
        compiler_params=pltpu.CompilerParams(vmem_limit_bytes=ENCODE_MIB * MIB),
        name="encode",
    )(*parts, weight, bias, *after)


def split(info, value, out, sent, j):
    cols = out.shape[2]
    low, high = value[:, :cols], value[:, cols:]

    @pl.when(info[4] == 0)
    def _():
        out[j] = low
        sent[j] = high.astype(sent.dtype)

    @pl.when(info[4] == 1)
    def _():
        out[j] = high
        sent[j] = low.astype(sent.dtype)


def halves(shards, rows, width):
    shape = (shards // 2, rows, width // shards)
    return [jax.ShapeDtypeStruct(shape, jnp.float32), jax.ShapeDtypeStruct(shape, jnp.bfloat16)]


def first_wave_kernel(counts, info, *refs):
    groups = []
    for count in counts:
        groups.append(refs[:count])
        refs = refs[count:]
    mine, theirs, direct, swapped = groups
    weights, out, sent, total, *kept = refs[:6]
    rings, ring_sems, kept_sems = refs[-3:]
    step, steps = pl.program_id(0), pl.num_programs(0)
    slots, block = rings.shape[1], rings.shape[2]
    odd, upper = info[0] == 1, info[1] == 1

    def rows(k):
        return pl.ds(pl.multiple_of(k * block, block), block)

    def fetch(source, k):
        slot = lax.rem(k, slots)
        return pltpu.make_async_copy(
            weights.at[0, source, rows(k)], rings.at[source, slot], ring_sems.at[source, slot]
        )

    def keep(source, k):
        return pltpu.make_async_copy(
            weights.at[0, info[2 + source], rows(k)],
            kept[source].at[rows(k)],
            kept_sems.at[source, k],
        )

    def fetch_all(k):
        fetch(0, k).start()
        pl.when(odd)(lambda: fetch(1, k).start())

        @pl.when(upper)
        def _():
            keep(0, k).start()
            keep(1, k).start()

    @pl.when(step == 0)
    def _():
        for k in range(slots - 1):
            fetch_all(jnp.int32(k))
        total[...] = jnp.zeros_like(total)

    pl.when(step + slots - 1 < steps)(lambda: fetch_all(step + slots - 1))

    def product(parts, weight):
        values = [part[...] for part in parts]
        acts = values[0] if len(values) == 1 else jnp.concatenate(values, axis=0)
        return jnp.dot(acts, weight, preferred_element_type=jnp.float32)

    slot = lax.rem(step, slots)
    fetch(0, step).wait()

    @pl.when(jnp.logical_not(odd))
    def _():
        total[...] += product(mine, rings[0, slot])

    @pl.when(odd)
    def _():
        fetch(1, step).wait()
        total[...] += product(mine, rings[0, slot]) + product(theirs, rings[1, slot])

    done = out.shape[1]

    @pl.when(upper)
    def _():
        keep(0, step).wait()
        keep(1, step).wait()
        total[:done, :] += product(direct, kept[0][rows(step), :]) + product(
            swapped, kept[1][rows(step), :]
        )

    @pl.when(step == steps - 1)
    def _():
        cols = out.shape[2]
        for j in range(out.shape[0]):
            split(info, total[:done, 2 * j * cols : 2 * (j + 1) * cols], out, sent, j)


def decode_first(info, mine, theirs, direct, swapped, decoder, shards, after):
    _, _, features, width = decoder.shape
    block = min(512, features)
    steps = features // block
    rows = sum(part.shape[0] for part in mine)
    done = sum(part.shape[0] for part in direct)

    def acts(part, flag):
        return pl.BlockSpec(
            (part.shape[0], block), lambda k, info: (0, k if flag is None else k * info[flag])
        )

    groups = (mine, theirs, direct, swapped)
    in_specs = [acts(p, flag) for parts, flag in zip(groups, (None, 0, 1, 1)) for p in parts]
    return pl.pallas_call(
        functools.partial(first_wave_kernel, [len(parts) for parts in groups]),
        grid_spec=pltpu.PrefetchScalarGridSpec(
            num_scalar_prefetch=1,
            grid=(steps,),
            in_specs=in_specs + [ANYWHERE] * (1 + len(after)),
            out_specs=[
                *[pl.BlockSpec(h.shape, lambda k, info: (0, 0, 0)) for h in halves(shards, done, width)],
                pl.BlockSpec((rows, width), lambda k, info: (0, 0)),
                WHOLE,
                WHOLE,
            ],
            scratch_shapes=[
                pltpu.VMEM((2, SLOTS, block, width), decoder.dtype),
                pltpu.SemaphoreType.DMA((2, SLOTS)),
                pltpu.SemaphoreType.DMA((2, steps)),
            ],
        ),
        out_shape=[
            *halves(shards, done, width),
            pltpu.HBM((rows, width), jnp.float32),
            pltpu.VMEM((features, width), decoder.dtype),
            pltpu.VMEM((features, width), decoder.dtype),
        ],
        compiler_params=pltpu.CompilerParams(vmem_limit_bytes=DECODE_MIB * MIB),
        name="decode_first",
    )(info, *sum(groups, []), decoder, *after)


def later_wave_kernel(order, row, n, info, *refs):
    direct, swapped, (base, *kept) = refs[:n], refs[n : 2 * n], refs[2 * n : 2 * n + 3]
    out, sent, first, second, start, sem = refs[-6:]
    rows = out.shape[1]
    pairs, cols = out.shape[0], out.shape[2]
    copy = pltpu.make_async_copy(base.at[pl.ds(row, rows)], start, sem)
    copy.start()
    fill(order, direct, first)
    fill(order, swapped, second)
    copy.wait()

    @pl.loop(0, pairs)
    def _(j):
        at = pl.ds(pl.multiple_of(j * 2 * cols, 2 * cols), 2 * cols)

        @pl.when(info[1] == 1)
        def _():
            start[:, at] += jnp.dot(
                first[...], kept[0][:, at], preferred_element_type=jnp.float32
            ) + jnp.dot(second[...], kept[1][:, at], preferred_element_type=jnp.float32)

        split(info, start[:, at], out, sent, j)


def decode_later(info, direct, swapped, order, base, kept, row, shards, after):
    rows = sum(size for _, _, size in order)
    features, width = kept[0].shape
    kept = [pltpu.with_memory_space_constraint(weight, pltpu.VMEM) for weight in kept]
    return pl.pallas_call(
        functools.partial(later_wave_kernel, order, row, len(direct)),
        in_specs=[pl.BlockSpec(memory_space=pltpu.SMEM)]
        + [WHOLE] * (2 * len(direct))
        + [ANYWHERE, WHOLE, WHOLE]
        + [ANYWHERE] * len(after),
        out_specs=[WHOLE, WHOLE],
        out_shape=halves(shards, rows, width),
        scratch_shapes=[
            pltpu.VMEM((rows, features), jnp.bfloat16),
            pltpu.VMEM((rows, features), jnp.bfloat16),
            pltpu.VMEM((rows, width), jnp.float32),
            pltpu.SemaphoreType.DMA,
        ],
        compiler_params=pltpu.CompilerParams(vmem_limit_bytes=DECODE_MIB * MIB),
        name="decode_later",
    )(info, *direct, *swapped, base, *kept, *after)


def pair_kernel(size, n_after, info, mine, theirs, *refs):
    outs = refs[n_after:]
    z = info[5]
    rows = mine.shape[1]
    for q, out in enumerate(outs):
        for at in range(0, rows, size):
            partner = at // size ^ 1
            total = mine[z ^ q, pl.ds(at, size), :] + theirs[
                z ^ q, pl.ds(partner * size, size), :
            ].astype(jnp.float32)
            out[pl.ds(at, size), :] = total.astype(out.dtype)


def add_pair(info, mine, theirs, size, after):
    count, rows, cols = mine.shape
    return pl.pallas_call(
        functools.partial(pair_kernel, size, len(after)),
        in_specs=[pl.BlockSpec(memory_space=pltpu.SMEM), WHOLE, WHOLE] + [ANYWHERE] * len(after),
        out_specs=[WHOLE] * count,
        out_shape=[
            jax.ShapeDtypeStruct((rows, cols), jnp.float32 if q == 0 else jnp.bfloat16)
            for q in range(count)
        ],
        compiler_params=pltpu.CompilerParams(vmem_limit_bytes=SUM_MIB * MIB),
        name="add_pair",
    )(info, mine, theirs, *after)


def sum_kernel(sign, pieces, info, base, *refs):
    received, out = refs[: len(pieces)], refs[-1]
    me = info[6]
    out[...] = sign * base[...]
    for ref, (source, blocks) in zip(received, pieces):
        size = ref.shape[0] // len(blocks)
        for k, s in enumerate(blocks):
            at = pl.ds(pl.multiple_of((me ^ (source ^ s)) * size, size), size)
            out[at, :] += ref[pl.ds(k * size, size), :].astype(jnp.float32)


def add_up(info, base, sign, pieces, received, after):
    return pl.pallas_call(
        functools.partial(sum_kernel, sign, pieces),
        in_specs=[pl.BlockSpec(memory_space=pltpu.SMEM)]
        + [WHOLE] * (1 + len(received))
        + [ANYWHERE] * len(after),
        out_specs=WHOLE,
        out_shape=jax.ShapeDtypeStruct(base.shape, base.dtype),
        compiler_params=pltpu.CompilerParams(vmem_limit_bytes=SUM_MIB * MIB),
        name="add_up",
    )(info, base, *received, *after)


def pipelined(layer_inputs, targets, encoder, encoder_bias, decoder):
    shards = lax.axis_size("feat")
    layers = lax.axis_size("layer")
    half = layers // 2
    layer = lax.axis_index("layer")
    feat = lax.axis_index("feat")
    upper = layer >= half
    info = jnp.stack(
        [
            layer & 1,
            upper.astype(jnp.int32),
            jnp.full_like(layer, half),
            jnp.where(upper, layer - ((layer ^ 1) - half), 0),
            feat & 1,
            feat >> 1,
            feat,
        ]
    ).astype(jnp.int32)

    def up(a):
        return lax.ppermute(a, "layer", [(i, i + half) for i in range(half)])

    def across(a):
        return lax.ppermute(a, "layer", [(i, i ^ 1) for i in range(half, layers)])

    def beside(a):
        return lax.ppermute(a, "layer", [(i, i + 1) for i in range(0, layers, 2)])

    def after(value, *earlier):
        return lax.optimization_barrier((value, *earlier))[0]

    tokens = layer_inputs[0]
    size = tokens.shape[0]
    near = exchange(tokens, "feat", 1)
    far = [exchange(tokens, "feat", s) for s in range(2, shards, 2)]
    three = exchange(near, "feat", 2)

    a0, a0a, a0b, encoder_kept = encode(
        [tokens, near],
        [(0, 0, size), (1, 0, size)],
        [(0, 2 * size), (0, size), (size, size)],
        encoder,
        encoder_bias,
        [],
        stream=True,
    )
    d0a, d0b, n0 = up(a0a), up(a0b), beside(a0)
    rest = exchange(after(jnp.concatenate(far[1:], axis=0), far[0], three), "feat", 1)
    (a1,) = encode(
        [far[0], three],
        [(0, 0, size), (1, 0, size)],
        [(0, 2 * size)],
        encoder_kept,
        encoder_bias,
        [a0],
    )
    d1, n1 = up(a1), beside(a1)
    others = shards - 4
    order = []
    for k in range(others // 2):
        order += [(k, 0, size), (others // 2, k * size, size)]
    a2, a2a, a2b = encode(
        far[1:] + [rest],
        order,
        [(0, others * size), (0, (others - 1) * size), ((others - 1) * size, size)],
        encoder_kept,
        encoder_bias,
        [a1, d0a],
    )
    d2, d3, n2 = up(a2a), up(a2b), beside(after(a2, d0b))

    c0a, c0b = across(after(d0a, n2)), across(after(d0b, n2))
    mine, sent, base, *kept = decode_first(
        info, [a0, a1, a2], [n0, n1, n2], [d0a, d0b], [c0a, c0b], decoder, shards, []
    )
    slots = [[0, 1], [2, 3], list(range(4, shards - 2)), [shards - 2, shards - 1]]

    def meet(mine, sent, *earlier):
        return add_pair(info, mine, exchange(sent, "feat", 1), size, list(earlier))

    def spread(number, sums):
        parts = [part if q == 0 else exchange(part, "feat", 2 * q) for q, part in enumerate(sums)]
        return [(2 * q, slots[number]) for q in range(len(parts))], parts

    def later(number, direct, swapped, order, *earlier):
        row = slots[number][0] * size
        return decode_later(info, direct, swapped, order, base, kept, row, shards, list(earlier))

    c1 = across(after(d1, sent))
    mine1, sent1 = later(1, [d1], [c1], [(0, 0, 2 * size)], sent)
    met0 = meet(mine, sent, sent1)
    where0, parts0 = spread(0, met0)
    c2 = across(after(d2, met0[0]))
    early = (others - 2) * size
    mine2, sent2 = later(2, [d2], [c2], [(0, 0, early)], met0[0], *parts0)
    met1 = meet(mine1, sent1, sent2)
    where1, parts1 = spread(1, met1)
    c3 = across(after(d3, met1[0]))
    total = add_up(info, targets[0], -1.0, where0 + where1, parts0 + parts1, [met1[0]])
    order = [(0, early, size), (1, 0, size)]
    mine3, sent3 = later(3, [d2, d3], [c2, c3], order, sent2, total)
    met2 = meet(mine2, sent2, sent3)
    where2, parts2 = spread(2, met2)
    met3 = meet(mine3, sent3, met2[0], parts2[1])
    where3, parts3 = spread(3, met3)
    return add_up(info, total, 1.0, where2 + where3, parts2 + parts3, [])[None]


def grouped(layer_inputs, targets, encoder, encoder_bias, decoder):
    groups = lax.axis_size("layer") // L_WIN
    depth_bits = groups.bit_length() - 1
    position = lax.axis_index("layer")
    target_layer = position // groups
    group_index = position % groups
    gathered = lax.all_gather(layer_inputs[0], "feat", axis=0, tiled=True)
    for bit_index in range(depth_bits):
        partner = exchange(gathered, "layer", 1 << bit_index)
        upper_bit = position >> bit_index & 1
        gathered = jnp.where(
            upper_bit == 1,
            jnp.concatenate([partner, gathered], 0),
            jnp.concatenate([gathered, partner], 0),
        )
    preact = (
        jnp.dot(gathered, encoder[0], preferred_element_type=jnp.float32) + encoder_bias[0][None, :]
    )
    features = jax.nn.relu(preact).astype(jnp.bfloat16)
    tok_count = features.shape[0]
    every_layer = lax.all_gather(features[None], "layer", axis=0, tiled=True)
    by_layer = every_layer.reshape(L_WIN, groups, tok_count, features.shape[1])
    mine_only = lax.dynamic_index_in_dim(by_layer, group_index, 1, keepdims=False)
    flipped = mine_only[::-1]
    padded = jnp.concatenate([flipped, jnp.zeros_like(flipped)], 0)
    stacked = lax.dynamic_slice_in_dim(padded, L_WIN - 1 - target_layer, L_WIN, 0)
    rebuilt = jnp.einsum("ktf,kfd->td", stacked, decoder[0], preferred_element_type=jnp.float32)
    for bit_index in reversed(range(depth_bits)):
        half_rows = rebuilt.shape[0] // 2
        upper_bit = position >> bit_index & 1
        kept_half = jnp.where(upper_bit == 1, rebuilt[half_rows:], rebuilt[:half_rows])
        sent_half = jnp.where(upper_bit == 1, rebuilt[:half_rows], rebuilt[half_rows:])
        rebuilt = kept_half + exchange(sent_half, "layer", 1 << bit_index)
    summed = lax.psum_scatter(rebuilt, "feat", scatter_dimension=1, tiled=True)
    residual = summed - targets[0]
    return residual[None]


def solution(mesh):
    placed = (
        P("layer", "feat", None),
        P("layer", None, "feat"),
        P("layer", None, "feat"),
        P("layer", "feat"),
        P("layer", None, "feat", None),
    )
    shards = mesh.shape["feat"]
    simple = mesh.shape["layer"] == L_WIN and shards >= 8 and shards & (shards - 1) == 0
    return jax.shard_map(
        pipelined if simple else grouped,
        mesh=mesh,
        in_specs=placed,
        out_specs=P("layer", None, "feat"),
        check_vma=False,
    )
```

```python
import functools

import jax
import jax.numpy as jnp
from jax import lax
from jax.experimental import pallas as pl
from jax.experimental.pallas import tpu as pltpu
from jax.sharding import PartitionSpec as P

L_WIN = 4
MIB = 1024 * 1024


def exchange(array, axis, flip):
    size = lax.axis_size(axis)
    return lax.ppermute(array, axis, [(i, i ^ flip) for i in range(size)])


ANYWHERE = pl.BlockSpec(memory_space=pl.ANY)
WHOLE = pl.BlockSpec(memory_space=pltpu.VMEM)
SLOTS = 3
ENCODE_MIB = 16
DECODE_MIB = 26
SUM_MIB = 12


def landed(array):
    return pltpu.with_memory_space_constraint(array, pltpu.VMEM)


def fill(order, parts, rows_of):
    at = 0
    for part, row, size in order:
        rows_of[pl.ds(at, size), :] = parts[part][pl.ds(row, size), :]
        at += size


def encode_kernel(order, pieces, n_in, n_after, stream, *refs):
    parts, weight, bias, refs = refs[:n_in], refs[n_in], refs[n_in + 1], refs[n_in + 2 + n_after :]
    outs, refs = refs[: len(pieces)], refs[len(pieces) :]
    features = weight.shape[2]
    if stream:
        kept, tokens, sems = refs
        block = features // sems.shape[0]
    else:
        kept, (tokens,) = weight, refs
        block = min(512, features)

    def fetch(j):
        cols = pl.ds(pl.multiple_of(j * block, block), block)
        return pltpu.make_async_copy(weight.at[0, :, cols], kept.at[0, :, cols], sems.at[j])

    if stream:
        for j in range(features // block):
            fetch(jnp.int32(j)).start()
    fill(order, parts, tokens)

    @pl.loop(0, features // block)
    def _(j):
        if stream:
            fetch(j).wait()
        cols = pl.ds(pl.multiple_of(j * block, block), block)
        preact = jnp.dot(tokens[...], kept[0, :, cols], preferred_element_type=jnp.float32)
        acts = jnp.maximum(preact + bias[:, cols], 0.0).astype(jnp.bfloat16)
        for out, (row, size) in zip(outs, pieces):
            out[:, cols] = acts[row : row + size]


def encode(parts, order, pieces, weight, bias, after, stream=False):
    rows = sum(size for _, _, size in order)
    _, width, features = weight.shape
    out_shape = [jax.ShapeDtypeStruct((size, features), jnp.bfloat16) for _, size in pieces]
    scratch = [pltpu.VMEM((rows, width), jnp.bfloat16)]
    if stream:
        out_shape.append(pltpu.VMEM(weight.shape, weight.dtype))
        scratch.append(pltpu.SemaphoreType.DMA((max(1, features // 512),)))
        weight = pltpu.with_memory_space_constraint(weight, pltpu.HBM)
    else:
        weight = pltpu.with_memory_space_constraint(weight, pltpu.VMEM)
    return pl.pallas_call(
        functools.partial(encode_kernel, order, pieces, len(parts), len(after), stream),
        in_specs=[WHOLE] * len(parts) + [ANYWHERE if stream else WHOLE, WHOLE] + [ANYWHERE] * len(after),
        out_specs=[WHOLE] * len(out_shape),
        out_shape=out_shape,
        scratch_shapes=scratch,
        compiler_params=pltpu.CompilerParams(vmem_limit_bytes=ENCODE_MIB * MIB),
        name="encode",
    )(*parts, weight, bias, *after)


def split(info, value, out, sent, j):
    cols = out.shape[2]
    low, high = value[:, :cols], value[:, cols:]

    @pl.when(info[4] == 0)
    def _():
        out[j] = low
        sent[j] = high.astype(sent.dtype)

    @pl.when(info[4] == 1)
    def _():
        out[j] = high
        sent[j] = low.astype(sent.dtype)


def halves(shards, rows, width):
    shape = (shards // 2, rows, width // shards)
    return [jax.ShapeDtypeStruct(shape, jnp.float32), jax.ShapeDtypeStruct(shape, jnp.bfloat16)]


def first_wave_kernel(counts, info, *refs):
    groups = []
    for count in counts:
        groups.append(refs[:count])
        refs = refs[count:]
    mine, theirs, direct, swapped = groups
    weights, out, sent, base, *kept = refs[:6]
    total, rings, ring_sems, kept_sems, base_sem = refs[-5:]
    step, steps = pl.program_id(0), pl.num_programs(0)
    slots, block = rings.shape[1], rings.shape[2]
    odd, upper = info[0] == 1, info[1] == 1

    def rows(k):
        return pl.ds(pl.multiple_of(k * block, block), block)

    def fetch(source, k):
        slot = lax.rem(k, slots)
        return pltpu.make_async_copy(
            weights.at[0, source, rows(k)], rings.at[source, slot], ring_sems.at[source, slot]
        )

    def keep(source, k):
        return pltpu.make_async_copy(
            weights.at[0, info[2 + source], rows(k)],
            kept[source].at[rows(k)],
            kept_sems.at[source, k],
        )

    def fetch_all(k):
        fetch(0, k).start()
        pl.when(odd)(lambda: fetch(1, k).start())

        @pl.when(upper)
        def _():
            keep(0, k).start()
            keep(1, k).start()

    @pl.when(step == 0)
    def _():
        for k in range(slots - 1):
            fetch_all(jnp.int32(k))
        total[...] = jnp.zeros_like(total)

    pl.when(step + slots - 1 < steps)(lambda: fetch_all(step + slots - 1))

    def product(parts, weight):
        values = [part[...] for part in parts]
        acts = values[0] if len(values) == 1 else jnp.concatenate(values, axis=0)
        return jnp.dot(acts, weight, preferred_element_type=jnp.float32)

    slot = lax.rem(step, slots)
    fetch(0, step).wait()

    @pl.when(jnp.logical_not(odd))
    def _():
        total[...] += product(mine, rings[0, slot])

    @pl.when(odd)
    def _():
        fetch(1, step).wait()
        total[...] += product(mine, rings[0, slot]) + product(theirs, rings[1, slot])

    done = out.shape[1]

    @pl.when(upper)
    def _():
        keep(0, step).wait()
        keep(1, step).wait()
        total[:done, :] += product(direct, kept[0][rows(step), :]) + product(
            swapped, kept[1][rows(step), :]
        )

    @pl.when(step == steps - 1)
    def _():
        rest = pl.ds(done, total.shape[0] - done)
        copy = pltpu.make_async_copy(total.at[rest], base, base_sem)
        copy.start()
        cols = out.shape[2]
        for j in range(out.shape[0]):
            split(info, total[:done, 2 * j * cols : 2 * (j + 1) * cols], out, sent, j)
        copy.wait()


def decode_first(info, mine, theirs, direct, swapped, decoder, shards, after):
    _, _, features, width = decoder.shape
    block = min(512, features)
    steps = features // block
    rows = sum(part.shape[0] for part in mine)
    done = sum(part.shape[0] for part in direct)

    def acts(part, flag):
        return pl.BlockSpec(
            (part.shape[0], block), lambda k, info: (0, k if flag is None else k * info[flag])
        )

    groups = (mine, theirs, direct, swapped)
    in_specs = [acts(p, flag) for parts, flag in zip(groups, (None, 0, 1, 1)) for p in parts]
    return pl.pallas_call(
        functools.partial(first_wave_kernel, [len(parts) for parts in groups]),
        grid_spec=pltpu.PrefetchScalarGridSpec(
            num_scalar_prefetch=1,
            grid=(steps,),
            in_specs=in_specs + [ANYWHERE] * (1 + len(after)),
            out_specs=[
                *[pl.BlockSpec(h.shape, lambda k, info: (0, 0, 0)) for h in halves(shards, done, width)],
                ANYWHERE,
                WHOLE,
                WHOLE,
            ],
            scratch_shapes=[
                pltpu.VMEM((rows, width), jnp.float32),
                pltpu.VMEM((2, SLOTS, block, width), decoder.dtype),
                pltpu.SemaphoreType.DMA((2, SLOTS)),
                pltpu.SemaphoreType.DMA((2, steps)),
                pltpu.SemaphoreType.DMA,
            ],
        ),
        out_shape=[
            *halves(shards, done, width),
            pltpu.HBM((rows - done, width), jnp.float32),
            pltpu.VMEM((features, width), decoder.dtype),
            pltpu.VMEM((features, width), decoder.dtype),
        ],
        compiler_params=pltpu.CompilerParams(vmem_limit_bytes=DECODE_MIB * MIB),
        name="decode_first",
    )(info, *sum(groups, []), decoder, *after)


def later_wave_kernel(order, row, n, info, *refs):
    direct, swapped, (base, *kept) = refs[:n], refs[n : 2 * n], refs[2 * n : 2 * n + 3]
    out, sent, first, second, start, sem = refs[-6:]
    rows = out.shape[1]
    pairs, cols = out.shape[0], out.shape[2]
    copy = pltpu.make_async_copy(base.at[pl.ds(row, rows)], start, sem)
    copy.start()
    fill(order, direct, first)
    fill(order, swapped, second)
    copy.wait()

    @pl.loop(0, pairs)
    def _(j):
        at = pl.ds(pl.multiple_of(j * 2 * cols, 2 * cols), 2 * cols)

        @pl.when(info[1] == 1)
        def _():
            start[:, at] += jnp.dot(
                first[...], kept[0][:, at], preferred_element_type=jnp.float32
            ) + jnp.dot(second[...], kept[1][:, at], preferred_element_type=jnp.float32)

        split(info, start[:, at], out, sent, j)


def decode_later(info, direct, swapped, order, base, kept, row, shards, after):
    rows = sum(size for _, _, size in order)
    features, width = kept[0].shape
    return pl.pallas_call(
        functools.partial(later_wave_kernel, order, row, len(direct)),
        in_specs=[pl.BlockSpec(memory_space=pltpu.SMEM)]
        + [WHOLE] * (2 * len(direct))
        + [ANYWHERE, WHOLE, WHOLE]
        + [ANYWHERE] * len(after),
        out_specs=[WHOLE, WHOLE],
        out_shape=halves(shards, rows, width),
        scratch_shapes=[
            pltpu.VMEM((rows, features), jnp.bfloat16),
            pltpu.VMEM((rows, features), jnp.bfloat16),
            pltpu.VMEM((rows, width), jnp.float32),
            pltpu.SemaphoreType.DMA,
        ],
        compiler_params=pltpu.CompilerParams(vmem_limit_bytes=DECODE_MIB * MIB),
        name="decode_later",
    )(info, *map(landed, direct), *map(landed, swapped), base, *map(landed, kept), *after)


def pair_kernel(size, n, n_after, info, *refs):
    mine, theirs, outs = refs[:n], refs[n : 2 * n], refs[2 * n + n_after :]
    z = info[5]
    for q, out in enumerate(outs):
        row = 0
        for kept, met in zip(mine, theirs):
            rows = kept.shape[1]
            for at in range(0, rows, size):
                partner = at // size ^ 1
                total = kept[z ^ q, pl.ds(at, size), :] + met[
                    z ^ q, pl.ds(partner * size, size), :
                ].astype(jnp.float32)
                out[pl.ds(row + at, size), :] = total.astype(out.dtype)
            row += rows


def add_pair(info, mine, theirs, size, after):
    count, _, cols = mine[0].shape
    rows = sum(kept.shape[1] for kept in mine)
    return pl.pallas_call(
        functools.partial(pair_kernel, size, len(mine), len(after)),
        in_specs=[pl.BlockSpec(memory_space=pltpu.SMEM)]
        + [WHOLE] * (2 * len(mine))
        + [ANYWHERE] * len(after),
        out_specs=[WHOLE] * count,
        out_shape=[
            jax.ShapeDtypeStruct((rows, cols), jnp.float32 if q == 0 else jnp.bfloat16)
            for q in range(count)
        ],
        compiler_params=pltpu.CompilerParams(vmem_limit_bytes=SUM_MIB * MIB),
        name="add_pair",
    )(info, *mine, *[landed(array) for array in theirs], *after)


def sum_kernel(sign, pieces, info, base, *refs):
    received, out = refs[: len(pieces)], refs[-1]
    me = info[6]
    out[...] = sign * base[...]
    for ref, (source, blocks) in zip(received, pieces):
        size = ref.shape[0] // len(blocks)
        for k, s in enumerate(blocks):
            at = pl.ds(pl.multiple_of((me ^ (source ^ s)) * size, size), size)
            out[at, :] += ref[pl.ds(k * size, size), :].astype(jnp.float32)


def add_up(info, base, sign, pieces, received, after):
    return pl.pallas_call(
        functools.partial(sum_kernel, sign, pieces),
        in_specs=[pl.BlockSpec(memory_space=pltpu.SMEM)]
        + [WHOLE] * (1 + len(received))
        + [ANYWHERE] * len(after),
        out_specs=WHOLE,
        out_shape=jax.ShapeDtypeStruct(base.shape, base.dtype),
        compiler_params=pltpu.CompilerParams(vmem_limit_bytes=SUM_MIB * MIB),
        name="add_up",
    )(info, base, *map(landed, received), *after)


def pipelined(layer_inputs, targets, encoder, encoder_bias, decoder):
    shards = lax.axis_size("feat")
    layers = lax.axis_size("layer")
    half = layers // 2
    layer = lax.axis_index("layer")
    feat = lax.axis_index("feat")
    upper = layer >= half
    info = jnp.stack(
        [
            layer & 1,
            upper.astype(jnp.int32),
            jnp.full_like(layer, half),
            jnp.where(upper, layer - ((layer ^ 1) - half), 0),
            feat & 1,
            feat >> 1,
            feat,
        ]
    ).astype(jnp.int32)

    def up(a):
        return lax.ppermute(a, "layer", [(i, i + half) for i in range(half)])

    def across(a):
        return lax.ppermute(a, "layer", [(i, i ^ 1) for i in range(half, layers)])

    def beside(a):
        return lax.ppermute(a, "layer", [(i, i + 1) for i in range(0, layers, 2)])

    def after(value, *earlier):
        return lax.optimization_barrier((value, *earlier))[0]

    tokens = layer_inputs[0]
    size = tokens.shape[0]
    near = exchange(tokens, "feat", 1)
    far = [exchange(tokens, "feat", s) for s in range(2, shards, 2)]
    three = exchange(near, "feat", 2)

    a0, a0a, a0b, encoder_kept = encode(
        [tokens, near],
        [(0, 0, size), (1, 0, size)],
        [(0, 2 * size), (0, size), (size, size)],
        encoder,
        encoder_bias,
        [],
        stream=True,
    )
    d0a, d0b, n0 = up(a0a), up(a0b), beside(a0)
    rest = exchange(after(jnp.concatenate(far[1:], axis=0), far[0], three), "feat", 1)
    (a1,) = encode(
        [far[0], three],
        [(0, 0, size), (1, 0, size)],
        [(0, 2 * size)],
        encoder_kept,
        encoder_bias,
        [a0],
    )
    d1, n1 = up(a1), beside(a1)
    others = shards - 4
    order = []
    for k in range(others // 2):
        order += [(k, 0, size), (others // 2, k * size, size)]
    a2, a2a, a2b = encode(
        far[1:] + [rest],
        order,
        [(0, others * size), (0, (others - 2) * size), ((others - 2) * size, 2 * size)],
        encoder_kept,
        encoder_bias,
        [a1, d0a],
    )
    d2, d3, n2 = up(a2a), up(a2b), beside(after(a2, d0b))

    c0a, c0b = across(after(d0a, n2)), across(after(d0b, n2))
    mine, sent, base, *kept = decode_first(
        info, [a0, a1, a2], [n0, n1, n2], [d0a, d0b], [c0a, c0b], decoder, shards, []
    )
    slots = [[0, 1], [2, 3], list(range(4, shards - 2)), [shards - 2, shards - 1]]

    def meet(mine, sent, *earlier):
        theirs = [exchange(array, "feat", 1) for array in sent]
        return add_pair(info, mine, theirs, size, list(earlier))

    def spread(blocks, sums):
        parts = [part if q == 0 else exchange(part, "feat", 2 * q) for q, part in enumerate(sums)]
        return [(2 * q, blocks) for q in range(len(parts))], parts

    def later(number, direct, swapped, *earlier):
        row = (slots[number][0] - slots[1][0]) * size
        order = [(0, 0, len(slots[number]) * size)]
        return decode_later(info, [direct], [swapped], order, base, kept, row, shards, list(earlier))

    c1, c2 = across(after(d1, sent)), across(after(d2, sent))
    mine1, sent1 = later(1, d1, c1, sent, d2)
    met1 = meet([mine, mine1], [sent, sent1])
    where1, parts1 = spread(slots[0] + slots[1], met1)
    c3 = across(after(d3, met1[0]))
    mine2, sent2 = later(2, d2, c2, met1[0])
    total = add_up(info, targets[0], -1.0, where1, parts1, [sent2])
    mine3, sent3 = later(3, d3, c3, sent2, total)
    met2 = meet([mine2], [sent2], sent3)
    where2, parts2 = spread(slots[2], met2)
    met3 = meet([mine3], [sent3], parts2[1])
    where3, parts3 = spread(slots[3], met3)
    return add_up(info, total, 1.0, where2 + where3, parts2 + parts3, [])[None]


def grouped(layer_inputs, targets, encoder, encoder_bias, decoder):
    groups = lax.axis_size("layer") // L_WIN
    depth_bits = groups.bit_length() - 1
    position = lax.axis_index("layer")
    target_layer = position // groups
    group_index = position % groups
    gathered = lax.all_gather(layer_inputs[0], "feat", axis=0, tiled=True)
    for bit_index in range(depth_bits):
        partner = exchange(gathered, "layer", 1 << bit_index)
        upper_bit = position >> bit_index & 1
        gathered = jnp.where(
            upper_bit == 1,
            jnp.concatenate([partner, gathered], 0),
            jnp.concatenate([gathered, partner], 0),
        )
    preact = (
        jnp.dot(gathered, encoder[0], preferred_element_type=jnp.float32) + encoder_bias[0][None, :]
    )
    features = jax.nn.relu(preact).astype(jnp.bfloat16)
    tok_count = features.shape[0]
    every_layer = lax.all_gather(features[None], "layer", axis=0, tiled=True)
    by_layer = every_layer.reshape(L_WIN, groups, tok_count, features.shape[1])
    mine_only = lax.dynamic_index_in_dim(by_layer, group_index, 1, keepdims=False)
    flipped = mine_only[::-1]
    padded = jnp.concatenate([flipped, jnp.zeros_like(flipped)], 0)
    stacked = lax.dynamic_slice_in_dim(padded, L_WIN - 1 - target_layer, L_WIN, 0)
    rebuilt = jnp.einsum("ktf,kfd->td", stacked, decoder[0], preferred_element_type=jnp.float32)
    for bit_index in reversed(range(depth_bits)):
        half_rows = rebuilt.shape[0] // 2
        upper_bit = position >> bit_index & 1
        kept_half = jnp.where(upper_bit == 1, rebuilt[half_rows:], rebuilt[:half_rows])
        sent_half = jnp.where(upper_bit == 1, rebuilt[:half_rows], rebuilt[half_rows:])
        rebuilt = kept_half + exchange(sent_half, "layer", 1 << bit_index)
    summed = lax.psum_scatter(rebuilt, "feat", scatter_dimension=1, tiled=True)
    residual = summed - targets[0]
    return residual[None]


def solution(mesh):
    placed = (
        P("layer", "feat", None),
        P("layer", None, "feat"),
        P("layer", None, "feat"),
        P("layer", "feat"),
        P("layer", None, "feat", None),
    )
    shards = mesh.shape["feat"]
    simple = mesh.shape["layer"] == L_WIN and shards >= 8 and shards & (shards - 1) == 0
    return jax.shard_map(
        pipelined if simple else grouped,
        mesh=mesh,
        in_specs=placed,
        out_specs=P("layer", None, "feat"),
        check_vma=False,
    )
```

```python
import functools

import jax
import jax.numpy as jnp
from jax import lax
from jax.experimental import pallas as pl
from jax.experimental.pallas import tpu as pltpu
from jax.sharding import PartitionSpec as P

L_WIN = 4
MIB = 1024 * 1024


def exchange(array, axis, flip):
    size = lax.axis_size(axis)
    return lax.ppermute(array, axis, [(i, i ^ flip) for i in range(size)])


ANYWHERE = pl.BlockSpec(memory_space=pl.ANY)
WHOLE = pl.BlockSpec(memory_space=pltpu.VMEM)
SLOTS = 3
ENCODE_MIB = 16
DECODE_MIB = 26
SUM_MIB = 12


def landed(array):
    return pltpu.with_memory_space_constraint(array, pltpu.VMEM)


def fill(order, parts, rows_of, at=0):
    for part, row, size in order:
        rows_of[pl.ds(at, size), :] = parts[part][pl.ds(row, size), :]
        at += size


def encode_kernel(order, pieces, n_in, n_after, stream, *refs):
    parts, weight, bias, refs = refs[:n_in], refs[n_in], refs[n_in + 1], refs[n_in + 2 + n_after :]
    outs, refs = refs[: len(pieces)], refs[len(pieces) :]
    features = weight.shape[2]
    if stream:
        kept, tokens, sems, bias_here, start_sems = refs
        block = features // sems.shape[0]
        size = parts[0].shape[0]
        starts = [
            pltpu.make_async_copy(parts[0], tokens.at[pl.ds(0, size)], start_sems.at[0]),
            pltpu.make_async_copy(bias, bias_here, start_sems.at[1]),
        ]
        for copy in starts:
            copy.start()
        bias = bias_here
    else:
        kept, (tokens,) = weight, refs
        block = min(512, features)

    def fetch(j):
        cols = pl.ds(pl.multiple_of(j * block, block), block)
        return pltpu.make_async_copy(weight.at[0, :, cols], kept.at[0, :, cols], sems.at[j])

    if stream:
        for j in range(features // block):
            fetch(jnp.int32(j)).start()
        fill(order[1:], parts, tokens, size)
        for copy in starts:
            copy.wait()
    else:
        fill(order, parts, tokens)

    @pl.loop(0, features // block)
    def _(j):
        if stream:
            fetch(j).wait()
        cols = pl.ds(pl.multiple_of(j * block, block), block)
        preact = jnp.dot(tokens[...], kept[0, :, cols], preferred_element_type=jnp.float32)
        acts = jnp.maximum(preact + bias[:, cols], 0.0).astype(jnp.bfloat16)
        for out, (row, size) in zip(outs, pieces):
            out[:, cols] = acts[row : row + size]


def encode(parts, order, pieces, weight, bias, after, stream=False):
    rows = sum(size for _, _, size in order)
    _, width, features = weight.shape
    out_shape = [jax.ShapeDtypeStruct((size, features), jnp.bfloat16) for _, size in pieces]
    scratch = [pltpu.VMEM((rows, width), jnp.bfloat16)]
    if stream:
        out_shape.append(pltpu.VMEM(weight.shape, weight.dtype))
        scratch += [
            pltpu.SemaphoreType.DMA((max(1, features // 512),)),
            pltpu.VMEM(bias.shape, bias.dtype),
            pltpu.SemaphoreType.DMA((2,)),
        ]
        first, weight, bias = (
            pltpu.with_memory_space_constraint(array, pltpu.HBM) for array in (parts[0], weight, bias)
        )
        parts = [first, *parts[1:]]
    else:
        weight = pltpu.with_memory_space_constraint(weight, pltpu.VMEM)
    return pl.pallas_call(
        functools.partial(encode_kernel, order, pieces, len(parts), len(after), stream),
        in_specs=[ANYWHERE if stream else WHOLE]
        + [WHOLE] * (len(parts) - 1)
        + [ANYWHERE if stream else WHOLE] * 2
        + [ANYWHERE] * len(after),
        out_specs=[WHOLE] * len(out_shape),
        out_shape=out_shape,
        scratch_shapes=scratch,
        compiler_params=pltpu.CompilerParams(vmem_limit_bytes=ENCODE_MIB * MIB),
        name="encode",
    )(*parts, weight, bias, *after)


def split(info, value, out, sent, j):
    cols = out.shape[2]
    low, high = value[:, :cols], value[:, cols:]

    @pl.when(info[4] == 0)
    def _():
        out[j] = low
        sent[j] = high.astype(sent.dtype)

    @pl.when(info[4] == 1)
    def _():
        out[j] = high
        sent[j] = low.astype(sent.dtype)


def halves(shards, rows, width):
    shape = (shards // 2, rows, width // shards)
    return [jax.ShapeDtypeStruct(shape, jnp.float32), jax.ShapeDtypeStruct(shape, jnp.bfloat16)]


def first_wave_kernel(counts, info, *refs):
    groups = []
    for count in counts:
        groups.append(refs[:count])
        refs = refs[count:]
    mine, theirs, direct, swapped = groups
    weights, out, sent, base, *kept = refs[:6]
    total, rings, ring_sems, kept_sems, base_sem = refs[-5:]
    step, steps = pl.program_id(0), pl.num_programs(0)
    slots, block = rings.shape[1], rings.shape[2]
    odd, upper = info[0] == 1, info[1] == 1

    def rows(k):
        return pl.ds(pl.multiple_of(k * block, block), block)

    def fetch(source, k):
        slot = lax.rem(k, slots)
        return pltpu.make_async_copy(
            weights.at[0, source, rows(k)], rings.at[source, slot], ring_sems.at[source, slot]
        )

    def keep(source, k):
        return pltpu.make_async_copy(
            weights.at[0, info[2 + source], rows(k)],
            kept[source].at[rows(k)],
            kept_sems.at[source, k],
        )

    def fetch_all(k):
        fetch(0, k).start()
        pl.when(odd)(lambda: fetch(1, k).start())

        @pl.when(upper)
        def _():
            keep(0, k).start()
            keep(1, k).start()

    @pl.when(step == 0)
    def _():
        for k in range(slots - 1):
            fetch_all(jnp.int32(k))
        total[...] = jnp.zeros_like(total)

    pl.when(step + slots - 1 < steps)(lambda: fetch_all(step + slots - 1))

    def product(parts, weight):
        values = [part[...] for part in parts]
        acts = values[0] if len(values) == 1 else jnp.concatenate(values, axis=0)
        return jnp.dot(acts, weight, preferred_element_type=jnp.float32)

    slot = lax.rem(step, slots)
    fetch(0, step).wait()

    @pl.when(jnp.logical_not(odd))
    def _():
        total[...] += product(mine, rings[0, slot])

    @pl.when(odd)
    def _():
        fetch(1, step).wait()
        total[...] += product(mine, rings[0, slot]) + product(theirs, rings[1, slot])

    done = out.shape[1]

    @pl.when(upper)
    def _():
        keep(0, step).wait()
        keep(1, step).wait()
        total[:done, :] += product(direct, kept[0][rows(step), :]) + product(
            swapped, kept[1][rows(step), :]
        )

    @pl.when(step == steps - 1)
    def _():
        rest = pl.ds(done, total.shape[0] - done)
        copy = pltpu.make_async_copy(total.at[rest], base, base_sem)
        copy.start()
        cols = out.shape[2]
        for j in range(out.shape[0]):
            split(info, total[:done, 2 * j * cols : 2 * (j + 1) * cols], out, sent, j)
        copy.wait()


def decode_first(info, mine, theirs, direct, swapped, decoder, shards, after):
    _, _, features, width = decoder.shape
    block = min(512, features)
    steps = features // block
    rows = sum(part.shape[0] for part in mine)
    done = sum(part.shape[0] for part in direct)

    def acts(part, flag):
        return pl.BlockSpec(
            (part.shape[0], block), lambda k, info: (0, k if flag is None else k * info[flag])
        )

    groups = (mine, theirs, direct, swapped)
    in_specs = [acts(p, flag) for parts, flag in zip(groups, (None, 0, 1, 1)) for p in parts]
    return pl.pallas_call(
        functools.partial(first_wave_kernel, [len(parts) for parts in groups]),
        grid_spec=pltpu.PrefetchScalarGridSpec(
            num_scalar_prefetch=1,
            grid=(steps,),
            in_specs=in_specs + [ANYWHERE] * (1 + len(after)),
            out_specs=[
                *[pl.BlockSpec(h.shape, lambda k, info: (0, 0, 0)) for h in halves(shards, done, width)],
                ANYWHERE,
                WHOLE,
                WHOLE,
            ],
            scratch_shapes=[
                pltpu.VMEM((rows, width), jnp.float32),
                pltpu.VMEM((2, SLOTS, block, width), decoder.dtype),
                pltpu.SemaphoreType.DMA((2, SLOTS)),
                pltpu.SemaphoreType.DMA((2, steps)),
                pltpu.SemaphoreType.DMA,
            ],
        ),
        out_shape=[
            *halves(shards, done, width),
            pltpu.HBM((rows - done, width), jnp.float32),
            pltpu.VMEM((features, width), decoder.dtype),
            pltpu.VMEM((features, width), decoder.dtype),
        ],
        compiler_params=pltpu.CompilerParams(vmem_limit_bytes=DECODE_MIB * MIB),
        name="decode_first",
    )(info, *sum(groups, []), decoder, *after)


def later_wave_kernel(order, row, n, info, *refs):
    direct, swapped, (base, *kept) = refs[:n], refs[n : 2 * n], refs[2 * n : 2 * n + 3]
    out, sent, first, second, start, sem = refs[-6:]
    rows = out.shape[1]
    pairs, cols = out.shape[0], out.shape[2]
    copy = pltpu.make_async_copy(base.at[pl.ds(row, rows)], start, sem)
    copy.start()
    fill(order, direct, first)
    fill(order, swapped, second)
    copy.wait()

    @pl.loop(0, pairs)
    def _(j):
        at = pl.ds(pl.multiple_of(j * 2 * cols, 2 * cols), 2 * cols)

        @pl.when(info[1] == 1)
        def _():
            start[:, at] += jnp.dot(
                first[...], kept[0][:, at], preferred_element_type=jnp.float32
            ) + jnp.dot(second[...], kept[1][:, at], preferred_element_type=jnp.float32)

        split(info, start[:, at], out, sent, j)


def decode_later(info, direct, swapped, order, base, kept, row, shards, after):
    rows = sum(size for _, _, size in order)
    features, width = kept[0].shape
    return pl.pallas_call(
        functools.partial(later_wave_kernel, order, row, len(direct)),
        in_specs=[pl.BlockSpec(memory_space=pltpu.SMEM)]
        + [WHOLE] * (2 * len(direct))
        + [ANYWHERE, WHOLE, WHOLE]
        + [ANYWHERE] * len(after),
        out_specs=[WHOLE, WHOLE],
        out_shape=halves(shards, rows, width),
        scratch_shapes=[
            pltpu.VMEM((rows, features), jnp.bfloat16),
            pltpu.VMEM((rows, features), jnp.bfloat16),
            pltpu.VMEM((rows, width), jnp.float32),
            pltpu.SemaphoreType.DMA,
        ],
        compiler_params=pltpu.CompilerParams(vmem_limit_bytes=DECODE_MIB * MIB),
        name="decode_later",
    )(info, *map(landed, direct), *map(landed, swapped), base, *map(landed, kept), *after)


def pair_kernel(size, n, n_after, info, *refs):
    mine, theirs, outs = refs[:n], refs[n : 2 * n], refs[2 * n + n_after :]
    z = info[5]
    for q, out in enumerate(outs):
        row = 0
        for kept, met in zip(mine, theirs):
            rows = kept.shape[1]
            for at in range(0, rows, size):
                partner = at // size ^ 1
                total = kept[z ^ q, pl.ds(at, size), :] + met[
                    z ^ q, pl.ds(partner * size, size), :
                ].astype(jnp.float32)
                out[pl.ds(row + at, size), :] = total.astype(out.dtype)
            row += rows


def add_pair(info, mine, theirs, size, after):
    count, _, cols = mine[0].shape
    rows = sum(kept.shape[1] for kept in mine)
    return pl.pallas_call(
        functools.partial(pair_kernel, size, len(mine), len(after)),
        in_specs=[pl.BlockSpec(memory_space=pltpu.SMEM)]
        + [WHOLE] * (2 * len(mine))
        + [ANYWHERE] * len(after),
        out_specs=[WHOLE] * count,
        out_shape=[
            jax.ShapeDtypeStruct((rows, cols), jnp.float32 if q == 0 else jnp.bfloat16)
            for q in range(count)
        ],
        compiler_params=pltpu.CompilerParams(vmem_limit_bytes=SUM_MIB * MIB),
        name="add_pair",
    )(info, *mine, *[landed(array) for array in theirs], *after)


def sum_kernel(sign, pieces, info, base, *refs):
    received, out = refs[: len(pieces)], refs[-1]
    me = info[6]
    out[...] = sign * base[...]
    for ref, (source, blocks) in zip(received, pieces):
        size = ref.shape[0] // len(blocks)
        for k, s in enumerate(blocks):
            at = pl.ds(pl.multiple_of((me ^ (source ^ s)) * size, size), size)
            out[at, :] += ref[pl.ds(k * size, size), :].astype(jnp.float32)


def add_up(info, base, sign, pieces, received, after):
    return pl.pallas_call(
        functools.partial(sum_kernel, sign, pieces),
        in_specs=[pl.BlockSpec(memory_space=pltpu.SMEM)]
        + [WHOLE] * (1 + len(received))
        + [ANYWHERE] * len(after),
        out_specs=WHOLE,
        out_shape=jax.ShapeDtypeStruct(base.shape, base.dtype),
        compiler_params=pltpu.CompilerParams(vmem_limit_bytes=SUM_MIB * MIB),
        name="add_up",
    )(info, base, *map(landed, received), *after)


def pipelined(layer_inputs, targets, encoder, encoder_bias, decoder):
    shards = lax.axis_size("feat")
    layers = lax.axis_size("layer")
    half = layers // 2
    layer = lax.axis_index("layer")
    feat = lax.axis_index("feat")
    upper = layer >= half
    info = jnp.stack(
        [
            layer & 1,
            upper.astype(jnp.int32),
            jnp.full_like(layer, half),
            jnp.where(upper, layer - ((layer ^ 1) - half), 0),
            feat & 1,
            feat >> 1,
            feat,
        ]
    ).astype(jnp.int32)

    def up(a):
        return lax.ppermute(a, "layer", [(i, i + half) for i in range(half)])

    def across(a):
        return lax.ppermute(a, "layer", [(i, i ^ 1) for i in range(half, layers)])

    def beside(a):
        return lax.ppermute(a, "layer", [(i, i + 1) for i in range(0, layers, 2)])

    def after(value, *earlier):
        return lax.optimization_barrier((value, *earlier))[0]

    tokens = layer_inputs[0]
    size = tokens.shape[0]
    near = exchange(tokens, "feat", 1)
    far = [exchange(tokens, "feat", s) for s in range(2, shards, 2)]
    three = exchange(near, "feat", 2)

    a0, a0a, a0b, encoder_kept = encode(
        [tokens, near],
        [(0, 0, size), (1, 0, size)],
        [(0, 2 * size), (0, size), (size, size)],
        encoder,
        encoder_bias,
        [],
        stream=True,
    )
    d0a, d0b, n0 = up(a0a), up(a0b), beside(a0)
    rest = exchange(after(jnp.concatenate(far[1:], axis=0), far[0], three), "feat", 1)
    (a1,) = encode(
        [far[0], three],
        [(0, 0, size), (1, 0, size)],
        [(0, 2 * size)],
        encoder_kept,
        encoder_bias,
        [a0],
    )
    d1, n1 = up(a1), beside(a1)
    others = shards - 4
    order = []
    for k in range(others // 2):
        order += [(k, 0, size), (others // 2, k * size, size)]
    a2, a2a, a2b = encode(
        far[1:] + [rest],
        order,
        [(0, others * size), (0, (others - 2) * size), ((others - 2) * size, 2 * size)],
        encoder_kept,
        encoder_bias,
        [a1, d0a],
    )
    d2, d3, n2 = up(a2a), up(a2b), beside(after(a2, d0b))

    c0a, c0b = across(after(d0a, n2)), across(after(d0b, n2))
    mine, sent, base, *kept = decode_first(
        info, [a0, a1, a2], [n0, n1, n2], [d0a, d0b], [c0a, c0b], decoder, shards, []
    )
    slots = [[0, 1], [2, 3], list(range(4, shards - 2)), [shards - 2, shards - 1]]

    def meet(mine, sent, *earlier):
        theirs = [exchange(array, "feat", 1) for array in sent]
        return add_pair(info, mine, theirs, size, list(earlier))

    def spread(blocks, sums):
        parts = [part if q == 0 else exchange(part, "feat", 2 * q) for q, part in enumerate(sums)]
        return [(2 * q, blocks) for q in range(len(parts))], parts

    def later(number, direct, swapped, *earlier):
        row = (slots[number][0] - slots[1][0]) * size
        order = [(0, 0, len(slots[number]) * size)]
        return decode_later(info, [direct], [swapped], order, base, kept, row, shards, list(earlier))

    c1, c2 = across(after(d1, sent)), across(after(d2, sent))
    mine1, sent1 = later(1, d1, c1, sent, d2, c2)
    mine2, sent2 = later(2, d2, c2, sent1)
    met1 = meet([mine, mine1], [sent, sent1], sent2)
    where1, parts1 = spread(slots[0] + slots[1], met1)
    c3 = across(after(d3, met1[0]))
    mine3, sent3 = later(3, d3, c3, sent2, *parts1)
    met2 = meet([mine2], [sent2], sent3)
    where2, parts2 = spread(slots[2], met2)
    met3 = meet([mine3], [sent3], parts2[1])
    where3, parts3 = spread(slots[3], met3)
    where, parts = where1 + where2 + where3, parts1 + parts2 + parts3
    return add_up(info, targets[0], -1.0, where, parts, [])[None]


def grouped(layer_inputs, targets, encoder, encoder_bias, decoder):
    groups = lax.axis_size("layer") // L_WIN
    depth_bits = groups.bit_length() - 1
    position = lax.axis_index("layer")
    target_layer = position // groups
    group_index = position % groups
    gathered = lax.all_gather(layer_inputs[0], "feat", axis=0, tiled=True)
    for bit_index in range(depth_bits):
        partner = exchange(gathered, "layer", 1 << bit_index)
        upper_bit = position >> bit_index & 1
        gathered = jnp.where(
            upper_bit == 1,
            jnp.concatenate([partner, gathered], 0),
            jnp.concatenate([gathered, partner], 0),
        )
    preact = (
        jnp.dot(gathered, encoder[0], preferred_element_type=jnp.float32) + encoder_bias[0][None, :]
    )
    features = jax.nn.relu(preact).astype(jnp.bfloat16)
    tok_count = features.shape[0]
    every_layer = lax.all_gather(features[None], "layer", axis=0, tiled=True)
    by_layer = every_layer.reshape(L_WIN, groups, tok_count, features.shape[1])
    mine_only = lax.dynamic_index_in_dim(by_layer, group_index, 1, keepdims=False)
    flipped = mine_only[::-1]
    padded = jnp.concatenate([flipped, jnp.zeros_like(flipped)], 0)
    stacked = lax.dynamic_slice_in_dim(padded, L_WIN - 1 - target_layer, L_WIN, 0)
    rebuilt = jnp.einsum("ktf,kfd->td", stacked, decoder[0], preferred_element_type=jnp.float32)
    for bit_index in reversed(range(depth_bits)):
        half_rows = rebuilt.shape[0] // 2
        upper_bit = position >> bit_index & 1
        kept_half = jnp.where(upper_bit == 1, rebuilt[half_rows:], rebuilt[:half_rows])
        sent_half = jnp.where(upper_bit == 1, rebuilt[:half_rows], rebuilt[half_rows:])
        rebuilt = kept_half + exchange(sent_half, "layer", 1 << bit_index)
    summed = lax.psum_scatter(rebuilt, "feat", scatter_dimension=1, tiled=True)
    residual = summed - targets[0]
    return residual[None]


def solution(mesh):
    placed = (
        P("layer", "feat", None),
        P("layer", None, "feat"),
        P("layer", None, "feat"),
        P("layer", "feat"),
        P("layer", None, "feat", None),
    )
    shards = mesh.shape["feat"]
    simple = mesh.shape["layer"] == L_WIN and shards >= 8 and shards & (shards - 1) == 0
    return jax.shard_map(
        pipelined if simple else grouped,
        mesh=mesh,
        in_specs=placed,
        out_specs=P("layer", None, "feat"),
        check_vma=False,
    )
```

```python
import functools

import jax
import jax.numpy as jnp
from jax import lax
from jax.experimental import pallas as pl
from jax.experimental.pallas import tpu as pltpu
from jax.sharding import PartitionSpec as P

L_WIN = 4
MIB = 1024 * 1024


def exchange(array, axis, flip):
    size = lax.axis_size(axis)
    return lax.ppermute(array, axis, [(i, i ^ flip) for i in range(size)])


ANYWHERE = pl.BlockSpec(memory_space=pl.ANY)
WHOLE = pl.BlockSpec(memory_space=pltpu.VMEM)
SLOTS = 3
ENCODE_MIB = 16
DECODE_MIB = 26
SUM_MIB = 12


def landed(array):
    return pltpu.with_memory_space_constraint(array, pltpu.VMEM)


def fill(order, parts, rows_of):
    at = 0
    for part, row, size in order:
        rows_of[pl.ds(at, size), :] = parts[part][pl.ds(row, size), :]
        at += size


def encode_kernel(order, pieces, n_in, n_after, stream, *refs):
    parts, weight, bias, refs = refs[:n_in], refs[n_in], refs[n_in + 1], refs[n_in + 2 + n_after :]
    outs, refs = refs[: len(pieces)], refs[len(pieces) :]
    features = weight.shape[2]
    if stream:
        kept, tokens, sems = refs
        block = features // sems.shape[0]
    else:
        kept, (tokens,) = weight, refs
        block = min(512, features)

    def fetch(j):
        cols = pl.ds(pl.multiple_of(j * block, block), block)
        return pltpu.make_async_copy(weight.at[0, :, cols], kept.at[0, :, cols], sems.at[j])

    if stream:
        for j in range(features // block):
            fetch(jnp.int32(j)).start()
    fill(order, parts, tokens)

    @pl.loop(0, features // block)
    def _(j):
        if stream:
            fetch(j).wait()
        cols = pl.ds(pl.multiple_of(j * block, block), block)
        preact = jnp.dot(tokens[...], kept[0, :, cols], preferred_element_type=jnp.float32)
        acts = jnp.maximum(preact + bias[:, cols], 0.0).astype(jnp.bfloat16)
        for out, (row, size) in zip(outs, pieces):
            out[:, cols] = acts[row : row + size]


def encode(parts, order, pieces, weight, bias, after, stream=False):
    rows = sum(size for _, _, size in order)
    _, width, features = weight.shape
    out_shape = [jax.ShapeDtypeStruct((size, features), jnp.bfloat16) for _, size in pieces]
    scratch = [pltpu.VMEM((rows, width), jnp.bfloat16)]
    if stream:
        out_shape.append(pltpu.VMEM(weight.shape, weight.dtype))
        scratch.append(pltpu.SemaphoreType.DMA((max(1, features // 512),)))
        weight = pltpu.with_memory_space_constraint(weight, pltpu.HBM)
    else:
        weight = pltpu.with_memory_space_constraint(weight, pltpu.VMEM)
    return pl.pallas_call(
        functools.partial(encode_kernel, order, pieces, len(parts), len(after), stream),
        in_specs=[WHOLE] * len(parts) + [ANYWHERE if stream else WHOLE, WHOLE] + [ANYWHERE] * len(after),
        out_specs=[WHOLE] * len(out_shape),
        out_shape=out_shape,
        scratch_shapes=scratch,
        compiler_params=pltpu.CompilerParams(vmem_limit_bytes=ENCODE_MIB * MIB),
        name="encode",
    )(*parts, weight, bias, *after)


def split(info, value, out, sent, j):
    cols = out.shape[2]
    low, high = value[:, :cols], value[:, cols:]

    @pl.when(info[4] == 0)
    def _():
        out[j] = low
        sent[j] = high.astype(sent.dtype)

    @pl.when(info[4] == 1)
    def _():
        out[j] = high
        sent[j] = low.astype(sent.dtype)


def halves(shards, rows, width):
    shape = (shards // 2, rows, width // shards)
    return [jax.ShapeDtypeStruct(shape, jnp.float32), jax.ShapeDtypeStruct(shape, jnp.bfloat16)]


def first_wave_kernel(counts, info, *refs):
    groups = []
    for count in counts:
        groups.append(refs[:count])
        refs = refs[count:]
    mine, theirs, direct, swapped = groups
    weights, out, sent, base, *kept = refs[:6]
    total, rings, ring_sems, kept_sems, base_sem = refs[-5:]
    step, steps = pl.program_id(0), pl.num_programs(0)
    slots, block = rings.shape[0], rings.shape[1] // 2
    odd, upper = info[0] == 1, info[1] == 1

    def rows(k):
        return pl.ds(pl.multiple_of(k * block, block), block)

    def fetch(source, k):
        slot = lax.rem(k, slots)
        return pltpu.make_async_copy(
            weights.at[0, source, rows(k)],
            rings.at[slot, pl.ds(source * block, block)],
            ring_sems.at[source, slot],
        )

    def keep(source, k):
        return pltpu.make_async_copy(
            weights.at[0, info[2 + source], rows(k)],
            kept[source].at[rows(k)],
            kept_sems.at[source, k],
        )

    def fetch_all(k):
        fetch(0, k).start()
        pl.when(odd)(lambda: fetch(1, k).start())

        @pl.when(upper)
        def _():
            keep(0, k).start()
            keep(1, k).start()

    @pl.when(step == 0)
    def _():
        for k in range(slots - 1):
            fetch_all(jnp.int32(k))
        total[...] = jnp.zeros_like(total)

    pl.when(step + slots - 1 < steps)(lambda: fetch_all(step + slots - 1))

    def stacked(parts):
        values = [part[...] for part in parts]
        return values[0] if len(values) == 1 else jnp.concatenate(values, axis=0)

    def product(parts, weight):
        return jnp.dot(stacked(parts), weight, preferred_element_type=jnp.float32)

    slot = lax.rem(step, slots)
    fetch(0, step).wait()

    @pl.when(jnp.logical_not(odd))
    def _():
        total[...] += product(mine, rings[slot, pl.ds(0, block), :])

    @pl.when(odd)
    def _():
        fetch(1, step).wait()
        both = jnp.concatenate([stacked(mine), stacked(theirs)], axis=1)
        total[...] += jnp.dot(both, rings[slot], preferred_element_type=jnp.float32)

    done = out.shape[1]

    @pl.when(upper)
    def _():
        keep(0, step).wait()
        keep(1, step).wait()
        total[:done, :] += product(direct, kept[0][rows(step), :]) + product(
            swapped, kept[1][rows(step), :]
        )

    @pl.when(step == steps - 1)
    def _():
        rest = pl.ds(done, total.shape[0] - done)
        copy = pltpu.make_async_copy(total.at[rest], base, base_sem)
        copy.start()
        cols = out.shape[2]
        for j in range(out.shape[0]):
            split(info, total[:done, 2 * j * cols : 2 * (j + 1) * cols], out, sent, j)
        copy.wait()


def decode_first(info, mine, theirs, direct, swapped, decoder, shards, after):
    _, _, features, width = decoder.shape
    block = min(512, features)
    steps = features // block
    rows = sum(part.shape[0] for part in mine)
    done = sum(part.shape[0] for part in direct)

    def acts(part, flag):
        return pl.BlockSpec(
            (part.shape[0], block), lambda k, info: (0, k if flag is None else k * info[flag])
        )

    groups = (mine, theirs, direct, swapped)
    in_specs = [acts(p, flag) for parts, flag in zip(groups, (None, 0, 1, 1)) for p in parts]
    return pl.pallas_call(
        functools.partial(first_wave_kernel, [len(parts) for parts in groups]),
        grid_spec=pltpu.PrefetchScalarGridSpec(
            num_scalar_prefetch=1,
            grid=(steps,),
            in_specs=in_specs + [ANYWHERE] * (1 + len(after)),
            out_specs=[
                *[pl.BlockSpec(h.shape, lambda k, info: (0, 0, 0)) for h in halves(shards, done, width)],
                ANYWHERE,
                WHOLE,
                WHOLE,
            ],
            scratch_shapes=[
                pltpu.VMEM((rows, width), jnp.float32),
                pltpu.VMEM((SLOTS, 2 * block, width), decoder.dtype),
                pltpu.SemaphoreType.DMA((2, SLOTS)),
                pltpu.SemaphoreType.DMA((2, steps)),
                pltpu.SemaphoreType.DMA,
            ],
        ),
        out_shape=[
            *halves(shards, done, width),
            pltpu.HBM((rows - done, width), jnp.float32),
            pltpu.VMEM((features, width), decoder.dtype),
            pltpu.VMEM((features, width), decoder.dtype),
        ],
        compiler_params=pltpu.CompilerParams(vmem_limit_bytes=DECODE_MIB * MIB),
        name="decode_first",
    )(info, *sum(groups, []), decoder, *after)


def later_wave_kernel(order, row, n, info, *refs):
    direct, swapped, (base, *kept) = refs[:n], refs[n : 2 * n], refs[2 * n : 2 * n + 3]
    out, sent, first, second, start, sem = refs[-6:]
    rows = out.shape[1]
    pairs, cols = out.shape[0], out.shape[2]
    copy = pltpu.make_async_copy(base.at[pl.ds(row, rows)], start, sem)
    copy.start()
    fill(order, direct, first)
    fill(order, swapped, second)
    copy.wait()

    @pl.loop(0, pairs)
    def _(j):
        at = pl.ds(pl.multiple_of(j * 2 * cols, 2 * cols), 2 * cols)

        @pl.when(info[1] == 1)
        def _():
            start[:, at] += jnp.dot(
                first[...], kept[0][:, at], preferred_element_type=jnp.float32
            ) + jnp.dot(second[...], kept[1][:, at], preferred_element_type=jnp.float32)

        split(info, start[:, at], out, sent, j)


def decode_later(info, direct, swapped, order, base, kept, row, shards, after):
    rows = sum(size for _, _, size in order)
    features, width = kept[0].shape
    return pl.pallas_call(
        functools.partial(later_wave_kernel, order, row, len(direct)),
        in_specs=[pl.BlockSpec(memory_space=pltpu.SMEM)]
        + [WHOLE] * (2 * len(direct))
        + [ANYWHERE, WHOLE, WHOLE]
        + [ANYWHERE] * len(after),
        out_specs=[WHOLE, WHOLE],
        out_shape=halves(shards, rows, width),
        scratch_shapes=[
            pltpu.VMEM((rows, features), jnp.bfloat16),
            pltpu.VMEM((rows, features), jnp.bfloat16),
            pltpu.VMEM((rows, width), jnp.float32),
            pltpu.SemaphoreType.DMA,
        ],
        compiler_params=pltpu.CompilerParams(vmem_limit_bytes=DECODE_MIB * MIB),
        name="decode_later",
    )(info, *map(landed, direct), *map(landed, swapped), base, *map(landed, kept), *after)


def pair_kernel(size, n, n_after, info, *refs):
    mine, theirs, outs = refs[:n], refs[n : 2 * n], refs[2 * n + n_after :]
    z = info[5]
    for q, out in enumerate(outs):
        row = 0
        for kept, met in zip(mine, theirs):
            rows = kept.shape[1]
            for at in range(0, rows, size):
                partner = at // size ^ 1
                total = kept[z ^ q, pl.ds(at, size), :] + met[
                    z ^ q, pl.ds(partner * size, size), :
                ].astype(jnp.float32)
                out[pl.ds(row + at, size), :] = total.astype(out.dtype)
            row += rows


def add_pair(info, mine, theirs, size, after):
    count, _, cols = mine[0].shape
    rows = sum(kept.shape[1] for kept in mine)
    return pl.pallas_call(
        functools.partial(pair_kernel, size, len(mine), len(after)),
        in_specs=[pl.BlockSpec(memory_space=pltpu.SMEM)]
        + [WHOLE] * (2 * len(mine))
        + [ANYWHERE] * len(after),
        out_specs=[WHOLE] * count,
        out_shape=[
            jax.ShapeDtypeStruct((rows, cols), jnp.float32 if q == 0 else jnp.bfloat16)
            for q in range(count)
        ],
        compiler_params=pltpu.CompilerParams(vmem_limit_bytes=SUM_MIB * MIB),
        name="add_pair",
    )(info, *mine, *[landed(array) for array in theirs], *after)


def sum_kernel(sign, pieces, info, base, *refs):
    received, out = refs[: len(pieces)], refs[-1]
    me = info[6]
    out[...] = sign * base[...]
    for ref, (source, blocks) in zip(received, pieces):
        size = ref.shape[0] // len(blocks)
        for k, s in enumerate(blocks):
            at = pl.ds(pl.multiple_of((me ^ (source ^ s)) * size, size), size)
            out[at, :] += ref[pl.ds(k * size, size), :].astype(jnp.float32)


def add_up(info, base, sign, pieces, received, after):
    return pl.pallas_call(
        functools.partial(sum_kernel, sign, pieces),
        in_specs=[pl.BlockSpec(memory_space=pltpu.SMEM)]
        + [WHOLE] * (1 + len(received))
        + [ANYWHERE] * len(after),
        out_specs=WHOLE,
        out_shape=jax.ShapeDtypeStruct(base.shape, base.dtype),
        compiler_params=pltpu.CompilerParams(vmem_limit_bytes=SUM_MIB * MIB),
        name="add_up",
    )(info, base, *map(landed, received), *after)


def pipelined(layer_inputs, targets, encoder, encoder_bias, decoder):
    shards = lax.axis_size("feat")
    layers = lax.axis_size("layer")
    half = layers // 2
    layer = lax.axis_index("layer")
    feat = lax.axis_index("feat")
    upper = layer >= half
    info = jnp.stack(
        [
            layer & 1,
            upper.astype(jnp.int32),
            jnp.full_like(layer, half),
            jnp.where(upper, layer - ((layer ^ 1) - half), 0),
            feat & 1,
            feat >> 1,
            feat,
        ]
    ).astype(jnp.int32)

    def up(a):
        return lax.ppermute(a, "layer", [(i, i + half) for i in range(half)])

    def across(a):
        return lax.ppermute(a, "layer", [(i, i ^ 1) for i in range(half, layers)])

    def beside(a):
        return lax.ppermute(a, "layer", [(i, i + 1) for i in range(0, layers, 2)])

    def after(value, *earlier):
        return lax.optimization_barrier((value, *earlier))[0]

    tokens = layer_inputs[0]
    size = tokens.shape[0]
    near = exchange(tokens, "feat", 1)
    far = [exchange(tokens, "feat", s) for s in range(2, shards, 2)]
    three = exchange(near, "feat", 2)

    a0, a0a, a0b, encoder_kept = encode(
        [tokens, near],
        [(0, 0, size), (1, 0, size)],
        [(0, 2 * size), (0, size), (size, size)],
        encoder,
        encoder_bias,
        [],
        stream=True,
    )
    d0a, d0b, n0 = up(a0a), up(a0b), beside(a0)
    rest = exchange(after(jnp.concatenate(far[1:], axis=0), far[0], three), "feat", 1)
    (a1,) = encode(
        [far[0], three],
        [(0, 0, size), (1, 0, size)],
        [(0, 2 * size)],
        encoder_kept,
        encoder_bias,
        [a0],
    )
    d1, n1 = up(a1), beside(a1)
    others = shards - 4
    order = []
    for k in range(others // 2):
        order += [(k, 0, size), (others // 2, k * size, size)]
    (a2,) = encode(
        far[1:] + [rest],
        order,
        [(0, others * size)],
        encoder_kept,
        encoder_bias,
        [a1, d0a],
    )
    d2, n2 = up(a2), beside(after(a2, d0b))

    c0a, c0b = across(after(d0a, n2)), across(after(d0b, n2))
    mine, sent, base, *kept = decode_first(
        info, [a0, a1, a2], [n0, n1, n2], [d0a, d0b], [c0a, c0b], decoder, shards, []
    )
    slots = [[0, 1], [2, 3], list(range(4, shards - 2)), [shards - 2, shards - 1]]

    def meet(mine, sent, *earlier):
        theirs = [exchange(array, "feat", 1) for array in sent]
        return add_pair(info, mine, theirs, size, list(earlier))

    def spread(blocks, sums):
        parts = [part if q == 0 else exchange(part, "feat", 2 * q) for q, part in enumerate(sums)]
        return [(2 * q, blocks) for q in range(len(parts))], parts

    def later(number, direct, swapped, skip, *earlier):
        row = (slots[number][0] - slots[1][0]) * size
        order = [(0, skip * size, len(slots[number]) * size)]
        return decode_later(info, [direct], [swapped], order, base, kept, row, shards, list(earlier))

    c1 = across(after(d1, sent))
    mine1, sent1 = later(1, d1, c1, 0, sent)
    met1 = meet([mine, mine1], [sent, sent1])
    where1, parts1 = spread(slots[0] + slots[1], met1)
    c2 = across(after(d2, met1[0]))
    mine2, sent2 = later(2, d2, c2, 0, met1[0])
    total = add_up(info, targets[0], -1.0, where1, parts1, [sent2])
    mine3, sent3 = later(3, d2, c2, others - 2, sent2, total)
    met2 = meet([mine2], [sent2], sent3)
    where2, parts2 = spread(slots[2], met2)
    met3 = meet([mine3], [sent3], parts2[1])
    where3, parts3 = spread(slots[3], met3)
    return add_up(info, total, 1.0, where2 + where3, parts2 + parts3, [])[None]


def grouped(layer_inputs, targets, encoder, encoder_bias, decoder):
    groups = lax.axis_size("layer") // L_WIN
    depth_bits = groups.bit_length() - 1
    position = lax.axis_index("layer")
    target_layer = position // groups
    group_index = position % groups
    gathered = lax.all_gather(layer_inputs[0], "feat", axis=0, tiled=True)
    for bit_index in range(depth_bits):
        partner = exchange(gathered, "layer", 1 << bit_index)
        upper_bit = position >> bit_index & 1
        gathered = jnp.where(
            upper_bit == 1,
            jnp.concatenate([partner, gathered], 0),
            jnp.concatenate([gathered, partner], 0),
        )
    preact = (
        jnp.dot(gathered, encoder[0], preferred_element_type=jnp.float32) + encoder_bias[0][None, :]
    )
    features = jax.nn.relu(preact).astype(jnp.bfloat16)
    tok_count = features.shape[0]
    every_layer = lax.all_gather(features[None], "layer", axis=0, tiled=True)
    by_layer = every_layer.reshape(L_WIN, groups, tok_count, features.shape[1])
    mine_only = lax.dynamic_index_in_dim(by_layer, group_index, 1, keepdims=False)
    flipped = mine_only[::-1]
    padded = jnp.concatenate([flipped, jnp.zeros_like(flipped)], 0)
    stacked = lax.dynamic_slice_in_dim(padded, L_WIN - 1 - target_layer, L_WIN, 0)
    rebuilt = jnp.einsum("ktf,kfd->td", stacked, decoder[0], preferred_element_type=jnp.float32)
    for bit_index in reversed(range(depth_bits)):
        half_rows = rebuilt.shape[0] // 2
        upper_bit = position >> bit_index & 1
        kept_half = jnp.where(upper_bit == 1, rebuilt[half_rows:], rebuilt[:half_rows])
        sent_half = jnp.where(upper_bit == 1, rebuilt[:half_rows], rebuilt[half_rows:])
        rebuilt = kept_half + exchange(sent_half, "layer", 1 << bit_index)
    summed = lax.psum_scatter(rebuilt, "feat", scatter_dimension=1, tiled=True)
    residual = summed - targets[0]
    return residual[None]


def solution(mesh):
    placed = (
        P("layer", "feat", None),
        P("layer", None, "feat"),
        P("layer", None, "feat"),
        P("layer", "feat"),
        P("layer", None, "feat", None),
    )
    shards = mesh.shape["feat"]
    simple = mesh.shape["layer"] == L_WIN and shards >= 8 and shards & (shards - 1) == 0
    return jax.shard_map(
        pipelined if simple else grouped,
        mesh=mesh,
        in_specs=placed,
        out_specs=P("layer", None, "feat"),
        check_vma=False,
    )
```

```python
import functools

import jax
import jax.numpy as jnp
from jax import lax
from jax.experimental import pallas as pl
from jax.experimental.pallas import tpu as pltpu
from jax.sharding import PartitionSpec as P

L_WIN = 4
MIB = 1024 * 1024


def exchange(array, axis, flip):
    size = lax.axis_size(axis)
    return lax.ppermute(array, axis, [(i, i ^ flip) for i in range(size)])


ANYWHERE = pl.BlockSpec(memory_space=pl.ANY)
WHOLE = pl.BlockSpec(memory_space=pltpu.VMEM)
SLOTS = 3
ENCODE_MIB = 16
DECODE_MIB = 26
SUM_MIB = 12


def landed(array):
    return pltpu.with_memory_space_constraint(array, pltpu.VMEM)


def fetched(array):
    return pltpu.with_memory_space_constraint(array, pltpu.HBM)


def fill(order, parts, rows_of):
    at = 0
    for part, row, size in order:
        rows_of[pl.ds(at, size), :] = parts[part][pl.ds(row, size), :]
        at += size


def encode_kernel(order, pieces, n_in, n_after, stream, *refs):
    parts, weight, bias, refs = refs[:n_in], refs[n_in], refs[n_in + 1], refs[n_in + 2 + n_after :]
    outs, refs = refs[: len(pieces)], refs[len(pieces) :]
    features = weight.shape[2]
    if stream:
        kept, tokens, sems = refs
        block = features // sems.shape[0]
    else:
        kept, (tokens,) = weight, refs
        block = min(512, features)

    def fetch(j):
        cols = pl.ds(pl.multiple_of(j * block, block), block)
        return pltpu.make_async_copy(weight.at[0, :, cols], kept.at[0, :, cols], sems.at[j])

    if stream:
        for j in range(features // block):
            fetch(jnp.int32(j)).start()
    fill(order, parts, tokens)

    @pl.loop(0, features // block)
    def _(j):
        if stream:
            fetch(j).wait()
        cols = pl.ds(pl.multiple_of(j * block, block), block)
        preact = jnp.dot(tokens[...], kept[0, :, cols], preferred_element_type=jnp.float32)
        acts = jnp.maximum(preact + bias[:, cols], 0.0).astype(jnp.bfloat16)
        for out, (row, size) in zip(outs, pieces):
            out[:, cols] = acts[row : row + size]


def encode(parts, order, pieces, weight, bias, after, stream=False):
    rows = sum(size for _, _, size in order)
    _, width, features = weight.shape
    out_shape = [jax.ShapeDtypeStruct((size, features), jnp.bfloat16) for _, size in pieces]
    scratch = [pltpu.VMEM((rows, width), jnp.bfloat16)]
    if stream:
        out_shape.append(pltpu.VMEM(weight.shape, weight.dtype))
        scratch.append(pltpu.SemaphoreType.DMA((max(1, features // 512),)))
        weight = pltpu.with_memory_space_constraint(weight, pltpu.HBM)
    else:
        weight = pltpu.with_memory_space_constraint(weight, pltpu.VMEM)
    return pl.pallas_call(
        functools.partial(encode_kernel, order, pieces, len(parts), len(after), stream),
        in_specs=[WHOLE] * len(parts) + [ANYWHERE if stream else WHOLE, WHOLE] + [ANYWHERE] * len(after),
        out_specs=[WHOLE] * len(out_shape),
        out_shape=out_shape,
        scratch_shapes=scratch,
        compiler_params=pltpu.CompilerParams(vmem_limit_bytes=ENCODE_MIB * MIB),
        name="encode",
    )(*parts, weight, bias, *after)


def split(info, value, out, sent, j):
    cols = out.shape[2]
    low, high = value[:, :cols], value[:, cols:]

    @pl.when(info[4] == 0)
    def _():
        out[j] = low
        sent[j] = high.astype(sent.dtype)

    @pl.when(info[4] == 1)
    def _():
        out[j] = high
        sent[j] = low.astype(sent.dtype)


def halves(shards, rows, width):
    shape = (shards // 2, rows, width // shards)
    return [jax.ShapeDtypeStruct(shape, jnp.float32), jax.ShapeDtypeStruct(shape, jnp.bfloat16)]


def first_wave_kernel(counts, info, *refs):
    groups = []
    for count in counts:
        groups.append(refs[:count])
        refs = refs[count:]
    mine, theirs, direct, swapped = groups
    weights, out, sent, base, *kept = refs[:6]
    total, rings, ring_sems, kept_sems, base_sem = refs[-5:]
    step, steps = pl.program_id(0), pl.num_programs(0)
    slots, block = rings.shape[0], rings.shape[1] // 2
    odd, upper = info[0] == 1, info[1] == 1

    def rows(k):
        return pl.ds(pl.multiple_of(k * block, block), block)

    def fetch(source, k):
        slot = lax.rem(k, slots)
        return pltpu.make_async_copy(
            weights.at[0, source, rows(k)],
            rings.at[slot, pl.ds(source * block, block)],
            ring_sems.at[source, slot],
        )

    def keep(source, k):
        return pltpu.make_async_copy(
            weights.at[0, info[2 + source], rows(k)],
            kept[source].at[rows(k)],
            kept_sems.at[source, k],
        )

    def fetch_all(k):
        fetch(0, k).start()
        pl.when(odd)(lambda: fetch(1, k).start())

        @pl.when(upper)
        def _():
            keep(0, k).start()
            keep(1, k).start()

    @pl.when(step == 0)
    def _():
        for k in range(slots - 1):
            fetch_all(jnp.int32(k))
        total[...] = jnp.zeros_like(total)

    pl.when(step + slots - 1 < steps)(lambda: fetch_all(step + slots - 1))

    def stacked(parts):
        values = [part[...] for part in parts]
        return values[0] if len(values) == 1 else jnp.concatenate(values, axis=0)

    def product(parts, weight):
        return jnp.dot(stacked(parts), weight, preferred_element_type=jnp.float32)

    slot = lax.rem(step, slots)
    fetch(0, step).wait()

    @pl.when(jnp.logical_not(odd))
    def _():
        total[...] += product(mine, rings[slot, pl.ds(0, block), :])

    @pl.when(odd)
    def _():
        fetch(1, step).wait()
        both = jnp.concatenate([stacked(mine), stacked(theirs)], axis=1)
        total[...] += jnp.dot(both, rings[slot], preferred_element_type=jnp.float32)

    done = out.shape[1]

    @pl.when(upper)
    def _():
        keep(0, step).wait()
        keep(1, step).wait()
        total[:done, :] += product(direct, kept[0][rows(step), :]) + product(
            swapped, kept[1][rows(step), :]
        )

    @pl.when(step == steps - 1)
    def _():
        rest = pl.ds(done, total.shape[0] - done)
        copy = pltpu.make_async_copy(total.at[rest], base, base_sem)
        copy.start()
        cols = out.shape[2]
        for j in range(out.shape[0]):
            split(info, total[:done, 2 * j * cols : 2 * (j + 1) * cols], out, sent, j)
        copy.wait()


def decode_first(info, mine, theirs, direct, swapped, decoder, shards, after):
    _, _, features, width = decoder.shape
    block = min(512, features)
    steps = features // block
    rows = sum(part.shape[0] for part in mine)
    done = sum(part.shape[0] for part in direct)

    def acts(part, flag):
        return pl.BlockSpec(
            (part.shape[0], block), lambda k, info: (0, k if flag is None else k * info[flag])
        )

    groups = (mine, theirs, direct, swapped)
    in_specs = [acts(p, flag) for parts, flag in zip(groups, (None, 0, 1, 1)) for p in parts]
    return pl.pallas_call(
        functools.partial(first_wave_kernel, [len(parts) for parts in groups]),
        grid_spec=pltpu.PrefetchScalarGridSpec(
            num_scalar_prefetch=1,
            grid=(steps,),
            in_specs=in_specs + [ANYWHERE] * (1 + len(after)),
            out_specs=[
                *[pl.BlockSpec(h.shape, lambda k, info: (0, 0, 0)) for h in halves(shards, done, width)],
                ANYWHERE,
                WHOLE,
                WHOLE,
            ],
            scratch_shapes=[
                pltpu.VMEM((rows, width), jnp.float32),
                pltpu.VMEM((SLOTS, 2 * block, width), decoder.dtype),
                pltpu.SemaphoreType.DMA((2, SLOTS)),
                pltpu.SemaphoreType.DMA((2, steps)),
                pltpu.SemaphoreType.DMA,
            ],
        ),
        out_shape=[
            *halves(shards, done, width),
            pltpu.HBM((rows - done, width), jnp.float32),
            pltpu.VMEM((features, width), decoder.dtype),
            pltpu.VMEM((features, width), decoder.dtype),
        ],
        compiler_params=pltpu.CompilerParams(vmem_limit_bytes=DECODE_MIB * MIB),
        name="decode_first",
    )(info, *sum(groups, []), decoder, *after)


def later_wave_kernel(row, skip, info, direct, swapped, base, kept_direct, kept_swapped, *refs):
    kept = kept_direct, kept_swapped
    out, sent, first, second, start, sems = refs[-6:]
    rows = out.shape[1]
    pairs, cols = out.shape[0], out.shape[2]
    copies = [
        pltpu.make_async_copy(direct.at[pl.ds(skip, rows)], first, sems.at[0]),
        pltpu.make_async_copy(swapped.at[pl.ds(skip, rows)], second, sems.at[1]),
        pltpu.make_async_copy(base.at[pl.ds(row, rows)], start, sems.at[2]),
    ]
    for copy in copies:
        copy.start()
    for copy in copies:
        copy.wait()

    @pl.loop(0, pairs)
    def _(j):
        at = pl.ds(pl.multiple_of(j * 2 * cols, 2 * cols), 2 * cols)

        @pl.when(info[1] == 1)
        def _():
            start[:, at] += jnp.dot(
                first[...], kept[0][:, at], preferred_element_type=jnp.float32
            ) + jnp.dot(second[...], kept[1][:, at], preferred_element_type=jnp.float32)

        split(info, start[:, at], out, sent, j)


def decode_later(info, direct, swapped, skip, rows, base, kept, row, shards, after):
    features, width = kept[0].shape
    return pl.pallas_call(
        functools.partial(later_wave_kernel, row, skip),
        in_specs=[pl.BlockSpec(memory_space=pltpu.SMEM)]
        + [ANYWHERE] * 3
        + [WHOLE] * 2
        + [ANYWHERE] * len(after),
        out_specs=[WHOLE, WHOLE],
        out_shape=halves(shards, rows, width),
        scratch_shapes=[
            pltpu.VMEM((rows, features), jnp.bfloat16),
            pltpu.VMEM((rows, features), jnp.bfloat16),
            pltpu.VMEM((rows, width), jnp.float32),
            pltpu.SemaphoreType.DMA((3,)),
        ],
        compiler_params=pltpu.CompilerParams(vmem_limit_bytes=DECODE_MIB * MIB),
        name="decode_later",
    )(info, fetched(direct), landed(swapped), fetched(base), *map(landed, kept), *after)


def pair_kernel(size, n, n_after, info, *refs):
    theirs, outs, sems = refs[n : 2 * n], refs[2 * n + n_after : -1 - n], refs[-1]
    mine = refs[-1 - n : -1]
    copies = [pltpu.make_async_copy(refs[i], mine[i], sems.at[i]) for i in range(n)]
    for copy in copies:
        copy.start()
    for copy in copies:
        copy.wait()
    z = info[5]
    for q, out in enumerate(outs):
        row = 0
        for kept, met in zip(mine, theirs):
            rows = kept.shape[1]
            for at in range(0, rows, size):
                partner = at // size ^ 1
                total = kept[z ^ q, pl.ds(at, size), :] + met[
                    z ^ q, pl.ds(partner * size, size), :
                ].astype(jnp.float32)
                out[pl.ds(row + at, size), :] = total.astype(out.dtype)
            row += rows


def add_pair(info, mine, theirs, size, after):
    count, _, cols = mine[0].shape
    rows = sum(kept.shape[1] for kept in mine)
    return pl.pallas_call(
        functools.partial(pair_kernel, size, len(mine), len(after)),
        in_specs=[pl.BlockSpec(memory_space=pltpu.SMEM)]
        + [ANYWHERE] * len(mine)
        + [WHOLE] * len(theirs)
        + [ANYWHERE] * len(after),
        out_specs=[WHOLE] * count,
        scratch_shapes=[pltpu.VMEM(array.shape, array.dtype) for array in mine]
        + [pltpu.SemaphoreType.DMA((len(mine),))],
        out_shape=[
            jax.ShapeDtypeStruct((rows, cols), jnp.float32 if q == 0 else jnp.bfloat16)
            for q in range(count)
        ],
        compiler_params=pltpu.CompilerParams(vmem_limit_bytes=SUM_MIB * MIB),
        name="add_pair",
    )(info, *map(fetched, mine), *map(landed, theirs), *after)


def sum_kernel(sign, pieces, info, base, *refs):
    received, (out, total, sems) = refs[: len(pieces)], refs[-3:]
    me = info[6]
    copy = pltpu.make_async_copy(base, total, sems.at[0])
    copy.start()
    copy.wait()
    if sign != 1.0:
        total[...] = sign * total[...]
    for ref, (source, blocks) in zip(received, pieces):
        size = ref.shape[0] // len(blocks)
        for k, s in enumerate(blocks):
            at = pl.ds(pl.multiple_of((me ^ (source ^ s)) * size, size), size)
            total[at, :] += ref[pl.ds(k * size, size), :].astype(jnp.float32)
    copy = pltpu.make_async_copy(total, out, sems.at[1])
    copy.start()
    copy.wait()


def add_up(info, base, sign, pieces, received, after):
    return pl.pallas_call(
        functools.partial(sum_kernel, sign, pieces),
        in_specs=[pl.BlockSpec(memory_space=pltpu.SMEM)]
        + [ANYWHERE]
        + [WHOLE] * len(received)
        + [ANYWHERE] * len(after),
        out_specs=ANYWHERE,
        out_shape=pltpu.HBM(base.shape, base.dtype),
        scratch_shapes=[pltpu.VMEM(base.shape, base.dtype), pltpu.SemaphoreType.DMA((2,))],
        compiler_params=pltpu.CompilerParams(vmem_limit_bytes=SUM_MIB * MIB),
        name="add_up",
    )(info, fetched(base), *map(landed, received), *after)


def pipelined(layer_inputs, targets, encoder, encoder_bias, decoder):
    shards = lax.axis_size("feat")
    layers = lax.axis_size("layer")
    half = layers // 2
    layer = lax.axis_index("layer")
    feat = lax.axis_index("feat")
    upper = layer >= half
    info = jnp.stack(
        [
            layer & 1,
            upper.astype(jnp.int32),
            jnp.full_like(layer, half),
            jnp.where(upper, layer - ((layer ^ 1) - half), 0),
            feat & 1,
            feat >> 1,
            feat,
        ]
    ).astype(jnp.int32)

    def up(a):
        return lax.ppermute(a, "layer", [(i, i + half) for i in range(half)])

    def across(a):
        return lax.ppermute(a, "layer", [(i, i ^ 1) for i in range(half, layers)])

    def beside(a):
        return lax.ppermute(a, "layer", [(i, i + 1) for i in range(0, layers, 2)])

    def after(value, *earlier):
        return lax.optimization_barrier((value, *earlier))[0]

    tokens = layer_inputs[0]
    size = tokens.shape[0]
    near = exchange(tokens, "feat", 1)
    far = [exchange(tokens, "feat", s) for s in range(2, shards, 2)]
    three = exchange(near, "feat", 2)

    a0, a0a, a0b, encoder_kept = encode(
        [tokens, near],
        [(0, 0, size), (1, 0, size)],
        [(0, 2 * size), (0, size), (size, size)],
        encoder,
        encoder_bias,
        [],
        stream=True,
    )
    d0a, d0b, n0 = up(a0a), up(a0b), beside(a0)
    rest = exchange(after(jnp.concatenate(far[1:], axis=0), far[0], three), "feat", 1)
    (a1,) = encode(
        [far[0], three],
        [(0, 0, size), (1, 0, size)],
        [(0, 2 * size)],
        encoder_kept,
        encoder_bias,
        [a0],
    )
    d1, n1 = up(a1), beside(a1)
    others = shards - 4
    order = []
    for k in range(others // 2):
        order += [(k, 0, size), (others // 2, k * size, size)]
    (a2,) = encode(
        far[1:] + [rest],
        order,
        [(0, others * size)],
        encoder_kept,
        encoder_bias,
        [a1, d0a],
    )
    d2, n2 = up(a2), beside(after(a2, d0b))

    c0a, c0b = across(after(d0a, n2)), across(after(d0b, n2))
    mine, sent, base, *kept = decode_first(
        info, [a0, a1, a2], [n0, n1, n2], [d0a, d0b], [c0a, c0b], decoder, shards, []
    )
    slots = [[0, 1], [2, 3], list(range(4, shards - 2)), [shards - 2, shards - 1]]

    def meet(mine, sent, *earlier):
        theirs = [exchange(array, "feat", 1) for array in sent]
        return add_pair(info, mine, theirs, size, list(earlier))

    def spread(blocks, sums):
        parts = [part if q == 0 else exchange(part, "feat", 2 * q) for q, part in enumerate(sums)]
        return [(2 * q, blocks) for q in range(len(parts))], parts

    def later(number, direct, swapped, skip, *earlier):
        row = (slots[number][0] - slots[1][0]) * size
        rows = len(slots[number]) * size
        return decode_later(
            info, direct, swapped, skip * size, rows, base, kept, row, shards, list(earlier)
        )

    c1 = across(after(d1, sent))
    mine1, sent1 = later(1, d1, c1, 0, sent)
    met1 = meet([mine, mine1], [sent, sent1])
    where1, parts1 = spread(slots[0] + slots[1], met1)
    c2 = across(after(d2, met1[0]))
    mine2, sent2 = later(2, d2, c2, 0, met1[0])
    total = add_up(info, targets[0], -1.0, where1, parts1, [sent2])
    mine3, sent3 = later(3, d2, c2, others - 2, sent2, total)
    met2 = meet([mine2], [sent2], sent3)
    where2, parts2 = spread(slots[2], met2)
    met3 = meet([mine3], [sent3], parts2[1])
    where3, parts3 = spread(slots[3], met3)
    return add_up(info, total, 1.0, where2 + where3, parts2 + parts3, [])[None]


def grouped(layer_inputs, targets, encoder, encoder_bias, decoder):
    groups = lax.axis_size("layer") // L_WIN
    depth_bits = groups.bit_length() - 1
    position = lax.axis_index("layer")
    target_layer = position // groups
    group_index = position % groups
    gathered = lax.all_gather(layer_inputs[0], "feat", axis=0, tiled=True)
    for bit_index in range(depth_bits):
        partner = exchange(gathered, "layer", 1 << bit_index)
        upper_bit = position >> bit_index & 1
        gathered = jnp.where(
            upper_bit == 1,
            jnp.concatenate([partner, gathered], 0),
            jnp.concatenate([gathered, partner], 0),
        )
    preact = (
        jnp.dot(gathered, encoder[0], preferred_element_type=jnp.float32) + encoder_bias[0][None, :]
    )
    features = jax.nn.relu(preact).astype(jnp.bfloat16)
    tok_count = features.shape[0]
    every_layer = lax.all_gather(features[None], "layer", axis=0, tiled=True)
    by_layer = every_layer.reshape(L_WIN, groups, tok_count, features.shape[1])
    mine_only = lax.dynamic_index_in_dim(by_layer, group_index, 1, keepdims=False)
    flipped = mine_only[::-1]
    padded = jnp.concatenate([flipped, jnp.zeros_like(flipped)], 0)
    stacked = lax.dynamic_slice_in_dim(padded, L_WIN - 1 - target_layer, L_WIN, 0)
    rebuilt = jnp.einsum("ktf,kfd->td", stacked, decoder[0], preferred_element_type=jnp.float32)
    for bit_index in reversed(range(depth_bits)):
        half_rows = rebuilt.shape[0] // 2
        upper_bit = position >> bit_index & 1
        kept_half = jnp.where(upper_bit == 1, rebuilt[half_rows:], rebuilt[:half_rows])
        sent_half = jnp.where(upper_bit == 1, rebuilt[:half_rows], rebuilt[half_rows:])
        rebuilt = kept_half + exchange(sent_half, "layer", 1 << bit_index)
    summed = lax.psum_scatter(rebuilt, "feat", scatter_dimension=1, tiled=True)
    residual = summed - targets[0]
    return residual[None]


def solution(mesh):
    placed = (
        P("layer", "feat", None),
        P("layer", None, "feat"),
        P("layer", None, "feat"),
        P("layer", "feat"),
        P("layer", None, "feat", None),
    )
    shards = mesh.shape["feat"]
    simple = mesh.shape["layer"] == L_WIN and shards >= 8 and shards & (shards - 1) == 0
    return jax.shard_map(
        pipelined if simple else grouped,
        mesh=mesh,
        in_specs=placed,
        out_specs=P("layer", None, "feat"),
        check_vma=False,
    )
```

```python
import functools

import jax
import jax.numpy as jnp
from jax import lax
from jax.experimental import pallas as pl
from jax.experimental.pallas import tpu as pltpu
from jax.sharding import PartitionSpec as P

L_WIN = 4
MIB = 1024 * 1024


def exchange(array, axis, flip):
    size = lax.axis_size(axis)
    return lax.ppermute(array, axis, [(i, i ^ flip) for i in range(size)])


ANYWHERE = pl.BlockSpec(memory_space=pl.ANY)
WHOLE = pl.BlockSpec(memory_space=pltpu.VMEM)
SLOTS = 3
ENCODE_MIB = 16
DECODE_MIB = 26
SUM_MIB = 12


def landed(array):
    return pltpu.with_memory_space_constraint(array, pltpu.VMEM)


def fetched(array):
    return pltpu.with_memory_space_constraint(array, pltpu.HBM)


def fill(order, parts, rows_of):
    at = 0
    for part, row, size in order:
        rows_of[pl.ds(at, size), :] = parts[part][pl.ds(row, size), :]
        at += size


def encode_kernel(order, pieces, n_in, n_after, stream, *refs):
    parts, weight, bias, refs = refs[:n_in], refs[n_in], refs[n_in + 1], refs[n_in + 2 :]
    earlier, refs = refs[:n_after], refs[n_after:]
    outs, refs = refs[: len(pieces)], refs[len(pieces) :]
    features = weight.shape[2]
    if stream:
        kept, tokens, sems = refs
        block = features // sems.shape[0]
    else:
        kept, (tokens,) = weight, refs
        block = min(512, features)

    def fetch(j):
        cols = pl.ds(pl.multiple_of(j * block, block), block)
        return pltpu.make_async_copy(weight.at[0, :, cols], kept.at[0, :, cols], sems.at[j])

    if stream:
        for j in range(features // block):
            fetch(jnp.int32(j)).start()
    fill(order, parts, tokens)

    @pl.loop(0, features // block)
    def _(j):
        if stream:
            fetch(j).wait()
        cols = pl.ds(pl.multiple_of(j * block, block), block)
        preact = jnp.dot(tokens[...], kept[0, :, cols], preferred_element_type=jnp.float32)
        acts = jnp.maximum(preact + bias[:, cols], 0.0).astype(jnp.bfloat16)
        for out, (row, size) in zip(outs, pieces):
            before = out.shape[0] - size
            out[pl.ds(before, size), cols] = acts[row : row + size]
            if before:
                out[pl.ds(0, before), cols] = earlier[0][:, cols]


def encode(parts, order, pieces, weight, bias, after, stream=False, join=False):
    rows = sum(size for _, _, size in order)
    _, width, features = weight.shape
    out_shape = [jax.ShapeDtypeStruct((size, features), jnp.bfloat16) for _, size in pieces]
    if join:
        joined = (after[0].shape[0] + pieces[0][1], features)
        out_shape[0] = jax.ShapeDtypeStruct(joined, jnp.bfloat16)
    scratch = [pltpu.VMEM((rows, width), jnp.bfloat16)]
    if stream:
        out_shape.append(pltpu.VMEM(weight.shape, weight.dtype))
        scratch.append(pltpu.SemaphoreType.DMA((max(1, features // 512),)))
        weight = pltpu.with_memory_space_constraint(weight, pltpu.HBM)
    else:
        weight = pltpu.with_memory_space_constraint(weight, pltpu.VMEM)
    return pl.pallas_call(
        functools.partial(encode_kernel, order, pieces, len(parts), len(after), stream),
        in_specs=[WHOLE] * len(parts) + [ANYWHERE if stream else WHOLE, WHOLE] + [WHOLE if join and i == 0 else ANYWHERE for i in range(len(after))],
        out_specs=[WHOLE] * len(out_shape),
        out_shape=out_shape,
        scratch_shapes=scratch,
        compiler_params=pltpu.CompilerParams(vmem_limit_bytes=ENCODE_MIB * MIB),
        name="encode",
    )(*parts, weight, bias, *after)


def split(info, value, out, sent, j):
    cols = out.shape[2]
    low, high = value[:, :cols], value[:, cols:]

    @pl.when(info[4] == 0)
    def _():
        out[j] = low
        sent[j] = high.astype(sent.dtype)

    @pl.when(info[4] == 1)
    def _():
        out[j] = high
        sent[j] = low.astype(sent.dtype)


def halves(shards, rows, width):
    shape = (shards // 2, rows, width // shards)
    return [jax.ShapeDtypeStruct(shape, jnp.float32), jax.ShapeDtypeStruct(shape, jnp.bfloat16)]


def first_wave_kernel(counts, info, *refs):
    groups = []
    for count in counts:
        groups.append(refs[:count])
        refs = refs[count:]
    mine, theirs, direct, swapped = groups
    weights, out, sent, base, *kept = refs[:6]
    total, rings, ring_sems, kept_sems, base_sem = refs[-5:]
    step, steps = pl.program_id(0), pl.num_programs(0)
    slots, block = rings.shape[0], rings.shape[1] // 2
    odd, upper = info[0] == 1, info[1] == 1

    def rows(k):
        return pl.ds(pl.multiple_of(k * block, block), block)

    def fetch(source, k):
        slot = lax.rem(k, slots)
        return pltpu.make_async_copy(
            weights.at[0, source, rows(k)],
            rings.at[slot, pl.ds(source * block, block)],
            ring_sems.at[source, slot],
        )

    def keep(source, k):
        return pltpu.make_async_copy(
            weights.at[0, info[2 + source], rows(k)],
            kept[source].at[rows(k)],
            kept_sems.at[source, k],
        )

    def fetch_all(k):
        fetch(0, k).start()
        pl.when(odd)(lambda: fetch(1, k).start())

        @pl.when(upper)
        def _():
            keep(0, k).start()
            keep(1, k).start()

    @pl.when(step == 0)
    def _():
        for k in range(slots - 1):
            fetch_all(jnp.int32(k))
        total[...] = jnp.zeros_like(total)

    pl.when(step + slots - 1 < steps)(lambda: fetch_all(step + slots - 1))

    def stacked(parts):
        values = [part[...] for part in parts]
        return values[0] if len(values) == 1 else jnp.concatenate(values, axis=0)

    def product(parts, weight):
        return jnp.dot(stacked(parts), weight, preferred_element_type=jnp.float32)

    slot = lax.rem(step, slots)
    fetch(0, step).wait()

    @pl.when(jnp.logical_not(odd))
    def _():
        total[...] += product(mine, rings[slot, pl.ds(0, block), :])

    @pl.when(odd)
    def _():
        fetch(1, step).wait()
        both = jnp.concatenate([stacked(mine), stacked(theirs)], axis=1)
        total[...] += jnp.dot(both, rings[slot], preferred_element_type=jnp.float32)

    done = out.shape[1]

    @pl.when(upper)
    def _():
        keep(0, step).wait()
        keep(1, step).wait()
        total[:done, :] += product(direct, kept[0][rows(step), :]) + product(
            swapped, kept[1][rows(step), :]
        )

    @pl.when(step == steps - 1)
    def _():
        rest = pl.ds(done, total.shape[0] - done)
        copy = pltpu.make_async_copy(total.at[rest], base, base_sem)
        copy.start()
        cols = out.shape[2]
        for j in range(out.shape[0]):
            split(info, total[:done, 2 * j * cols : 2 * (j + 1) * cols], out, sent, j)
        copy.wait()


def decode_first(info, mine, theirs, direct, swapped, decoder, shards, after):
    _, _, features, width = decoder.shape
    block = min(512, features)
    steps = features // block
    rows = sum(part.shape[0] for part in mine)
    done = sum(part.shape[0] for part in direct)

    def acts(part, flag):
        return pl.BlockSpec(
            (part.shape[0], block), lambda k, info: (0, k if flag is None else k * info[flag])
        )

    groups = (mine, theirs, direct, swapped)
    in_specs = [acts(p, flag) for parts, flag in zip(groups, (None, 0, 1, 1)) for p in parts]
    return pl.pallas_call(
        functools.partial(first_wave_kernel, [len(parts) for parts in groups]),
        grid_spec=pltpu.PrefetchScalarGridSpec(
            num_scalar_prefetch=1,
            grid=(steps,),
            in_specs=in_specs + [ANYWHERE] * (1 + len(after)),
            out_specs=[
                *[pl.BlockSpec(h.shape, lambda k, info: (0, 0, 0)) for h in halves(shards, done, width)],
                ANYWHERE,
                WHOLE,
                WHOLE,
            ],
            scratch_shapes=[
                pltpu.VMEM((rows, width), jnp.float32),
                pltpu.VMEM((SLOTS, 2 * block, width), decoder.dtype),
                pltpu.SemaphoreType.DMA((2, SLOTS)),
                pltpu.SemaphoreType.DMA((2, steps)),
                pltpu.SemaphoreType.DMA,
            ],
        ),
        out_shape=[
            *halves(shards, done, width),
            pltpu.HBM((rows - done, width), jnp.float32),
            pltpu.VMEM((features, width), decoder.dtype),
            pltpu.VMEM((features, width), decoder.dtype),
        ],
        compiler_params=pltpu.CompilerParams(vmem_limit_bytes=DECODE_MIB * MIB),
        name="decode_first",
    )(info, *sum(groups, []), decoder, *after)


def later_wave_kernel(row, skip, info, direct, swapped, base, kept_direct, kept_swapped, *refs):
    kept = kept_direct, kept_swapped
    out, sent, first, second, start, sems = refs[-6:]
    rows = out.shape[1]
    pairs, cols = out.shape[0], out.shape[2]
    copies = [
        pltpu.make_async_copy(direct.at[pl.ds(skip, rows)], first, sems.at[0]),
        pltpu.make_async_copy(swapped.at[pl.ds(skip, rows)], second, sems.at[1]),
        pltpu.make_async_copy(base.at[pl.ds(row, rows)], start, sems.at[2]),
    ]
    for copy in copies:
        copy.start()
    for copy in copies:
        copy.wait()

    @pl.loop(0, pairs)
    def _(j):
        at = pl.ds(pl.multiple_of(j * 2 * cols, 2 * cols), 2 * cols)

        @pl.when(info[1] == 1)
        def _():
            start[:, at] += jnp.dot(
                first[...], kept[0][:, at], preferred_element_type=jnp.float32
            ) + jnp.dot(second[...], kept[1][:, at], preferred_element_type=jnp.float32)

        split(info, start[:, at], out, sent, j)


def decode_later(info, direct, swapped, skip, rows, base, kept, row, shards, after):
    features, width = kept[0].shape
    return pl.pallas_call(
        functools.partial(later_wave_kernel, row, skip),
        in_specs=[pl.BlockSpec(memory_space=pltpu.SMEM)]
        + [ANYWHERE] * 3
        + [WHOLE] * 2
        + [ANYWHERE] * len(after),
        out_specs=[WHOLE, WHOLE],
        out_shape=halves(shards, rows, width),
        scratch_shapes=[
            pltpu.VMEM((rows, features), jnp.bfloat16),
            pltpu.VMEM((rows, features), jnp.bfloat16),
            pltpu.VMEM((rows, width), jnp.float32),
            pltpu.SemaphoreType.DMA((3,)),
        ],
        compiler_params=pltpu.CompilerParams(vmem_limit_bytes=DECODE_MIB * MIB),
        name="decode_later",
    )(info, fetched(direct), landed(swapped), fetched(base), *map(landed, kept), *after)


def pair_kernel(size, n, n_after, info, *refs):
    theirs, outs, sems = refs[n : 2 * n], refs[2 * n + n_after : -1 - n], refs[-1]
    mine = refs[-1 - n : -1]
    copies = [pltpu.make_async_copy(refs[i], mine[i], sems.at[i]) for i in range(n)]
    for copy in copies:
        copy.start()
    for copy in copies:
        copy.wait()
    z = info[5]
    for q, out in enumerate(outs):
        row = 0
        for kept, met in zip(mine, theirs):
            rows = kept.shape[1]
            for at in range(0, rows, size):
                partner = at // size ^ 1
                total = kept[z ^ q, pl.ds(at, size), :] + met[
                    z ^ q, pl.ds(partner * size, size), :
                ].astype(jnp.float32)
                out[pl.ds(row + at, size), :] = total.astype(out.dtype)
            row += rows


def add_pair(info, mine, theirs, size, after):
    count, _, cols = mine[0].shape
    rows = sum(kept.shape[1] for kept in mine)
    return pl.pallas_call(
        functools.partial(pair_kernel, size, len(mine), len(after)),
        in_specs=[pl.BlockSpec(memory_space=pltpu.SMEM)]
        + [ANYWHERE] * len(mine)
        + [WHOLE] * len(theirs)
        + [ANYWHERE] * len(after),
        out_specs=[WHOLE] * count,
        scratch_shapes=[pltpu.VMEM(array.shape, array.dtype) for array in mine]
        + [pltpu.SemaphoreType.DMA((len(mine),))],
        out_shape=[
            jax.ShapeDtypeStruct((rows, cols), jnp.float32 if q == 0 else jnp.bfloat16)
            for q in range(count)
        ],
        compiler_params=pltpu.CompilerParams(vmem_limit_bytes=SUM_MIB * MIB),
        name="add_pair",
    )(info, *map(fetched, mine), *map(landed, theirs), *after)


def sum_kernel(sign, pieces, info, base, *refs):
    received, out = refs[: len(pieces)], refs[-1]
    me = info[6]
    out[...] = sign * base[...]
    for ref, (source, blocks) in zip(received, pieces):
        size = ref.shape[0] // len(blocks)
        for k, s in enumerate(blocks):
            at = pl.ds(pl.multiple_of((me ^ (source ^ s)) * size, size), size)
            out[at, :] += ref[pl.ds(k * size, size), :].astype(jnp.float32)


def add_up(info, base, sign, pieces, received, after):
    return pl.pallas_call(
        functools.partial(sum_kernel, sign, pieces),
        in_specs=[pl.BlockSpec(memory_space=pltpu.SMEM)]
        + [WHOLE] * (1 + len(received))
        + [ANYWHERE] * len(after),
        out_specs=WHOLE,
        out_shape=pltpu.HBM(base.shape, base.dtype),
        compiler_params=pltpu.CompilerParams(vmem_limit_bytes=SUM_MIB * MIB),
        name="add_up",
    )(info, base, *map(landed, received), *after)


def pipelined(layer_inputs, targets, encoder, encoder_bias, decoder):
    shards = lax.axis_size("feat")
    layers = lax.axis_size("layer")
    half = layers // 2
    layer = lax.axis_index("layer")
    feat = lax.axis_index("feat")
    upper = layer >= half
    info = jnp.stack(
        [
            layer & 1,
            upper.astype(jnp.int32),
            jnp.full_like(layer, half),
            jnp.where(upper, layer - ((layer ^ 1) - half), 0),
            feat & 1,
            feat >> 1,
            feat,
        ]
    ).astype(jnp.int32)

    def up(a):
        return lax.ppermute(a, "layer", [(i, i + half) for i in range(half)])

    def across(a):
        return lax.ppermute(a, "layer", [(i, i ^ 1) for i in range(half, layers)])

    def beside(a):
        return lax.ppermute(a, "layer", [(i, i + 1) for i in range(0, layers, 2)])

    def after(value, *earlier):
        return lax.optimization_barrier((value, *earlier))[0]

    tokens = layer_inputs[0]
    size = tokens.shape[0]
    near = exchange(tokens, "feat", 1)
    far = [exchange(tokens, "feat", s) for s in range(2, shards, 2)]
    three = exchange(near, "feat", 2)

    a0, a0a, a0b, encoder_kept = encode(
        [tokens, near],
        [(0, 0, size), (1, 0, size)],
        [(0, 2 * size), (0, size), (size, size)],
        encoder,
        encoder_bias,
        [],
        stream=True,
    )
    d0a, d0b = up(a0a), up(a0b)
    rest = exchange(after(jnp.concatenate(far[1:], axis=0), far[0], three), "feat", 1)
    a01, a1 = encode(
        [far[0], three],
        [(0, 0, size), (1, 0, size)],
        [(0, 2 * size), (0, 2 * size)],
        encoder_kept,
        encoder_bias,
        [a0],
        join=True,
    )
    d1, n01 = up(a1), beside(a01)
    others = shards - 4
    order = []
    for k in range(others // 2):
        order += [(k, 0, size), (others // 2, k * size, size)]
    (a2,) = encode(
        far[1:] + [rest],
        order,
        [(0, others * size)],
        encoder_kept,
        encoder_bias,
        [a1, d0a],
    )
    d2, n2 = up(a2), beside(after(a2, d0b))

    c0a, c0b = across(after(d0a, n2)), across(after(d0b, n2))
    mine, sent, base, *kept = decode_first(
        info, [a01, a2], [n01, n2], [d0a, d0b], [c0a, c0b], decoder, shards, []
    )
    slots = [[0, 1], [2, 3], list(range(4, shards - 2)), [shards - 2, shards - 1]]

    def meet(mine, sent, *earlier):
        theirs = [exchange(array, "feat", 1) for array in sent]
        return add_pair(info, mine, theirs, size, list(earlier))

    def spread(blocks, sums):
        parts = [part if q == 0 else exchange(part, "feat", 2 * q) for q, part in enumerate(sums)]
        return [(2 * q, blocks) for q in range(len(parts))], parts

    def later(number, direct, swapped, skip, *earlier):
        row = (slots[number][0] - slots[1][0]) * size
        rows = len(slots[number]) * size
        return decode_later(
            info, direct, swapped, skip * size, rows, base, kept, row, shards, list(earlier)
        )

    c1 = across(after(d1, sent))
    mine1, sent1 = later(1, d1, c1, 0, sent)
    met1 = meet([mine, mine1], [sent, sent1])
    where1, parts1 = spread(slots[0] + slots[1], met1)
    c2 = across(after(d2, met1[0]))
    mine2, sent2 = later(2, d2, c2, 0, met1[0])
    total = add_up(info, targets[0], -1.0, where1, parts1, [sent2])
    mine3, sent3 = later(3, d2, c2, others - 2, sent2, total)
    met2 = meet([mine2], [sent2], sent3)
    where2, parts2 = spread(slots[2], met2)
    met3 = meet([mine3], [sent3], parts2[1])
    where3, parts3 = spread(slots[3], met3)
    return add_up(info, total, 1.0, where2 + where3, parts2 + parts3, [])[None]


def grouped(layer_inputs, targets, encoder, encoder_bias, decoder):
    groups = lax.axis_size("layer") // L_WIN
    depth_bits = groups.bit_length() - 1
    position = lax.axis_index("layer")
    target_layer = position // groups
    group_index = position % groups
    gathered = lax.all_gather(layer_inputs[0], "feat", axis=0, tiled=True)
    for bit_index in range(depth_bits):
        partner = exchange(gathered, "layer", 1 << bit_index)
        upper_bit = position >> bit_index & 1
        gathered = jnp.where(
            upper_bit == 1,
            jnp.concatenate([partner, gathered], 0),
            jnp.concatenate([gathered, partner], 0),
        )
    preact = (
        jnp.dot(gathered, encoder[0], preferred_element_type=jnp.float32) + encoder_bias[0][None, :]
    )
    features = jax.nn.relu(preact).astype(jnp.bfloat16)
    tok_count = features.shape[0]
    every_layer = lax.all_gather(features[None], "layer", axis=0, tiled=True)
    by_layer = every_layer.reshape(L_WIN, groups, tok_count, features.shape[1])
    mine_only = lax.dynamic_index_in_dim(by_layer, group_index, 1, keepdims=False)
    flipped = mine_only[::-1]
    padded = jnp.concatenate([flipped, jnp.zeros_like(flipped)], 0)
    stacked = lax.dynamic_slice_in_dim(padded, L_WIN - 1 - target_layer, L_WIN, 0)
    rebuilt = jnp.einsum("ktf,kfd->td", stacked, decoder[0], preferred_element_type=jnp.float32)
    for bit_index in reversed(range(depth_bits)):
        half_rows = rebuilt.shape[0] // 2
        upper_bit = position >> bit_index & 1
        kept_half = jnp.where(upper_bit == 1, rebuilt[half_rows:], rebuilt[:half_rows])
        sent_half = jnp.where(upper_bit == 1, rebuilt[:half_rows], rebuilt[half_rows:])
        rebuilt = kept_half + exchange(sent_half, "layer", 1 << bit_index)
    summed = lax.psum_scatter(rebuilt, "feat", scatter_dimension=1, tiled=True)
    residual = summed - targets[0]
    return residual[None]


def solution(mesh):
    placed = (
        P("layer", "feat", None),
        P("layer", None, "feat"),
        P("layer", None, "feat"),
        P("layer", "feat"),
        P("layer", None, "feat", None),
    )
    shards = mesh.shape["feat"]
    simple = mesh.shape["layer"] == L_WIN and shards >= 8 and shards & (shards - 1) == 0
    return jax.shard_map(
        pipelined if simple else grouped,
        mesh=mesh,
        in_specs=placed,
        out_specs=P("layer", None, "feat"),
        check_vma=False,
    )
```

```python
import functools

import jax
import jax.numpy as jnp
from jax import lax
from jax.experimental import pallas as pl
from jax.experimental.pallas import tpu as pltpu
from jax.sharding import PartitionSpec as P

L_WIN = 4
MIB = 1024 * 1024


def exchange(array, axis, flip):
    size = lax.axis_size(axis)
    return lax.ppermute(array, axis, [(i, i ^ flip) for i in range(size)])


ANYWHERE = pl.BlockSpec(memory_space=pl.ANY)
WHOLE = pl.BlockSpec(memory_space=pltpu.VMEM)
SLOTS = 3
ENCODE_MIB = 16
DECODE_MIB = 26
SUM_MIB = 12


def landed(array):
    return pltpu.with_memory_space_constraint(array, pltpu.VMEM)


def fetched(array):
    return pltpu.with_memory_space_constraint(array, pltpu.HBM)


def fill(order, parts, rows_of):
    at = 0
    for part, row, size in order:
        rows_of[pl.ds(at, size), :] = parts[part][pl.ds(row, size), :]
        at += size


def encode_kernel(order, pieces, n_in, n_after, stream, *refs):
    parts, weight, bias, refs = refs[:n_in], refs[n_in], refs[n_in + 1], refs[n_in + 2 :]
    earlier, refs = refs[:n_after], refs[n_after:]
    outs, refs = refs[: len(pieces)], refs[len(pieces) :]
    features = weight.shape[2]
    if stream:
        kept, tokens, sems = refs
        block = features // sems.shape[0]
    else:
        kept, (tokens,) = weight, refs
        block = min(512, features)

    def fetch(j):
        cols = pl.ds(pl.multiple_of(j * block, block), block)
        return pltpu.make_async_copy(weight.at[0, :, cols], kept.at[0, :, cols], sems.at[j])

    if stream:
        for j in range(features // block):
            fetch(jnp.int32(j)).start()
    fill(order, parts, tokens)

    @pl.loop(0, features // block)
    def _(j):
        if stream:
            fetch(j).wait()
        cols = pl.ds(pl.multiple_of(j * block, block), block)
        preact = jnp.dot(tokens[...], kept[0, :, cols], preferred_element_type=jnp.float32)
        acts = jnp.maximum(preact + bias[:, cols], 0.0).astype(jnp.bfloat16)
        for out, (row, size) in zip(outs, pieces):
            before = out.shape[0] - size
            out[pl.ds(before, size), cols] = acts[row : row + size]
            if before:
                out[pl.ds(0, before), cols] = earlier[0][:, cols]


def encode(parts, order, pieces, weight, bias, after, stream=False, join=False):
    rows = sum(size for _, _, size in order)
    _, width, features = weight.shape
    out_shape = [jax.ShapeDtypeStruct((size, features), jnp.bfloat16) for _, size in pieces]
    if join:
        joined = (after[0].shape[0] + pieces[0][1], features)
        out_shape[0] = jax.ShapeDtypeStruct(joined, jnp.bfloat16)
    scratch = [pltpu.VMEM((rows, width), jnp.bfloat16)]
    if stream:
        out_shape.append(pltpu.VMEM(weight.shape, weight.dtype))
        scratch.append(pltpu.SemaphoreType.DMA((max(1, features // 512),)))
        weight = pltpu.with_memory_space_constraint(weight, pltpu.HBM)
    else:
        weight = pltpu.with_memory_space_constraint(weight, pltpu.VMEM)
    return pl.pallas_call(
        functools.partial(encode_kernel, order, pieces, len(parts), len(after), stream),
        in_specs=[WHOLE] * len(parts) + [ANYWHERE if stream else WHOLE, WHOLE] + [WHOLE if join and i == 0 else ANYWHERE for i in range(len(after))],
        out_specs=[WHOLE] * len(out_shape),
        out_shape=out_shape,
        scratch_shapes=scratch,
        compiler_params=pltpu.CompilerParams(vmem_limit_bytes=ENCODE_MIB * MIB),
        name="encode",
    )(*parts, weight, bias, *after)


def split(info, value, out, sent, j):
    cols = out.shape[2]
    low, high = value[:, :cols], value[:, cols:]

    @pl.when(info[4] == 0)
    def _():
        out[j] = low
        sent[j] = high.astype(sent.dtype)

    @pl.when(info[4] == 1)
    def _():
        out[j] = high
        sent[j] = low.astype(sent.dtype)


def halves(shards, rows, width):
    shape = (shards // 2, rows, width // shards)
    return [jax.ShapeDtypeStruct(shape, jnp.float32), jax.ShapeDtypeStruct(shape, jnp.bfloat16)]


def first_wave_kernel(counts, info, *refs):
    groups = []
    for count in counts:
        groups.append(refs[:count])
        refs = refs[count:]
    mine, theirs, direct, swapped = groups
    weights, out, sent, base, *kept = refs[:6]
    total, rings, ring_sems, kept_sems, base_sem = refs[-5:]
    step, steps = pl.program_id(0), pl.num_programs(0)
    slots, block = rings.shape[0], rings.shape[1] // 2
    odd, upper = info[0] == 1, info[1] == 1

    def rows(k):
        return pl.ds(pl.multiple_of(k * block, block), block)

    def fetch(source, k):
        slot = lax.rem(k, slots)
        return pltpu.make_async_copy(
            weights.at[0, source, rows(k)],
            rings.at[slot, pl.ds(source * block, block)],
            ring_sems.at[source, slot],
        )

    def keep(source, k):
        return pltpu.make_async_copy(
            weights.at[0, info[2 + source], rows(k)],
            kept[source].at[rows(k)],
            kept_sems.at[source, k],
        )

    def fetch_all(k):
        fetch(0, k).start()
        pl.when(odd)(lambda: fetch(1, k).start())

        @pl.when(upper)
        def _():
            keep(0, k).start()
            keep(1, k).start()

    @pl.when(step == 0)
    def _():
        for k in range(slots - 1):
            fetch_all(jnp.int32(k))
        total[...] = jnp.zeros_like(total)

    pl.when(step + slots - 1 < steps)(lambda: fetch_all(step + slots - 1))

    def stacked(parts):
        values = [part[...] for part in parts]
        return values[0] if len(values) == 1 else jnp.concatenate(values, axis=0)

    def product(parts, weight):
        return jnp.dot(stacked(parts), weight, preferred_element_type=jnp.float32)

    slot = lax.rem(step, slots)
    fetch(0, step).wait()

    @pl.when(jnp.logical_not(odd))
    def _():
        total[...] += product(mine, rings[slot, pl.ds(0, block), :])

    @pl.when(odd)
    def _():
        fetch(1, step).wait()
        both = jnp.concatenate([stacked(mine), stacked(theirs)], axis=1)
        total[...] += jnp.dot(both, rings[slot], preferred_element_type=jnp.float32)

    done = out.shape[1]

    @pl.when(upper)
    def _():
        keep(0, step).wait()
        keep(1, step).wait()
        total[:done, :] += product(direct, kept[0][rows(step), :]) + product(
            swapped, kept[1][rows(step), :]
        )

    @pl.when(step == steps - 1)
    def _():
        rest = pl.ds(done, total.shape[0] - done)
        copy = pltpu.make_async_copy(total.at[rest], base, base_sem)
        copy.start()
        cols = out.shape[2]
        for j in range(out.shape[0]):
            split(info, total[:done, 2 * j * cols : 2 * (j + 1) * cols], out, sent, j)
        copy.wait()


def decode_first(info, mine, theirs, direct, swapped, decoder, shards, after):
    _, _, features, width = decoder.shape
    block = min(512, features)
    steps = features // block
    rows = sum(part.shape[0] for part in mine)
    done = sum(part.shape[0] for part in direct)

    def acts(part, flag):
        return pl.BlockSpec(
            (part.shape[0], block), lambda k, info: (0, k if flag is None else k * info[flag])
        )

    groups = (mine, theirs, direct, swapped)
    in_specs = [acts(p, flag) for parts, flag in zip(groups, (None, 0, 1, 1)) for p in parts]
    return pl.pallas_call(
        functools.partial(first_wave_kernel, [len(parts) for parts in groups]),
        grid_spec=pltpu.PrefetchScalarGridSpec(
            num_scalar_prefetch=1,
            grid=(steps,),
            in_specs=in_specs + [ANYWHERE] * (1 + len(after)),
            out_specs=[
                *[pl.BlockSpec(h.shape, lambda k, info: (0, 0, 0)) for h in halves(shards, done, width)],
                ANYWHERE,
                WHOLE,
                WHOLE,
            ],
            scratch_shapes=[
                pltpu.VMEM((rows, width), jnp.float32),
                pltpu.VMEM((SLOTS, 2 * block, width), decoder.dtype),
                pltpu.SemaphoreType.DMA((2, SLOTS)),
                pltpu.SemaphoreType.DMA((2, steps)),
                pltpu.SemaphoreType.DMA,
            ],
        ),
        out_shape=[
            *halves(shards, done, width),
            pltpu.HBM((rows - done, width), jnp.float32),
            pltpu.VMEM((features, width), decoder.dtype),
            pltpu.VMEM((features, width), decoder.dtype),
        ],
        compiler_params=pltpu.CompilerParams(vmem_limit_bytes=DECODE_MIB * MIB),
        name="decode_first",
    )(info, *sum(groups, []), decoder, *after)


def later_wave_kernel(row, skip, info, direct, swapped, base, kept_direct, kept_swapped, *refs):
    kept = kept_direct, kept_swapped
    out, sent, first, second, start, sems = refs[-6:]
    rows = out.shape[1]
    pairs, cols = out.shape[0], out.shape[2]
    copies = [
        pltpu.make_async_copy(direct.at[pl.ds(skip, rows)], first, sems.at[0]),
        pltpu.make_async_copy(swapped.at[pl.ds(skip, rows)], second, sems.at[1]),
        pltpu.make_async_copy(base.at[pl.ds(row, rows)], start, sems.at[2]),
    ]
    for copy in copies:
        copy.start()
    for copy in copies:
        copy.wait()

    @pl.loop(0, pairs)
    def _(j):
        at = pl.ds(pl.multiple_of(j * 2 * cols, 2 * cols), 2 * cols)

        @pl.when(info[1] == 1)
        def _():
            start[:, at] += jnp.dot(
                first[...], kept[0][:, at], preferred_element_type=jnp.float32
            ) + jnp.dot(second[...], kept[1][:, at], preferred_element_type=jnp.float32)

        split(info, start[:, at], out, sent, j)


def decode_later(info, direct, swapped, skip, rows, base, kept, row, shards, after):
    features, width = kept[0].shape
    return pl.pallas_call(
        functools.partial(later_wave_kernel, row, skip),
        in_specs=[pl.BlockSpec(memory_space=pltpu.SMEM)]
        + [ANYWHERE] * 3
        + [WHOLE] * 2
        + [ANYWHERE] * len(after),
        out_specs=[WHOLE, WHOLE],
        out_shape=halves(shards, rows, width),
        scratch_shapes=[
            pltpu.VMEM((rows, features), jnp.bfloat16),
            pltpu.VMEM((rows, features), jnp.bfloat16),
            pltpu.VMEM((rows, width), jnp.float32),
            pltpu.SemaphoreType.DMA((3,)),
        ],
        compiler_params=pltpu.CompilerParams(vmem_limit_bytes=DECODE_MIB * MIB),
        name="decode_later",
    )(info, fetched(direct), landed(swapped), fetched(base), *map(landed, kept), *after)


def pair_kernel(size, n, n_after, info, *refs):
    theirs, outs, sems = refs[n : 2 * n], refs[2 * n + n_after : -1 - n], refs[-1]
    mine = refs[-1 - n : -1]
    copies = [pltpu.make_async_copy(refs[i], mine[i], sems.at[i]) for i in range(n)]
    for copy in copies:
        copy.start()
    for copy in copies:
        copy.wait()
    z = info[5]
    for q, out in enumerate(outs):
        row = 0
        for kept, met in zip(mine, theirs):
            rows = kept.shape[1]
            for at in range(0, rows, size):
                partner = at // size ^ 1
                total = kept[z ^ q, pl.ds(at, size), :] + met[
                    z ^ q, pl.ds(partner * size, size), :
                ].astype(jnp.float32)
                out[pl.ds(row + at, size), :] = total.astype(out.dtype)
            row += rows


def add_pair(info, mine, theirs, size, after):
    count, _, cols = mine[0].shape
    rows = sum(kept.shape[1] for kept in mine)
    return pl.pallas_call(
        functools.partial(pair_kernel, size, len(mine), len(after)),
        in_specs=[pl.BlockSpec(memory_space=pltpu.SMEM)]
        + [ANYWHERE] * len(mine)
        + [WHOLE] * len(theirs)
        + [ANYWHERE] * len(after),
        out_specs=[WHOLE] * count,
        scratch_shapes=[pltpu.VMEM(array.shape, array.dtype) for array in mine]
        + [pltpu.SemaphoreType.DMA((len(mine),))],
        out_shape=[
            jax.ShapeDtypeStruct((rows, cols), jnp.float32 if q == 0 else jnp.bfloat16)
            for q in range(count)
        ],
        compiler_params=pltpu.CompilerParams(vmem_limit_bytes=SUM_MIB * MIB),
        name="add_pair",
    )(info, *map(fetched, mine), *map(landed, theirs), *after)


def sum_kernel(sign, pieces, info, base, *refs):
    received, out = refs[: len(pieces)], refs[-1]
    me = info[6]
    out[...] = sign * base[...]
    for ref, (source, blocks) in zip(received, pieces):
        size = ref.shape[0] // len(blocks)
        for k, s in enumerate(blocks):
            at = pl.ds(pl.multiple_of((me ^ (source ^ s)) * size, size), size)
            out[at, :] += ref[pl.ds(k * size, size), :].astype(jnp.float32)


def add_up(info, base, sign, pieces, received, after):
    return pl.pallas_call(
        functools.partial(sum_kernel, sign, pieces),
        in_specs=[pl.BlockSpec(memory_space=pltpu.SMEM)]
        + [WHOLE] * (1 + len(received))
        + [ANYWHERE] * len(after),
        out_specs=WHOLE,
        out_shape=pltpu.HBM(base.shape, base.dtype),
        compiler_params=pltpu.CompilerParams(vmem_limit_bytes=SUM_MIB * MIB),
        name="add_up",
    )(info, base, *map(landed, received), *after)


def pipelined(layer_inputs, targets, encoder, encoder_bias, decoder):
    shards = lax.axis_size("feat")
    layers = lax.axis_size("layer")
    half = layers // 2
    layer = lax.axis_index("layer")
    feat = lax.axis_index("feat")
    upper = layer >= half
    info = jnp.stack(
        [
            layer & 1,
            upper.astype(jnp.int32),
            jnp.full_like(layer, half),
            jnp.where(upper, layer - ((layer ^ 1) - half), 0),
            feat & 1,
            feat >> 1,
            feat,
        ]
    ).astype(jnp.int32)

    def up(a):
        return lax.ppermute(a, "layer", [(i, i + half) for i in range(half)])

    def across(a):
        return lax.ppermute(a, "layer", [(i, i ^ 1) for i in range(half, layers)])

    def beside(a):
        return lax.ppermute(a, "layer", [(i, i + 1) for i in range(0, layers, 2)])

    def after(value, *earlier):
        return lax.optimization_barrier((value, *earlier))[0]

    tokens = layer_inputs[0]
    size = tokens.shape[0]
    near = exchange(tokens, "feat", 1)
    far = [exchange(tokens, "feat", s) for s in range(2, shards, 2)]
    three = exchange(near, "feat", 2)

    a0, a0a, a0b, encoder_kept = encode(
        [tokens, near],
        [(0, 0, size), (1, 0, size)],
        [(0, 2 * size), (0, size), (size, size)],
        encoder,
        encoder_bias,
        [],
        stream=True,
    )
    d0a, d0b = up(a0a), up(a0b)
    rest = exchange(after(jnp.concatenate(far[1:], axis=0), far[0], three), "feat", 1)
    a01, a1 = encode(
        [far[0], three],
        [(0, 0, size), (1, 0, size)],
        [(0, 2 * size), (0, 2 * size)],
        encoder_kept,
        encoder_bias,
        [a0],
        join=True,
    )
    d1, n01 = up(a1), beside(a01)
    others = shards - 4
    order = []
    for k in range(others // 2):
        order += [(k, 0, size), (others // 2, k * size, size)]
    (a2,) = encode(
        far[1:] + [rest],
        order,
        [(0, others * size)],
        encoder_kept,
        encoder_bias,
        [a1, d0a],
    )
    d2, n2 = up(a2), beside(after(a2, d0b))

    c0a, c0b = across(after(d0a, n2, n01)), across(after(d0b, n2, n01))
    mine, sent, base, *kept = decode_first(
        info, [a01, a2], [n01, n2], [d0a, d0b], [c0a, c0b], decoder, shards, []
    )
    slots = [[0, 1], [2, 3], list(range(4, shards - 2)), [shards - 2, shards - 1]]

    def meet(mine, sent, *earlier):
        theirs = [exchange(array, "feat", 1) for array in sent]
        return add_pair(info, mine, theirs, size, list(earlier))

    def spread(blocks, sums):
        parts = [part if q == 0 else exchange(part, "feat", 2 * q) for q, part in enumerate(sums)]
        return [(2 * q, blocks) for q in range(len(parts))], parts

    def later(number, direct, swapped, skip, *earlier):
        row = (slots[number][0] - slots[1][0]) * size
        rows = len(slots[number]) * size
        return decode_later(
            info, direct, swapped, skip * size, rows, base, kept, row, shards, list(earlier)
        )

    c1 = across(after(d1, sent))
    mine1, sent1 = later(1, d1, c1, 0, sent)
    met1 = meet([mine, mine1], [sent, sent1])
    where1, parts1 = spread(slots[0] + slots[1], met1)
    c2 = across(after(d2, met1[0]))
    mine2, sent2 = later(2, d2, c2, 0, met1[0])
    total = add_up(info, targets[0], -1.0, where1, parts1, [sent2])
    mine3, sent3 = later(3, d2, c2, others - 2, sent2, total)
    met2 = meet([mine2], [sent2], sent3)
    where2, parts2 = spread(slots[2], met2)
    met3 = meet([mine3], [sent3], parts2[1])
    where3, parts3 = spread(slots[3], met3)
    return add_up(info, total, 1.0, where2 + where3, parts2 + parts3, [])[None]


def grouped(layer_inputs, targets, encoder, encoder_bias, decoder):
    groups = lax.axis_size("layer") // L_WIN
    depth_bits = groups.bit_length() - 1
    position = lax.axis_index("layer")
    target_layer = position // groups
    group_index = position % groups
    gathered = lax.all_gather(layer_inputs[0], "feat", axis=0, tiled=True)
    for bit_index in range(depth_bits):
        partner = exchange(gathered, "layer", 1 << bit_index)
        upper_bit = position >> bit_index & 1
        gathered = jnp.where(
            upper_bit == 1,
            jnp.concatenate([partner, gathered], 0),
            jnp.concatenate([gathered, partner], 0),
        )
    preact = (
        jnp.dot(gathered, encoder[0], preferred_element_type=jnp.float32) + encoder_bias[0][None, :]
    )
    features = jax.nn.relu(preact).astype(jnp.bfloat16)
    tok_count = features.shape[0]
    every_layer = lax.all_gather(features[None], "layer", axis=0, tiled=True)
    by_layer = every_layer.reshape(L_WIN, groups, tok_count, features.shape[1])
    mine_only = lax.dynamic_index_in_dim(by_layer, group_index, 1, keepdims=False)
    flipped = mine_only[::-1]
    padded = jnp.concatenate([flipped, jnp.zeros_like(flipped)], 0)
    stacked = lax.dynamic_slice_in_dim(padded, L_WIN - 1 - target_layer, L_WIN, 0)
    rebuilt = jnp.einsum("ktf,kfd->td", stacked, decoder[0], preferred_element_type=jnp.float32)
    for bit_index in reversed(range(depth_bits)):
        half_rows = rebuilt.shape[0] // 2
        upper_bit = position >> bit_index & 1
        kept_half = jnp.where(upper_bit == 1, rebuilt[half_rows:], rebuilt[:half_rows])
        sent_half = jnp.where(upper_bit == 1, rebuilt[:half_rows], rebuilt[half_rows:])
        rebuilt = kept_half + exchange(sent_half, "layer", 1 << bit_index)
    summed = lax.psum_scatter(rebuilt, "feat", scatter_dimension=1, tiled=True)
    residual = summed - targets[0]
    return residual[None]


def solution(mesh):
    placed = (
        P("layer", "feat", None),
        P("layer", None, "feat"),
        P("layer", None, "feat"),
        P("layer", "feat"),
        P("layer", None, "feat", None),
    )
    shards = mesh.shape["feat"]
    simple = mesh.shape["layer"] == L_WIN and shards >= 8 and shards & (shards - 1) == 0
    return jax.shard_map(
        pipelined if simple else grouped,
        mesh=mesh,
        in_specs=placed,
        out_specs=P("layer", None, "feat"),
        check_vma=False,
    )
```

```python
import functools

import jax
import jax.numpy as jnp
from jax import lax
from jax.experimental import pallas as pl
from jax.experimental.pallas import tpu as pltpu
from jax.sharding import PartitionSpec as P

L_WIN = 4
MIB = 1024 * 1024


def exchange(array, axis, flip):
    size = lax.axis_size(axis)
    return lax.ppermute(array, axis, [(i, i ^ flip) for i in range(size)])


ANYWHERE = pl.BlockSpec(memory_space=pl.ANY)
WHOLE = pl.BlockSpec(memory_space=pltpu.VMEM)
SLOTS = 3
ENCODE_MIB = 16
DECODE_MIB = 26
SUM_MIB = 12


def landed(array):
    return pltpu.with_memory_space_constraint(array, pltpu.VMEM)


def fetched(array):
    return pltpu.with_memory_space_constraint(array, pltpu.HBM)


def fill(order, parts, rows_of):
    at = 0
    for part, row, size in order:
        rows_of[pl.ds(at, size), :] = parts[part][pl.ds(row, size), :]
        at += size


def encode_kernel(order, pieces, n_in, n_after, stream, *refs):
    parts, weight, bias, refs = refs[:n_in], refs[n_in], refs[n_in + 1], refs[n_in + 2 :]
    earlier, refs = refs[:n_after], refs[n_after:]
    outs, refs = refs[: len(pieces)], refs[len(pieces) :]
    features = weight.shape[2]
    if stream:
        kept, tokens, sems = refs
        block = features // sems.shape[0]
    else:
        kept, (tokens,) = weight, refs
        block = min(512, features)

    def fetch(j):
        cols = pl.ds(pl.multiple_of(j * block, block), block)
        return pltpu.make_async_copy(weight.at[0, :, cols], kept.at[0, :, cols], sems.at[j])

    if stream:
        for j in range(features // block):
            fetch(jnp.int32(j)).start()
    fill(order, parts, tokens)

    @pl.loop(0, features // block)
    def _(j):
        if stream:
            fetch(j).wait()
        cols = pl.ds(pl.multiple_of(j * block, block), block)
        preact = jnp.dot(tokens[...], kept[0, :, cols], preferred_element_type=jnp.float32)
        acts = jnp.maximum(preact + bias[:, cols], 0.0).astype(jnp.bfloat16)
        for out, (row, size) in zip(outs, pieces):
            before = out.shape[0] - size
            out[pl.ds(before, size), cols] = acts[row : row + size]
            if before:
                out[pl.ds(0, before), cols] = earlier[0][:, cols]


def encode(parts, order, pieces, weight, bias, after, stream=False, join=False):
    rows = sum(size for _, _, size in order)
    _, width, features = weight.shape
    out_shape = [jax.ShapeDtypeStruct((size, features), jnp.bfloat16) for _, size in pieces]
    if join:
        joined = (after[0].shape[0] + pieces[0][1], features)
        out_shape[0] = jax.ShapeDtypeStruct(joined, jnp.bfloat16)
    scratch = [pltpu.VMEM((rows, width), jnp.bfloat16)]
    if stream:
        out_shape.append(pltpu.VMEM(weight.shape, weight.dtype))
        scratch.append(pltpu.SemaphoreType.DMA((max(1, features // 512),)))
        weight = pltpu.with_memory_space_constraint(weight, pltpu.HBM)
    else:
        weight = pltpu.with_memory_space_constraint(weight, pltpu.VMEM)
    return pl.pallas_call(
        functools.partial(encode_kernel, order, pieces, len(parts), len(after), stream),
        in_specs=[WHOLE] * len(parts) + [ANYWHERE if stream else WHOLE, WHOLE] + [WHOLE if join and i == 0 else ANYWHERE for i in range(len(after))],
        out_specs=[WHOLE] * len(out_shape),
        out_shape=out_shape,
        scratch_shapes=scratch,
        compiler_params=pltpu.CompilerParams(vmem_limit_bytes=ENCODE_MIB * MIB),
        name="encode",
    )(*parts, weight, bias, *after)


def split(info, value, out, sent, j):
    cols = out.shape[2]
    low, high = value[:, :cols], value[:, cols:]

    @pl.when(info[4] == 0)
    def _():
        out[j] = low
        sent[j] = high.astype(sent.dtype)

    @pl.when(info[4] == 1)
    def _():
        out[j] = high
        sent[j] = low.astype(sent.dtype)


def halves(shards, rows, width):
    shape = (shards // 2, rows, width // shards)
    return [jax.ShapeDtypeStruct(shape, jnp.float32), jax.ShapeDtypeStruct(shape, jnp.bfloat16)]


def first_wave_kernel(counts, info, *refs):
    groups = []
    for count in counts:
        groups.append(refs[:count])
        refs = refs[count:]
    mine, theirs, direct, swapped = groups
    weights, out, sent, base, *kept = refs[:6]
    total, rings, ring_sems, kept_sems, base_sem = refs[-5:]
    step, steps = pl.program_id(0), pl.num_programs(0)
    slots, block = rings.shape[0], rings.shape[1] // 2
    odd, upper = info[0] == 1, info[1] == 1

    def rows(k):
        return pl.ds(pl.multiple_of(k * block, block), block)

    def fetch(source, k):
        slot = lax.rem(k, slots)
        return pltpu.make_async_copy(
            weights.at[0, source, rows(k)],
            rings.at[slot, pl.ds(source * block, block)],
            ring_sems.at[source, slot],
        )

    def keep(source, k):
        return pltpu.make_async_copy(
            weights.at[0, info[2 + source], rows(k)],
            kept[source].at[rows(k)],
            kept_sems.at[source, k],
        )

    def fetch_own(k):
        fetch(0, k).start()
        pl.when(odd)(lambda: fetch(1, k).start())

    def fetch_kept(k):
        @pl.when(upper)
        def _():
            keep(0, k).start()
            keep(1, k).start()

    @pl.when(step == 0)
    def _():
        for k in range(slots - 1):
            fetch_own(jnp.int32(k))
        for k in range(slots - 1):
            fetch_kept(jnp.int32(k))
        total[...] = jnp.zeros_like(total)

    @pl.when(step + slots - 1 < steps)
    def _():
        fetch_own(step + slots - 1)
        fetch_kept(step + slots - 1)

    def stacked(parts):
        values = [part[...] for part in parts]
        return values[0] if len(values) == 1 else jnp.concatenate(values, axis=0)

    def product(parts, weight):
        return jnp.dot(stacked(parts), weight, preferred_element_type=jnp.float32)

    slot = lax.rem(step, slots)
    fetch(0, step).wait()

    @pl.when(jnp.logical_not(odd))
    def _():
        total[...] += product(mine, rings[slot, pl.ds(0, block), :])

    @pl.when(odd)
    def _():
        fetch(1, step).wait()
        both = jnp.concatenate([stacked(mine), stacked(theirs)], axis=1)
        total[...] += jnp.dot(both, rings[slot], preferred_element_type=jnp.float32)

    done = out.shape[1]

    @pl.when(upper)
    def _():
        keep(0, step).wait()
        keep(1, step).wait()
        total[:done, :] += product(direct, kept[0][rows(step), :]) + product(
            swapped, kept[1][rows(step), :]
        )

    @pl.when(step == steps - 1)
    def _():
        rest = pl.ds(done, total.shape[0] - done)
        copy = pltpu.make_async_copy(total.at[rest], base, base_sem)
        copy.start()
        cols = out.shape[2]
        for j in range(out.shape[0]):
            split(info, total[:done, 2 * j * cols : 2 * (j + 1) * cols], out, sent, j)
        copy.wait()


def decode_first(info, mine, theirs, direct, swapped, decoder, shards, after):
    _, _, features, width = decoder.shape
    block = min(512, features)
    steps = features // block
    rows = sum(part.shape[0] for part in mine)
    done = sum(part.shape[0] for part in direct)

    def acts(part, flag):
        return pl.BlockSpec(
            (part.shape[0], block), lambda k, info: (0, k if flag is None else k * info[flag])
        )

    groups = (mine, theirs, direct, swapped)
    in_specs = [acts(p, flag) for parts, flag in zip(groups, (None, 0, 1, 1)) for p in parts]
    return pl.pallas_call(
        functools.partial(first_wave_kernel, [len(parts) for parts in groups]),
        grid_spec=pltpu.PrefetchScalarGridSpec(
            num_scalar_prefetch=1,
            grid=(steps,),
            in_specs=in_specs + [ANYWHERE] * (1 + len(after)),
            out_specs=[
                *[pl.BlockSpec(h.shape, lambda k, info: (0, 0, 0)) for h in halves(shards, done, width)],
                ANYWHERE,
                WHOLE,
                WHOLE,
            ],
            scratch_shapes=[
                pltpu.VMEM((rows, width), jnp.float32),
                pltpu.VMEM((SLOTS, 2 * block, width), decoder.dtype),
                pltpu.SemaphoreType.DMA((2, SLOTS)),
                pltpu.SemaphoreType.DMA((2, steps)),
                pltpu.SemaphoreType.DMA,
            ],
        ),
        out_shape=[
            *halves(shards, done, width),
            pltpu.HBM((rows - done, width), jnp.float32),
            pltpu.VMEM((features, width), decoder.dtype),
            pltpu.VMEM((features, width), decoder.dtype),
        ],
        compiler_params=pltpu.CompilerParams(vmem_limit_bytes=DECODE_MIB * MIB),
        name="decode_first",
    )(info, *sum(groups, []), decoder, *after)


def later_wave_kernel(row, skip, info, direct, swapped, base, kept_direct, kept_swapped, *refs):
    kept = kept_direct, kept_swapped
    out, sent, first, second, start, sems = refs[-6:]
    rows = out.shape[1]
    pairs, cols = out.shape[0], out.shape[2]
    copies = [
        pltpu.make_async_copy(direct.at[pl.ds(skip, rows)], first, sems.at[0]),
        pltpu.make_async_copy(swapped.at[pl.ds(skip, rows)], second, sems.at[1]),
        pltpu.make_async_copy(base.at[pl.ds(row, rows)], start, sems.at[2]),
    ]
    for copy in copies:
        copy.start()
    for copy in copies:
        copy.wait()

    @pl.loop(0, pairs)
    def _(j):
        at = pl.ds(pl.multiple_of(j * 2 * cols, 2 * cols), 2 * cols)

        @pl.when(info[1] == 1)
        def _():
            start[:, at] += jnp.dot(
                first[...], kept[0][:, at], preferred_element_type=jnp.float32
            ) + jnp.dot(second[...], kept[1][:, at], preferred_element_type=jnp.float32)

        split(info, start[:, at], out, sent, j)


def decode_later(info, direct, swapped, skip, rows, base, kept, row, shards, after):
    features, width = kept[0].shape
    return pl.pallas_call(
        functools.partial(later_wave_kernel, row, skip),
        in_specs=[pl.BlockSpec(memory_space=pltpu.SMEM)]
        + [ANYWHERE] * 3
        + [WHOLE] * 2
        + [ANYWHERE] * len(after),
        out_specs=[WHOLE, WHOLE],
        out_shape=halves(shards, rows, width),
        scratch_shapes=[
            pltpu.VMEM((rows, features), jnp.bfloat16),
            pltpu.VMEM((rows, features), jnp.bfloat16),
            pltpu.VMEM((rows, width), jnp.float32),
            pltpu.SemaphoreType.DMA((3,)),
        ],
        compiler_params=pltpu.CompilerParams(vmem_limit_bytes=DECODE_MIB * MIB),
        name="decode_later",
    )(info, fetched(direct), landed(swapped), fetched(base), *map(landed, kept), *after)


def pair_kernel(size, n, n_after, info, *refs):
    theirs, outs, sems = refs[n : 2 * n], refs[2 * n + n_after : -1 - n], refs[-1]
    mine = refs[-1 - n : -1]
    copies = [pltpu.make_async_copy(refs[i], mine[i], sems.at[i]) for i in range(n)]
    for copy in copies:
        copy.start()
    for copy in copies:
        copy.wait()
    z = info[5]
    for q, out in enumerate(outs):
        row = 0
        for kept, met in zip(mine, theirs):
            rows = kept.shape[1]
            for at in range(0, rows, size):
                partner = at // size ^ 1
                total = kept[z ^ q, pl.ds(at, size), :] + met[
                    z ^ q, pl.ds(partner * size, size), :
                ].astype(jnp.float32)
                out[pl.ds(row + at, size), :] = total.astype(out.dtype)
            row += rows


def add_pair(info, mine, theirs, size, after):
    count, _, cols = mine[0].shape
    rows = sum(kept.shape[1] for kept in mine)
    return pl.pallas_call(
        functools.partial(pair_kernel, size, len(mine), len(after)),
        in_specs=[pl.BlockSpec(memory_space=pltpu.SMEM)]
        + [ANYWHERE] * len(mine)
        + [WHOLE] * len(theirs)
        + [ANYWHERE] * len(after),
        out_specs=[WHOLE] * count,
        scratch_shapes=[pltpu.VMEM(array.shape, array.dtype) for array in mine]
        + [pltpu.SemaphoreType.DMA((len(mine),))],
        out_shape=[
            jax.ShapeDtypeStruct((rows, cols), jnp.float32 if q == 0 else jnp.bfloat16)
            for q in range(count)
        ],
        compiler_params=pltpu.CompilerParams(vmem_limit_bytes=SUM_MIB * MIB),
        name="add_pair",
    )(info, *map(fetched, mine), *map(landed, theirs), *after)


def sum_kernel(sign, pieces, info, base, *refs):
    received, out = refs[: len(pieces)], refs[-1]
    me = info[6]
    out[...] = sign * base[...]
    for ref, (source, blocks) in zip(received, pieces):
        size = ref.shape[0] // len(blocks)
        for k, s in enumerate(blocks):
            at = pl.ds(pl.multiple_of((me ^ (source ^ s)) * size, size), size)
            out[at, :] += ref[pl.ds(k * size, size), :].astype(jnp.float32)


def add_up(info, base, sign, pieces, received, after):
    return pl.pallas_call(
        functools.partial(sum_kernel, sign, pieces),
        in_specs=[pl.BlockSpec(memory_space=pltpu.SMEM)]
        + [WHOLE] * (1 + len(received))
        + [ANYWHERE] * len(after),
        out_specs=WHOLE,
        out_shape=pltpu.HBM(base.shape, base.dtype),
        compiler_params=pltpu.CompilerParams(vmem_limit_bytes=SUM_MIB * MIB),
        name="add_up",
    )(info, base, *map(landed, received), *after)


def pipelined(layer_inputs, targets, encoder, encoder_bias, decoder):
    shards = lax.axis_size("feat")
    layers = lax.axis_size("layer")
    half = layers // 2
    layer = lax.axis_index("layer")
    feat = lax.axis_index("feat")
    upper = layer >= half
    info = jnp.stack(
        [
            layer & 1,
            upper.astype(jnp.int32),
            jnp.full_like(layer, half),
            jnp.where(upper, layer - ((layer ^ 1) - half), 0),
            feat & 1,
            feat >> 1,
            feat,
        ]
    ).astype(jnp.int32)

    def up(a):
        return lax.ppermute(a, "layer", [(i, i + half) for i in range(half)])

    def across(a):
        return lax.ppermute(a, "layer", [(i, i ^ 1) for i in range(half, layers)])

    def beside(a):
        return lax.ppermute(a, "layer", [(i, i + 1) for i in range(0, layers, 2)])

    def after(value, *earlier):
        return lax.optimization_barrier((value, *earlier))[0]

    tokens = layer_inputs[0]
    size = tokens.shape[0]
    near = exchange(tokens, "feat", 1)
    far = [exchange(tokens, "feat", s) for s in range(2, shards, 2)]
    three = exchange(near, "feat", 2)

    a0, a0a, a0b, encoder_kept = encode(
        [tokens, near],
        [(0, 0, size), (1, 0, size)],
        [(0, 2 * size), (0, size), (size, size)],
        encoder,
        encoder_bias,
        [],
        stream=True,
    )
    d0a, d0b = up(a0a), up(a0b)
    rest = exchange(after(jnp.concatenate(far[1:], axis=0), far[0], three), "feat", 1)
    a01, a1 = encode(
        [far[0], three],
        [(0, 0, size), (1, 0, size)],
        [(0, 2 * size), (0, 2 * size)],
        encoder_kept,
        encoder_bias,
        [a0],
        join=True,
    )
    d1, n01 = up(a1), beside(a01)
    others = shards - 4
    order = []
    for k in range(others // 2):
        order += [(k, 0, size), (others // 2, k * size, size)]
    (a2,) = encode(
        far[1:] + [rest],
        order,
        [(0, others * size)],
        encoder_kept,
        encoder_bias,
        [a1, d0a],
    )
    d2, n2 = up(a2), beside(after(a2, d0b))

    c0a, c0b = across(after(d0a, n2, n01)), across(after(d0b, n2, n01))
    mine, sent, base, *kept = decode_first(
        info, [a01, a2], [n01, n2], [d0a, d0b], [c0a, c0b], decoder, shards, []
    )
    slots = [[0, 1], [2, 3], list(range(4, shards - 2)), [shards - 2, shards - 1]]

    def meet(mine, sent, *earlier):
        theirs = [exchange(array, "feat", 1) for array in sent]
        return add_pair(info, mine, theirs, size, list(earlier))

    def spread(blocks, sums):
        parts = [part if q == 0 else exchange(part, "feat", 2 * q) for q, part in enumerate(sums)]
        return [(2 * q, blocks) for q in range(len(parts))], parts

    def later(number, direct, swapped, skip, *earlier):
        row = (slots[number][0] - slots[1][0]) * size
        rows = len(slots[number]) * size
        return decode_later(
            info, direct, swapped, skip * size, rows, base, kept, row, shards, list(earlier)
        )

    c1 = across(after(d1, sent))
    mine1, sent1 = later(1, d1, c1, 0, sent)
    met1 = meet([mine, mine1], [sent, sent1])
    where1, parts1 = spread(slots[0] + slots[1], met1)
    c2 = across(after(d2, met1[0]))
    mine2, sent2 = later(2, d2, c2, 0, met1[0])
    total = add_up(info, targets[0], -1.0, where1, parts1, [sent2])
    mine3, sent3 = later(3, d2, c2, others - 2, sent2, total)
    met2 = meet([mine2], [sent2], sent3)
    where2, parts2 = spread(slots[2], met2)
    met3 = meet([mine3], [sent3], parts2[1])
    where3, parts3 = spread(slots[3], met3)
    return add_up(info, total, 1.0, where2 + where3, parts2 + parts3, [])[None]


def grouped(layer_inputs, targets, encoder, encoder_bias, decoder):
    groups = lax.axis_size("layer") // L_WIN
    depth_bits = groups.bit_length() - 1
    position = lax.axis_index("layer")
    target_layer = position // groups
    group_index = position % groups
    gathered = lax.all_gather(layer_inputs[0], "feat", axis=0, tiled=True)
    for bit_index in range(depth_bits):
        partner = exchange(gathered, "layer", 1 << bit_index)
        upper_bit = position >> bit_index & 1
        gathered = jnp.where(
            upper_bit == 1,
            jnp.concatenate([partner, gathered], 0),
            jnp.concatenate([gathered, partner], 0),
        )
    preact = (
        jnp.dot(gathered, encoder[0], preferred_element_type=jnp.float32) + encoder_bias[0][None, :]
    )
    features = jax.nn.relu(preact).astype(jnp.bfloat16)
    tok_count = features.shape[0]
    every_layer = lax.all_gather(features[None], "layer", axis=0, tiled=True)
    by_layer = every_layer.reshape(L_WIN, groups, tok_count, features.shape[1])
    mine_only = lax.dynamic_index_in_dim(by_layer, group_index, 1, keepdims=False)
    flipped = mine_only[::-1]
    padded = jnp.concatenate([flipped, jnp.zeros_like(flipped)], 0)
    stacked = lax.dynamic_slice_in_dim(padded, L_WIN - 1 - target_layer, L_WIN, 0)
    rebuilt = jnp.einsum("ktf,kfd->td", stacked, decoder[0], preferred_element_type=jnp.float32)
    for bit_index in reversed(range(depth_bits)):
        half_rows = rebuilt.shape[0] // 2
        upper_bit = position >> bit_index & 1
        kept_half = jnp.where(upper_bit == 1, rebuilt[half_rows:], rebuilt[:half_rows])
        sent_half = jnp.where(upper_bit == 1, rebuilt[:half_rows], rebuilt[half_rows:])
        rebuilt = kept_half + exchange(sent_half, "layer", 1 << bit_index)
    summed = lax.psum_scatter(rebuilt, "feat", scatter_dimension=1, tiled=True)
    residual = summed - targets[0]
    return residual[None]


def solution(mesh):
    placed = (
        P("layer", "feat", None),
        P("layer", None, "feat"),
        P("layer", None, "feat"),
        P("layer", "feat"),
        P("layer", None, "feat", None),
    )
    shards = mesh.shape["feat"]
    simple = mesh.shape["layer"] == L_WIN and shards >= 8 and shards & (shards - 1) == 0
    return jax.shard_map(
        pipelined if simple else grouped,
        mesh=mesh,
        in_specs=placed,
        out_specs=P("layer", None, "feat"),
        check_vma=False,
    )
```
